32 devices in a mesh: dp: 2 (over core), fsdp: 16 (over z, y, x).
Axes of the slice: x: 2, y: 2, z: 4, core: 2. Of those that a mesh axis runs over, the one named last changes fastest.
Arguments:
- tokens: bfloat16 [32768, 768], P(('dp', 'fsdp')), may hold values from -6 to 6
- clip_frames: int32 [8], replicated, may hold values from 8 to 16, as said below
- tube_clip: int32 [128], P(('dp', 'fsdp')), may hold values from 0 to 7, as said below
- first_gain: bfloat16 [768], P('fsdp'), may hold values from 0.25 to 1.75
- first_shift: bfloat16 [768], P('fsdp'), may hold values from -1.75 to 1.75
- qkv_weight: bfloat16 [768, 2304], P('fsdp'), may hold values from -0.21875 to 0.21875
- query_bias: bfloat16 [768], P('fsdp'), may hold values from -1.75 to 1.75
- value_bias: bfloat16 [768], P('fsdp'), may hold values from -1.75 to 1.75
- out_weight: bfloat16 [768, 768], P('fsdp'), may hold values from -2.5 to 2.5
- out_bias: bfloat16 [768], P('fsdp'), may hold values from -1.75 to 1.75
- second_gain: bfloat16 [768], P('fsdp'), may hold values from 0.25 to 1.75
- second_shift: bfloat16 [768], P('fsdp'), may hold values from -1.75 to 1.75
- up_weight: bfloat16 [768, 3072], P('fsdp'), may hold values from -0.21875 to 0.21875
- up_bias: bfloat16 [3072], P('fsdp'), may hold values from -1.75 to 1.75
- down_weight: bfloat16 [3072, 768], P('fsdp'), may hold values from -0.109375 to 0.109375
- down_bias: bfloat16 [768], P('fsdp'), may hold values from -1.75 to 1.75
- cotangent: bfloat16 [32768, 768], P(('dp', 'fsdp')), may hold values from -6 to 6
Outputs:
- block_out: bfloat16 [32768, 768], P(('dp', 'fsdp'))
- tokens_grad: bfloat16 [32768, 768], P(('dp', 'fsdp'))
- first_gain_grad: float32 [768], P('fsdp')
- first_shift_grad: float32 [768], P('fsdp')
- qkv_weight_grad: float32 [768, 2304], P('fsdp')
- query_bias_grad: float32 [768], P('fsdp')
- value_bias_grad: float32 [768], P('fsdp')
- out_weight_grad: float32 [768, 768], P('fsdp')
- out_bias_grad: float32 [768], P('fsdp')
- second_gain_grad: float32 [768], P('fsdp')
- second_shift_grad: float32 [768], P('fsdp')
- up_weight_grad: float32 [768, 3072], P('fsdp')
- up_bias_grad: float32 [3072], P('fsdp')
- down_weight_grad: float32 [3072, 768], P('fsdp')
- down_bias_grad: float32 [768], P('fsdp')
The draws below stay inside these ranges and needn't reach their ends.
Inputs may be any that keep to these rules, and one draw needn't show every extreme that they name: `clip_frames`: some clip has 16 real frames. `tube_clip`: each clip number names exactly 16 tubes.
All inputs are finite; a program needn't handle non-finite values.
Results may differ from the reference program's by a relative error of at most 0.014.
Values may be sent and summed in bfloat16 or wider, within the bound.
No kernel may reach another device: no remote copies, remote signals or barrier semaphores. Data moves between devices by JAX's collectives and lax.ppermute only.
A program may use at most 128 MiB of HBM per device.

```python
import jax
import jax.numpy as jnp
from jax import lax

D = 768
HEADS = 12
HEAD_DIM = 64
FF = 3072
FRAMES = 16
PATCH = 16
CLIP_TUBES = 16
TUBE = 256
TUBES = 128
CLIPS = 8


def draw_clip_frames(key, part):
    key = jax.random.fold_in(key, 11)
    pick_key, count_key = jax.random.split(key)
    counts = jax.random.randint(count_key, (CLIPS,), FRAMES // 2, FRAMES + 1)
    chosen = jax.random.randint(pick_key, (), 0, CLIPS)
    places = jnp.arange(CLIPS)
    counts = jnp.where(places == chosen, FRAMES, counts)
    return counts.astype(jnp.int32)


def draw_tube_clip(key, part):
    key = jax.random.fold_in(key, 23)
    shuffled = jax.random.permutation(key, TUBES)
    return (shuffled // CLIP_TUBES).astype(jnp.int32)


def block_levels(own_key, shape, shards, least, top_value):
    factor_of = 1.0
    for axis_at, parts in shards:
        draws = jax.random.uniform(jax.random.fold_in(jax.random.fold_in(own_key, 6), axis_at), (parts,), jnp.float32, least / len(shards), top_value / len(shards))
        factor_of = factor_of * jnp.repeat(jnp.exp(draws), shape[axis_at] // parts).reshape((-1,) + (1,) * (len(shape) - 1 - axis_at))
    return factor_of


def normal_values(own_key, extent, width, reach, shards=(), kind=jnp.bfloat16):
    array = jax.random.normal(own_key, extent, jnp.float32) * width
    if len(shards) > 0:
        array = block_levels(own_key, extent, shards, -0.22, 0.18) * array
    return jnp.clip(array, min=-reach, max=reach).astype(kind)


def setup_inputs(seed: int = 0) -> dict:
    arg_keys = jax.random.split(jax.random.key(seed), 18)
    tokens = normal_values(arg_keys[0], (TUBES * TUBE, D), 1.0, 6.0, ((0, 32),))
    clip_frames = draw_clip_frames(jax.random.fold_in(arg_keys[17], 71), 0)
    tube_clip = draw_tube_clip(jax.random.fold_in(arg_keys[17], 71), 0)
    first_gain = jnp.clip(1.0 + 0.15 * jax.random.normal(arg_keys[3], (D,), jnp.float32), 0.25, 1.75).astype(jnp.bfloat16)
    first_shift = normal_values(arg_keys[4], (D,), 0.3, 1.75, ((0, 16),))
    qkv_weight = normal_values(arg_keys[5], (D, 3 * D), D ** -0.5, 0.21875, ((0, 16),))
    query_bias = normal_values(arg_keys[6], (D,), 0.3, 1.75, ((0, 16),))
    value_bias = normal_values(arg_keys[7], (D,), 0.3, 1.75, ((0, 16),))
    out_weight = normal_values(arg_keys[8], (D, D), (max(D // 128, 1)) ** -0.5, 2.5, ((0, 16),))
    out_bias = normal_values(arg_keys[9], (D,), 0.3, 1.75, ((0, 16),))
    second_gain = jnp.clip(1.0 + 0.15 * jax.random.normal(arg_keys[10], (D,), jnp.float32), 0.25, 1.75).astype(jnp.bfloat16)
    second_shift = normal_values(arg_keys[11], (D,), 0.3, 1.75, ((0, 16),))
    up_weight = normal_values(arg_keys[12], (D, FF), D ** -0.5, 0.21875, ((0, 16),))
    up_bias = normal_values(arg_keys[13], (FF,), 0.3, 1.75, ((0, 16),))
    down_weight = normal_values(arg_keys[14], (FF, D), FF ** -0.5, 0.109375, ((0, 16),))
    down_bias = normal_values(arg_keys[15], (D,), 0.3, 1.75, ((0, 16),))
    cotangent = normal_values(arg_keys[16], (TUBES * TUBE, D), 1.0, 6.0, ((0, 32),))
    return dict(tokens=tokens, clip_frames=clip_frames, tube_clip=tube_clip, first_gain=first_gain, first_shift=first_shift, qkv_weight=qkv_weight, query_bias=query_bias, value_bias=value_bias, out_weight=out_weight, out_bias=out_bias, second_gain=second_gain, second_shift=second_shift, up_weight=up_weight, up_bias=up_bias, down_weight=down_weight, down_bias=down_bias, cotangent=cotangent)


@jax.custom_vjp
def low(v):
    return lax.optimization_barrier(v.astype(jnp.bfloat16)).astype(jnp.float32)

@jax.custom_vjp
def low_back(v):
    return v

def low_keep(v):
    return (low(v), None)

def low_pass(kept, grad):
    return (grad,)

def back_keep(v):
    return (v, None)

def back_low(kept, grad):
    return (low(grad),)
low.defvjp(low_keep, low_pass)
low_back.defvjp(back_keep, back_low)
EPSILON = 1e-05

def rounded_both(values):
    return low(low_back(values))

def norm_layer(values, gain, shift):
    average = lax.optimization_barrier(jnp.mean(values, axis=-1, keepdims=True))
    centred = values - average
    spread = lax.optimization_barrier(jnp.mean(centred * centred, axis=-1, keepdims=True))
    return centred * lax.rsqrt(spread + EPSILON) * gain + shift

def forward(params, inputs, key_ok):
    first_gain, first_shift, qkv_weight, query_bias, value_bias, out_weight, out_bias, second_gain, second_shift, up_weight, up_bias, down_weight, down_bias = params
    precise = lax.Precision.HIGHEST
    groups = key_ok.shape[0]
    normed_one = low(norm_layer(inputs, first_gain, first_shift))
    project = jnp.dot(normed_one, qkv_weight, precision=precise)
    query = rounded_both(project[:, :D] + query_bias).reshape(groups, TUBE, HEADS, HEAD_DIM)
    keys_part = rounded_both(project[:, D:2 * D]).reshape(groups, TUBE, HEADS, HEAD_DIM)
    values_part = rounded_both(project[:, 2 * D:] + value_bias).reshape(groups, TUBE, HEADS, HEAD_DIM)
    scores = jnp.einsum('gthd,gshd->ghts', query, keys_part, precision=precise) * HEAD_DIM ** (-0.5)
    scores = low_back(scores)
    masked = jnp.where(key_ok[:, None, None, :], scores, -1e+30)
    probs = low(jax.nn.softmax(masked, axis=-1))
    mixed = jnp.einsum('ghts,gshd->gthd', probs, values_part, precision=precise)
    mixed = rounded_both(mixed.reshape(groups * TUBE, D))
    attended = low_back(jnp.dot(mixed, out_weight, precision=precise) + out_bias)
    resid = inputs + attended
    normed_two = low(norm_layer(resid, second_gain, second_shift))
    hidden = low_back(jnp.dot(normed_two, up_weight, precision=precise) + up_bias)
    active = low(jax.nn.gelu(hidden, approximate=False))
    branch = low_back(jnp.dot(active, down_weight, precision=precise) + down_bias)
    return resid + branch

def reference(tokens, clip_frames, tube_clip, first_gain, first_shift, qkv_weight, query_bias, value_bias, out_weight, out_bias, second_gain, second_shift, up_weight, up_bias, down_weight, down_bias, cotangent):
    params = tuple((weight.astype(jnp.float32) for weight in (first_gain, first_shift, qkv_weight, query_bias, value_bias, out_weight, out_bias, second_gain, second_shift, up_weight, up_bias, down_weight, down_bias)))
    matches = tube_clip[:, None] == jnp.arange(CLIPS, dtype=jnp.int32)[None, :]
    tube_frames = lax.optimization_barrier(jnp.sum(jnp.where(matches, clip_frames[None, :], 0), axis=1))
    key_ok = jnp.arange(TUBE, dtype=jnp.int32)[None, :] // PATCH < tube_frames[:, None]
    rounds = TUBES // CLIP_TUBES
    inputs = tokens.astype(jnp.float32).reshape(rounds, CLIP_TUBES * TUBE, D)
    row_ok = key_ok.reshape(TUBES * TUBE, 1).astype(jnp.float32)
    upstream = (cotangent.astype(jnp.float32) * row_ok).reshape(rounds, CLIP_TUBES * TUBE, D)
    masks = key_ok.reshape(rounds, CLIP_TUBES, TUBE)
    empty = jax.tree.map(jnp.zeros_like, params)

    def group_step(totals, item):
        group_inputs, group_upstream, group_ok = item
        result, pullback = jax.vjp(lambda weights, values: forward(weights, values, group_ok), params, group_inputs)
        param_grads, input_grad = pullback(group_upstream)
        return (jax.tree.map(jnp.add, totals, param_grads), (result, input_grad))
    totals, (results, input_grads) = lax.scan(group_step, empty, (inputs, upstream, masks))
    block_out = results.reshape(TUBES * TUBE, D).astype(jnp.bfloat16)
    tokens_grad = input_grads.reshape(TUBES * TUBE, D).astype(jnp.bfloat16)
    return (block_out, tokens_grad, totals[0], totals[1], totals[2], totals[3], totals[4], totals[5], totals[6], totals[7], totals[8], totals[9], totals[10], totals[11], totals[12])
```

```python
import functools
import math

import jax
import jax.numpy as jnp
from jax import lax
from jax.experimental import pallas as pl
from jax.experimental.pallas import tpu as pltpu
from jax.sharding import PartitionSpec as P

HEADS = 12
HEAD_DIM = 64
PATCH = 16
EPSILON = 1e-05
SQRT_HALF = 0.7071067811865476
DENSITY = 0.3989422804014327
AXES = ("dp", "fsdp")
F32 = jnp.float32
BF16 = jnp.bfloat16
LANES = 128
MEBI = 1 << 20


def grid_of(shards):
    side = math.isqrt(shards // 4)
    assert 4 * side * side == shards
    return 4, side


def arrive(value, shards, kind, step):
    depth, side = grid_of(shards)
    pairs = []
    for core in range(2):
        for z in range(depth):
            for y in range(side):
                for x in range(side):
                    to = core * shards + (z * side + y) * side + x
                    at = [core, z, y, x]
                    if kind == "core":
                        at[0] = 1 - core
                    elif kind == "z":
                        at[1] = (z + step) % depth
                    elif (kind == "first") == (core == 0):
                        at[3] = (x + step) % side
                    else:
                        at[2] = (y + step) % side
                    pairs.append((at[0] * shards + (at[1] * side + at[2]) * side + at[3], to))
    return lax.ppermute(value, AXES, pairs)


def place(shards, half):
    _, side = grid_of(shards)
    at = lax.axis_index("fsdp")
    z, y, x = at // (side * side), (at // side) % side, at % side
    first = jnp.where(half == 0, x, y)
    second = jnp.where(half == 0, y, x)
    return jnp.stack([half, z, first, second, lax.axis_index("dp")]).astype(jnp.int32)


def gather(unit, shards):
    depth, side = grid_of(shards)
    got = jnp.stack([unit] + [arrive(unit, shards, "z", s) for s in range(1, depth)])
    got = jnp.stack([got] + [arrive(got, shards, "first", s) for s in range(1, side)])
    own = [got] + [arrive(got, shards, "second", s) for s in range(1, side)]
    return own, [arrive(part, shards, "core", 1) for part in own]


def row_of(where, depth, side, rel_second, rel_first, rel_z):
    z = lax.rem(where[1] + rel_z, depth)
    first = lax.rem(where[2] + rel_first, side)
    second = lax.rem(where[3] + rel_second, side)
    y = jnp.where(where[0] == 0, second, first)
    x = jnp.where(where[0] == 0, first, second)
    return (z * side + y) * side + x


def unroll_rows(parts, where, half, depth, side):
    rel = jnp.stack(parts)
    rel = jnp.roll(rel, where[3], axis=0)
    rel = jnp.roll(rel, where[2], axis=1)
    rel = jnp.roll(rel, where[1], axis=2)
    straight = jnp.where(half == 0, rel.transpose(2, 0, 1, 3, 4), rel.transpose(2, 1, 0, 3, 4))
    return straight.reshape(-1, rel.shape[-1])


def assemble(own, other, shards, cuts):
    depth, side = grid_of(shards)
    core = lax.axis_index("dp")
    here, there = place(shards, core), place(shards, 1 - core)
    mine = unroll_rows(own, here, core, depth, side)
    theirs = unroll_rows(other, there, 1 - core, depth, side)
    wholes = []
    for start, width, split in cuts:
        left, right = mine[:, start : start + width], theirs[:, start : start + width]
        if split:
            swapped = jnp.concatenate([right, left], axis=1)
            left = jnp.where(core == 0, jnp.concatenate([left, right], axis=1), swapped)
        wholes.append(left)
    return wholes


def grad_kernel(depth, side, rows, deep, adds, where, lhs, rhs, *refs):
    got = refs[0] if adds else None
    outs, acc = refs[adds : adds + side], refs[-1]
    acc[...] = lax.dot_general(lhs[...], rhs[...], (((0,), (0,)), ((), ())), preferred_element_type=F32)
    for second in range(side):
        for first in range(side):
            for z in range(deep):
                at = row_of(where, depth, side, second, first, z)
                if deep == 1:
                    at = lax.rem(at, side * side)
                piece = acc[pl.ds(pl.multiple_of(at * rows, 16), rows), :]
                if adds:
                    piece = piece + got[second, first, z].astype(F32)
                outs[second][first, z] = piece.astype(BF16)


def rel_grad(lhs, rhs, shards, half, got=None, tile=384):
    depth, side = grid_of(shards)
    length, features = lhs.shape
    width = rhs.shape[1] // 2
    rows = features // shards
    where = place(shards, half)
    if rows % 16 != 0:
        part = lax.dynamic_slice_in_dim(rhs, half * width, width, axis=1)
        whole = lax.dot_general(lhs, part, (((0,), (0,)), ((), ())), preferred_element_type=F32)
        whole = whole.reshape(depth, side, side, rows, width)
        rel = jnp.where(half == 0, whole.transpose(1, 2, 0, 3, 4), whole.transpose(2, 1, 0, 3, 4))
        rel = jnp.roll(rel, -where[3], axis=0)
        rel = jnp.roll(rel, -where[2], axis=1)
        rel = jnp.roll(rel, -where[1], axis=2)
        if got is not None:
            rel = rel + got.astype(F32)
        return [rel[s].astype(BF16) for s in range(side)]
    deep = depth if features <= 1024 else 1
    chunk = features if deep > 1 else features // depth
    tiles = width // tile
    adds = 0 if got is None else 1
    layers = depth // deep

    def lhs_at(k, j, where):
        return (0, 0) if deep > 1 else (0, lax.rem(where[1] + k, depth))

    def rhs_at(k, j, where):
        return (0, where[0] * tiles + j)

    def out_at(k, j, where):
        return (0, k, 0, j)

    in_specs = [pl.BlockSpec((length, chunk), lhs_at), pl.BlockSpec((length, tile), rhs_at)]
    args = [lhs, rhs]
    if adds:
        in_specs.append(pl.BlockSpec((side, side, deep, rows, tile), lambda k, j, where: (0, 0, k, 0, j)))
        args.append(got)
    return pl.pallas_call(
        functools.partial(grad_kernel, depth, side, rows, deep, adds),
        grid_spec=pltpu.PrefetchScalarGridSpec(
            num_scalar_prefetch=1,
            grid=(layers, tiles),
            in_specs=in_specs,
            out_specs=[pl.BlockSpec((side, deep, rows, tile), out_at)] * side,
            scratch_shapes=[pltpu.VMEM((chunk, tile), F32)],
        ),
        out_shape=[jax.ShapeDtypeStruct((side, depth, rows, width), BF16)] * side,
        compiler_params=pltpu.CompilerParams(vmem_limit_bytes=48 * MEBI),
        cost_estimate=pl.CostEstimate(
            flops=2 * length * features * width,
            bytes_accessed=2 * (length * (features + width) + features * width * (1 + adds)),
            transcendentals=0,
        ),
        name="grad",
    )(where, *args)


def reduce_half(lhs, rhs, shards, tile=384):
    depth, side = grid_of(shards)
    core = lax.axis_index("dp")
    away = jnp.stack(rel_grad(lhs, rhs, shards, 1 - core, None, tile))
    return reduce_tail(rel_grad(lhs, rhs, shards, core, arrive(away, shards, "core", 1), tile), shards)


def reduce_tail(parts, shards):
    depth, side = grid_of(shards)
    arrived = [arrive(parts[s], shards, "second", side - s) for s in range(1, side)]
    sums = []
    for f in range(side):
        total = parts[0][f].astype(F32)
        for part in arrived:
            total = total + part[f].astype(F32)
        sums.append(total.astype(BF16))
    arrived = [arrive(sums[f], shards, "first", side - f) for f in range(1, side)]
    layers = []
    for z in range(depth):
        total = sums[0][z].astype(F32)
        for part in arrived:
            total = total + part[z].astype(F32)
        layers.append(total.astype(BF16))
    total = layers[0].astype(F32)
    for z in range(1, depth):
        total = total + arrive(layers[z], shards, "z", depth - z).astype(F32)
    return total.astype(BF16)


def both_halves(mine, shards):
    theirs = arrive(mine, shards, "core", 1)
    core = lax.axis_index("dp")
    left = jnp.where(core == 0, mine, theirs)
    right = jnp.where(core == 0, theirs, mine)
    return jnp.concatenate([left, right], axis=1).astype(F32)


def relative(whole, shards):
    depth, side = grid_of(shards)
    core = lax.axis_index("dp")
    where = place(shards, core)
    whole = whole.reshape(depth, side, side, *whole.shape[1:])
    rel = jnp.where(core == 0, whole.transpose(1, 2, 0, 3, 4), whole.transpose(2, 1, 0, 3, 4))
    rel = jnp.roll(rel, -where[3], axis=0)
    rel = jnp.roll(rel, -where[2], axis=1)
    rel = jnp.roll(rel, -where[1], axis=2)
    return [rel[s] for s in range(side)]


GAIN_ONE, SHIFT_ONE, BIAS_QUERY, BIAS_VALUE, BIAS_OUT, GAIN_TWO, SHIFT_TWO, BIAS_DOWN = range(8)
SCALE = HEAD_DIM ** (-0.5)


def weight_copies(plan, here, there, parts, outs, sems, first=0):
    copies = []
    if plan is None:
        for part, out in zip(parts, outs):
            copies.append(pltpu.make_async_copy(part, out, sems.at[first + len(copies)]))
        return copies
    depth, side, rows, cuts = plan
    for group in range(2):
        where = here if group == 0 else there
        for second in range(side):
            for ahead in range(side):
                for z in range(depth):
                    at = pl.multiple_of(row_of(where, depth, side, second, ahead, z) * rows, 16)
                    source = parts[group * side + second].at[ahead, z]
                    for (start, width, split), out in zip(cuts, outs):
                        if group == 1 and not split:
                            continue
                        column = pl.multiple_of(where[0] * width, LANES) if split else 0
                        copies.append(
                            pltpu.make_async_copy(
                                source.at[:, pl.ds(start, width)],
                                out.at[pl.ds(at, rows), pl.ds(column, width)],
                                sems.at[first + len(copies)],
                            )
                        )
    return copies


def copies_of(plan, shards, cuts):
    if plan is None:
        return len(cuts)
    return shards * sum(2 if split else 1 for _, _, split in cuts)


def standardize(values):
    average = jnp.mean(values, axis=-1, keepdims=True)
    centred = values - average
    spread = jnp.mean(centred * centred, axis=-1, keepdims=True)
    inverse = lax.rsqrt(spread + EPSILON)
    return centred * inverse, inverse


def dot(a, b, dims=((1,), (0,))):
    return lax.dot_general(a, b, (dims, ((), ())), preferred_element_type=F32)


NT = ((1,), (1,))
TN = ((0,), (0,))


def attend_kernel(plan, count, here, there, frames, tokens, *refs):
    parts = refs[:count]
    normed_ref, qkv_ref, mixed_ref, probs_ref, lines_ref = refs[count : count + 5]
    weight, small, sems = refs[count + 5 :]
    tube = pl.program_id(0)
    width = tokens.shape[1]
    length = tokens.shape[0]

    @pl.when(tube == 0)
    def _():
        copies = weight_copies(plan, here, there, parts, (weight, small), sems)
        for copy in copies:
            copy.start()
        for copy in copies:
            copy.wait()
        lines_ref[...] = small[...].astype(F32).T[: lines_ref.shape[0], :]

    standard, _ = standardize(tokens[...].astype(F32))
    normed = (standard * lines_ref[pl.ds(GAIN_ONE, 1), :] + lines_ref[pl.ds(SHIFT_ONE, 1), :]).astype(BF16)
    normed_ref[...] = normed
    bias = (lines_ref[pl.ds(BIAS_QUERY, 1), :], None, lines_ref[pl.ds(BIAS_VALUE, 1), :])
    for part in range(3):
        columns = slice(part * width, (part + 1) * width)
        project = dot(normed, weight[:, columns])
        if bias[part] is not None:
            project = project + bias[part]
        qkv_ref[:, columns] = project.astype(BF16)
    key_ok = lax.broadcasted_iota(jnp.int32, (length, length), 1) < frames[tube] * PATCH
    lower = lax.broadcasted_iota(jnp.int32, (length, LANES), 1) < HEAD_DIM
    for pair in range(width // LANES):
        query = qkv_ref[:, pair * LANES : (pair + 1) * LANES]
        keys = qkv_ref[:, width + pair * LANES : width + (pair + 1) * LANES]
        values = qkv_ref[:, 2 * width + pair * LANES : 2 * width + (pair + 1) * LANES]
        mixed = []
        for k in range(2):
            own = jnp.where(lower if k == 0 else ~lower, query, jnp.zeros_like(query))
            scores = jnp.where(key_ok, dot(own, keys, NT) * SCALE, -1e30)
            top = jnp.max(scores, axis=-1, keepdims=True)
            power = jnp.exp(scores - top)
            probs = (power * (1.0 / jnp.sum(power, axis=-1, keepdims=True))).astype(BF16)
            probs_ref[0, 2 * pair + k] = probs
            mixed.append(dot(probs, values))
        mixed_ref[:, pair * LANES : (pair + 1) * LANES] = jnp.where(lower, mixed[0], mixed[1]).astype(BF16)


def feed_kernel(plan, count, here, there, frames, tokens, mixed, cotangent, lines, up_bias, *refs):
    parts = refs[:count]
    resid_ref, normed_ref, active_ref, slope_ref, upstream_ref = refs[count : count + 5]
    out_weight, up_weight, sems = refs[count + 5 :]
    tube = pl.program_id(0)

    @pl.when(tube == 0)
    def _():
        copies = weight_copies(plan, here, there, parts, (out_weight, up_weight), sems)
        for copy in copies:
            copy.start()
        for copy in copies:
            copy.wait()

    length = tokens.shape[0]
    row_ok = lax.broadcasted_iota(jnp.int32, (length, 1), 0) < frames[tube] * PATCH
    upstream_ref[...] = jnp.where(row_ok, cotangent[...], jnp.zeros_like(cotangent))
    attended = dot(mixed[...], out_weight[...]) + lines[pl.ds(BIAS_OUT, 1), :]
    resid = tokens[...].astype(F32) + attended
    resid_ref[...] = resid
    standard, _ = standardize(resid)
    normed = (standard * lines[pl.ds(GAIN_TWO, 1), :] + lines[pl.ds(SHIFT_TWO, 1), :]).astype(BF16)
    normed_ref[...] = normed
    units = up_weight.shape[1]
    step = 512
    for at in range(0, units, step):
        hidden = dot(normed, up_weight[:, at : at + step]) + up_bias[:, at : at + step]
        bell = jnp.exp(-0.5 * hidden * hidden)
        t = 1.0 / (1.0 + (0.3275911 * SQRT_HALF) * jnp.abs(hidden))
        series = t * (
            0.254829592 + t * (-0.284496736 + t * (1.421413741 + t * (-1.453152027 + t * 1.061405429)))
        )
        tail = 0.5 * series * bell
        cumulative = jnp.where(hidden >= 0.0, 1.0 - tail, tail)
        active_ref[:, at : at + step] = (hidden * cumulative).astype(BF16)
        slope_ref[:, at : at + step] = (cumulative + hidden * (DENSITY * bell)).astype(BF16)


def norm_back(grad, standard, inverse, gain):
    scaled = grad * gain
    first = jnp.mean(scaled, axis=-1, keepdims=True)
    second = jnp.mean(scaled * standard, axis=-1, keepdims=True)
    return inverse * (scaled - first - standard * second)


def column_sum(values):
    return jnp.sum(values, axis=0, keepdims=True)


SUM_GAIN_TWO, SUM_SHIFT_TWO, SUM_BIAS_OUT, SUM_BIAS_DOWN = range(4)


def feed_back_kernel(plans, counts, here, there, upstream, slope, resid, lines, *refs):
    ff_parts, down_parts = refs[: counts[0]], refs[counts[0] : sum(counts)]
    hidden_ref, resid_grad_ref, attended_ref, mixed_ref, sums_ref, up_sum_ref = refs[sum(counts) : sum(counts) + 6]
    out_weight, up_weight, down_weight, sems = refs[sum(counts) + 6 :]
    tube = pl.program_id(0)

    @pl.when(tube == 0)
    def _():
        copies = weight_copies(plans[1], here, there, down_parts, (down_weight,), sems)
        copies += weight_copies(plans[0], here, there, ff_parts, (out_weight, up_weight), sems, len(copies))
        for copy in copies:
            copy.start()
        for copy in copies:
            copy.wait()
        sums_ref[...] = jnp.zeros_like(sums_ref)
        up_sum_ref[...] = jnp.zeros_like(up_sum_ref)

    units = up_weight.shape[1]
    step = 768
    low = upstream[...]
    normed_grad = jnp.zeros(resid.shape, F32)
    for at in range(0, units, step):
        grad = dot(low, down_weight[at : at + step, :], NT) * slope[:, at : at + step].astype(F32)
        grad = grad.astype(BF16)
        hidden_ref[:, at : at + step] = grad
        up_sum_ref[:, at : at + step] += column_sum(grad.astype(F32))
        normed_grad = normed_grad + dot(grad, up_weight[:, at : at + step], NT)
    standard, inverse = standardize(resid[...])
    above = low.astype(F32)
    resid_grad = above + norm_back(normed_grad, standard, inverse, lines[pl.ds(GAIN_TWO, 1), :])
    resid_grad_ref[...] = resid_grad
    attended_grad = resid_grad.astype(BF16)
    attended_ref[...] = attended_grad
    mixed_ref[...] = dot(attended_grad, out_weight[...], NT).astype(BF16)
    sums_ref[pl.ds(SUM_GAIN_TWO, 1), :] += column_sum(normed_grad * standard)
    sums_ref[pl.ds(SUM_SHIFT_TWO, 1), :] += column_sum(normed_grad)
    sums_ref[pl.ds(SUM_BIAS_OUT, 1), :] += column_sum(attended_grad.astype(F32))
    sums_ref[pl.ds(SUM_BIAS_DOWN, 1), :] += column_sum(above)


def attend_back_kernel(qkv, probs_ref, mixed, mixed_grad, grad_ref, sums_ref):
    tube = pl.program_id(0)

    @pl.when(tube == 0)
    def _():
        sums_ref[...] = jnp.zeros_like(sums_ref)

    length, width = mixed.shape
    lower = lax.broadcasted_iota(jnp.int32, (length, LANES), 1) < HEAD_DIM
    for pair in range(width // LANES):
        lanes = slice(pair * LANES, (pair + 1) * LANES)
        query = qkv[:, lanes]
        keys = qkv[:, width + pair * LANES : width + (pair + 1) * LANES]
        values = qkv[:, 2 * width + pair * LANES : 2 * width + (pair + 1) * LANES]
        above = mixed_grad[:, lanes]
        product = above.astype(F32) * mixed[:, lanes].astype(F32)
        query_grad, keys_grad, values_grad = [], [], []
        for k in range(2):
            mine = lower if k == 0 else ~lower
            own = jnp.where(mine, above, jnp.zeros_like(above))
            probs = probs_ref[0, 2 * pair + k]
            inner = jnp.sum(jnp.where(mine, product, 0.0), axis=-1, keepdims=True)
            probs_grad = dot(own, values, NT)
            scores_grad = (probs.astype(F32) * (probs_grad - inner)).astype(BF16)
            values_grad.append(dot(probs, above, TN))
            query_grad.append(dot(scores_grad, keys))
            keys_grad.append(dot(scores_grad, query, TN))
        for part, (pieces, scale) in enumerate(((query_grad, SCALE), (keys_grad, SCALE), (values_grad, None))):
            piece = jnp.where(lower, pieces[0], pieces[1])
            if scale is not None:
                piece = piece * scale
            piece = piece.astype(BF16)
            grad_ref[:, part * width + pair * LANES : part * width + (pair + 1) * LANES] = piece
            if part != 1:
                sums_ref[pl.ds(part // 2, 1), lanes] += column_sum(piece.astype(F32))


def first_back_kernel(plan, count, here, there, tokens, project_grad, resid_grad, lines, *refs):
    parts = refs[:count]
    tokens_ref, sums_ref = refs[count : count + 2]
    weight, small, sems = refs[count + 2 :]
    tube = pl.program_id(0)

    @pl.when(tube == 0)
    def _():
        copies = weight_copies(plan, here, there, parts, (weight, small), sems)
        for copy in copies:
            copy.start()
        for copy in copies:
            copy.wait()
        sums_ref[...] = jnp.zeros_like(sums_ref)

    grad = dot(project_grad[...], weight[...], NT)
    standard, inverse = standardize(tokens[...].astype(F32))
    inputs_grad = norm_back(grad, standard, inverse, lines[pl.ds(GAIN_ONE, 1), :])
    tokens_ref[...] = (resid_grad[...] + inputs_grad).astype(BF16)
    sums_ref[pl.ds(0, 1), :] += column_sum(grad * standard)
    sums_ref[pl.ds(1, 1), :] += column_sum(grad)


def block_out_kernel(plan, count, here, there, active, resid, lines, *refs):
    parts = refs[:count]
    out_ref = refs[count]
    weight, sems = refs[count + 1 :]

    @pl.when(pl.program_id(0) == 0)
    def _():
        copies = weight_copies(plan, here, there, parts, (weight,), sems)
        for copy in copies:
            copy.start()
        for copy in copies:
            copy.wait()

    branch = dot(active[...], weight[...]) + lines[pl.ds(BIAS_DOWN, 1), :]
    out_ref[...] = (resid[...] + branch).astype(BF16)


SMEM = pl.BlockSpec(memory_space=pltpu.SMEM)
HBM = pl.BlockSpec(memory_space=pl.ANY)


def rows_of(width, length):
    return pl.BlockSpec((length, width), lambda t: (t, 0))


def fixed(*shape):
    return pl.BlockSpec(shape, lambda t: (0,) * len(shape))


def shape_of(*shape, kind=BF16):
    return jax.ShapeDtypeStruct(shape, kind)


def call(kernel, name, grid, in_specs, outs, scratch, flops, moved, vmem, *args):
    return pl.pallas_call(
        kernel,
        grid=(grid,),
        in_specs=in_specs,
        out_specs=[spec for spec, _ in outs],
        out_shape=[shape for _, shape in outs],
        scratch_shapes=scratch,
        compiler_params=pltpu.CompilerParams(vmem_limit_bytes=vmem * MEBI),
        cost_estimate=pl.CostEstimate(flops=flops, bytes_accessed=moved, transcendentals=0),
        name=name,
    )(*args)


def local(
    tokens,
    clip_frames,
    tube_clip,
    first_gain,
    first_shift,
    qkv_weight,
    query_bias,
    value_bias,
    out_weight,
    out_bias,
    second_gain,
    second_shift,
    up_weight,
    up_bias,
    down_weight,
    down_bias,
    cotangent,
):
    shards = lax.axis_size("fsdp")
    depth, side = grid_of(shards)
    core = lax.axis_index("dp")
    here, there = place(shards, core), place(shards, 1 - core)
    total, width = tokens.shape
    tubes = tube_clip.shape[0]
    length = total // tubes
    clip_count = clip_frames.shape[0]
    matches = tube_clip[:, None] == jnp.arange(clip_count, dtype=jnp.int32)[None, :]
    frames = jnp.sum(jnp.where(matches, clip_frames[None, :], 0), axis=1)

    def half(matrix):
        columns = matrix.shape[1] // 2
        return lax.dynamic_slice_in_dim(matrix, core * columns, columns, axis=1)

    small = jnp.stack(
        [first_gain, first_shift, query_bias, value_bias, out_bias, second_gain, second_shift, down_bias],
        axis=1,
    )
    small = jnp.concatenate([small, up_bias.reshape(-1, 4)], axis=1)
    small = jnp.pad(small, ((0, 0), (0, LANES - 12)))
    wide, full, ff = qkv_weight.shape[1] // 2, out_weight.shape[1] // 2, up_weight.shape[1] // 2
    units = 2 * ff
    packs = (
        jnp.concatenate([half(qkv_weight), small], axis=1),
        jnp.concatenate([half(out_weight), half(up_weight)], axis=1),
        half(down_weight),
    )
    cuts = (
        ((0, wide, True), (wide, LANES, False)),
        ((0, full, True), (full, ff, True)),
        ((0, full, True),),
    )
    plans, parts, counts = [], [], []
    for pack, cut in zip(packs, cuts):
        own, other = gather(pack, shards)
        rows = pack.shape[0]
        if rows % 16 == 0:
            plans.append((depth, side, rows, cut))
            parts.append([*own, *other])
        else:
            plans.append(None)
            parts.append(assemble(own, other, shards, cut))
        counts.append(len(parts[-1]))
    number = [copies_of(plan, shards, cut) for plan, cut in zip(plans, cuts)]
    sem = pltpu.SemaphoreType.DMA

    normed_one, qkv, mixed, probs, lines = call(
        functools.partial(attend_kernel, plans[0], counts[0]),
        "attend",
        tubes,
        [SMEM, SMEM, SMEM, rows_of(width, length)] + [HBM] * counts[0],
        [
            (rows_of(width, length), shape_of(total, width)),
            (rows_of(3 * width, length), shape_of(total, 3 * width)),
            (rows_of(width, length), shape_of(total, width)),
            (
                pl.BlockSpec((1, HEADS, length, length), lambda t: (t, 0, 0, 0)),
                shape_of(tubes, HEADS, length, length),
            ),
            (fixed(16, width), shape_of(16, width, kind=F32)),
        ],
        [pltpu.VMEM((width, 3 * width), BF16), pltpu.VMEM((width, LANES), BF16), sem((number[0],))],
        10 * total * width * width,
        20 * MEBI,
        48,
        here, there, frames, tokens, *parts[0],
    )
    up_row = lines[8:12].T.reshape(1, units)

    resid, normed_two, active, slope, upstream = call(
        functools.partial(feed_kernel, plans[1], counts[1]),
        "feed",
        tubes,
        [SMEM, SMEM, SMEM, rows_of(width, length), rows_of(width, length), rows_of(width, length)]
        + [fixed(16, width), fixed(1, units)]
        + [HBM] * counts[1],
        [
            (rows_of(width, length), shape_of(total, width, kind=F32)),
            (rows_of(width, length), shape_of(total, width)),
            (rows_of(units, length), shape_of(total, units)),
            (rows_of(units, length), shape_of(total, units)),
            (rows_of(width, length), shape_of(total, width)),
        ],
        [pltpu.VMEM((width, width), BF16), pltpu.VMEM((width, units), BF16), sem((number[1],))],
        10 * total * width * width,
        20 * MEBI,
        48,
        here, there, frames, tokens, mixed, cotangent, lines, up_row, *parts[1],
    )

    down_half = reduce_half(active, upstream, shards)

    hidden_grad, resid_grad, attended_grad, mixed_grad, sums_two, up_sum = call(
        functools.partial(feed_back_kernel, plans[1:], counts[1:]),
        "feed_back",
        tubes,
        [SMEM, SMEM, rows_of(width, length), rows_of(units, length), rows_of(width, length), fixed(16, width)]
        + [HBM] * (counts[1] + counts[2]),
        [
            (rows_of(units, length), shape_of(total, units)),
            (rows_of(width, length), shape_of(total, width, kind=F32)),
            (rows_of(width, length), shape_of(total, width)),
            (rows_of(width, length), shape_of(total, width)),
            (fixed(8, width), shape_of(8, width, kind=F32)),
            (fixed(1, units), shape_of(1, units, kind=F32)),
        ],
        [
            pltpu.VMEM((width, width), BF16),
            pltpu.VMEM((width, units), BF16),
            pltpu.VMEM((units, width), BF16),
            sem((number[1] + number[2],)),
        ],
        18 * total * width * width,
        30 * MEBI,
        52,
        here, there, upstream, slope, resid, lines, *parts[1], *parts[2],
    )
    up_half = reduce_half(normed_two, hidden_grad, shards)
    out_half = reduce_half(mixed, attended_grad, shards)

    project_grad, sums_heads = call(
        attend_back_kernel,
        "attend_back",
        tubes,
        [
            rows_of(3 * width, length),
            pl.BlockSpec((1, HEADS, length, length), lambda t: (t, 0, 0, 0)),
            rows_of(width, length),
            rows_of(width, length),
        ],
        [
            (rows_of(3 * width, length), shape_of(total, 3 * width)),
            (fixed(8, width), shape_of(8, width, kind=F32)),
        ],
        [],
        10 * total * width * width,
        20 * MEBI,
        40,
        qkv, probs, mixed, mixed_grad,
    )
    qkv_half = reduce_half(normed_one, project_grad, shards)

    tokens_grad, sums_one = call(
        functools.partial(first_back_kernel, plans[0], counts[0]),
        "first_back",
        tubes,
        [SMEM, SMEM, rows_of(width, length), rows_of(3 * width, length), rows_of(width, length)]
        + [fixed(16, width)]
        + [HBM] * counts[0],
        [
            (rows_of(width, length), shape_of(total, width)),
            (fixed(8, width), shape_of(8, width, kind=F32)),
        ],
        [pltpu.VMEM((width, 3 * width), BF16), pltpu.VMEM((width, LANES), BF16), sem((number[0],))],
        6 * total * width * width,
        14 * MEBI,
        40,
        here, there, tokens, project_grad, resid_grad, lines, *parts[0],
    )
    (block_out,) = call(
        functools.partial(block_out_kernel, plans[2], counts[2]),
        "block_out",
        tubes,
        [SMEM, SMEM, rows_of(units, length), rows_of(width, length), fixed(16, width)] + [HBM] * counts[2],
        [(rows_of(width, length), shape_of(total, width))],
        [pltpu.VMEM((units, width), BF16), sem((number[2],))],
        8 * total * width * width,
        16 * MEBI,
        40,
        here, there, active, resid, lines, *parts[2],
    )

    vectors = (
        sums_one[0], sums_one[1], sums_heads[0], sums_heads[1], sums_two[SUM_BIAS_OUT],
        sums_two[SUM_GAIN_TWO], sums_two[SUM_SHIFT_TWO], sums_two[SUM_BIAS_DOWN], up_sum[0],
    )
    packed = jnp.concatenate([v.reshape(shards, -1) for v in vectors], axis=1).astype(BF16)
    packed = (packed.astype(F32) + arrive(packed, shards, "core", 1).astype(F32)).astype(BF16)
    small_sum = reduce_tail(relative(packed[:, None, :], shards), shards)[0].astype(F32)
    rows = first_gain.shape[0]
    pieces = [small_sum[k * rows : (k + 1) * rows] for k in range(8)] + [small_sum[8 * rows :]]
    return (
        block_out,
        tokens_grad,
        pieces[0],
        pieces[1],
        both_halves(qkv_half, shards),
        pieces[2],
        pieces[3],
        both_halves(out_half, shards),
        pieces[4],
        pieces[5],
        pieces[6],
        both_halves(up_half, shards),
        pieces[8],
        both_halves(down_half, shards),
        pieces[7],
    )


def solution(mesh):
    return jax.shard_map(
        local,
        mesh=mesh,
        in_specs=(
            P(("dp", "fsdp"), None),
            P(),
            P(("dp", "fsdp")),
            P("fsdp"),
            P("fsdp"),
            P("fsdp", None),
            P("fsdp"),
            P("fsdp"),
            P("fsdp", None),
            P("fsdp"),
            P("fsdp"),
            P("fsdp"),
            P("fsdp", None),
            P("fsdp"),
            P("fsdp", None),
            P("fsdp"),
            P(("dp", "fsdp"), None),
        ),
        out_specs=(
            P(("dp", "fsdp"), None),
            P(("dp", "fsdp"), None),
            P("fsdp"),
            P("fsdp"),
            P("fsdp", None),
            P("fsdp"),
            P("fsdp"),
            P("fsdp", None),
            P("fsdp"),
            P("fsdp"),
            P("fsdp"),
            P("fsdp", None),
            P("fsdp"),
            P("fsdp", None),
            P("fsdp"),
        ),
        check_vma=False,
    )
```

```python
import functools
import math

import jax
import jax.numpy as jnp
from jax import lax
from jax.experimental import pallas as pl
from jax.experimental.pallas import tpu as pltpu
from jax.sharding import PartitionSpec as P

HEADS = 12
HEAD_DIM = 64
PATCH = 16
EPSILON = 1e-05
SQRT_HALF = 0.7071067811865476
LOG2_E = 1.4426950408889634
LOG2_DENSITY = -1.3257480647361593
AXES = ("dp", "fsdp")
F32 = jnp.float32
BF16 = jnp.bfloat16
LANES = 128
MEBI = 1 << 20
VMEM_MOST = 60
SMEM = pl.BlockSpec(memory_space=pltpu.SMEM)
HBM = pl.BlockSpec(memory_space=pl.ANY)


def grid_of(shards):
    side = math.isqrt(shards // 4)
    assert 4 * side * side == shards
    return 4, side


def arrive(value, shards, kind, step):
    depth, side = grid_of(shards)
    pairs = []
    for core in range(2):
        for z in range(depth):
            for y in range(side):
                for x in range(side):
                    to = core * shards + (z * side + y) * side + x
                    at = [core, z, y, x]
                    if kind == "core":
                        at[0] = 1 - core
                    elif kind == "z":
                        at[1] = (z + step) % depth
                    elif (kind == "first") == (core == 0):
                        at[3] = (x + step) % side
                    else:
                        at[2] = (y + step) % side
                    pairs.append((at[0] * shards + (at[1] * side + at[2]) * side + at[3], to))
    with jax.named_scope(f"{kind}_exchange"):
        return lax.ppermute(value, AXES, pairs)


def place(shards, half):
    _, side = grid_of(shards)
    at = lax.axis_index("fsdp")
    z, y, x = at // (side * side), (at // side) % side, at % side
    first = jnp.where(half == 0, x, y)
    second = jnp.where(half == 0, y, x)
    return jnp.stack([half, z, first, second, lax.axis_index("dp")]).astype(jnp.int32)


def after(value, *earlier):
    return lax.optimization_barrier((value, *earlier))[0]


def spread_lines(vectors, shards):
    unit = jnp.concatenate(vectors)
    unit = jnp.pad(unit, (0, -unit.shape[0] % 1024)).reshape(1, -1, LANES)
    at = lax.broadcasted_iota(jnp.int32, (shards, 1, 1), 0) == lax.axis_index("fsdp")
    return jnp.where(at, unit, jnp.zeros_like(unit))


def join_lines(spread, count, rows):
    shards = spread.shape[0]
    whole = spread.reshape(shards, -1)[:, : count * rows].reshape(shards, count, rows)
    whole = whole.transpose(1, 0, 2).reshape(count, -1)
    return jnp.pad(whole.astype(F32), ((0, 16 - count), (0, 0)))


def gather_z(unit, shards):
    depth, _ = grid_of(shards)
    return jnp.stack([unit] + [arrive(unit, shards, "z", s) for s in range(1, depth)])


def gather_first(got, shards):
    _, side = grid_of(shards)
    return jnp.stack([got] + [arrive(got, shards, "first", s) for s in range(1, side)])


def gather_second(got, shards):
    _, side = grid_of(shards)
    return [got] + [arrive(got, shards, "second", s) for s in range(1, side)]


def gather_core(own, shards):
    return [arrive(part, shards, "core", 1) for part in own]


def row_of(where, depth, side, rel_second, rel_first, rel_z):
    z = lax.rem(where[1] + rel_z, depth)
    first = lax.rem(where[2] + rel_first, side)
    second = lax.rem(where[3] + rel_second, side)
    y = jnp.where(where[0] == 0, second, first)
    x = jnp.where(where[0] == 0, first, second)
    return (z * side + y) * side + x


def unroll_rows(parts, where, half, depth, side):
    rel = jnp.stack(parts)
    rel = jnp.roll(rel, where[3], axis=0)
    rel = jnp.roll(rel, where[2], axis=1)
    rel = jnp.roll(rel, where[1], axis=2)
    straight = jnp.where(half == 0, rel.transpose(2, 0, 1, 3, 4), rel.transpose(2, 1, 0, 3, 4))
    return straight.reshape(-1, rel.shape[-1])


def assemble(own, other, shards, cuts):
    depth, side = grid_of(shards)
    core = lax.axis_index("dp")
    here, there = place(shards, core), place(shards, 1 - core)
    mine = unroll_rows(own, here, core, depth, side)
    theirs = unroll_rows(other, there, 1 - core, depth, side)
    wholes = []
    for start, width, split in cuts:
        left, right = mine[:, start : start + width], theirs[:, start : start + width]
        if split:
            swapped = jnp.concatenate([right, left], axis=1)
            left = jnp.where(core == 0, jnp.concatenate([left, right], axis=1), swapped)
        wholes.append(left)
    return wholes


def tiles_of(widths):
    tiles, start = [], 0
    for k, width in enumerate(widths):
        at = 0
        while at < width:
            step = min(768, width - at)
            tiles.append((k, at, start + at, step))
            at += step
        start += width
    return tiles


def put_pieces(acc, sums, group, columns, where, depth, side, rows, deep, ahead):
    step = columns.stop - columns.start
    for second in range(side):
        for first in range(side):
            for z in range(deep):
                from_row = row_of(where, depth, side, second, first, z)
                if deep == 1:
                    from_row = lax.rem(from_row, side * side)
                piece = acc[pl.ds(pl.multiple_of(from_row * rows, 16), rows), :step]
                sums[group, second, first, ahead + z, :, columns] = piece.astype(BF16)


def grad_kernel(depth, side, rows, deep, widths, there, here, *refs):
    count = len(widths)
    layers = depth // deep
    tiles = tiles_of(widths)
    pairs, refs = refs[: 2 * count], refs[2 * count :]
    away, outs, refs = refs[0], refs[1 : 1 + side], refs[1 + side :]
    left, turned, right, acc, sums, left_sems, right_sems, out_sems = refs
    chunk = left.shape[2]

    def left_copy(k, layer):
        column = pl.multiple_of(lax.rem(there[1] + layer, layers) * chunk, LANES) if layers > 1 else 0
        return pltpu.make_async_copy(
            pairs[2 * k].at[:, pl.ds(column, chunk)], left.at[k * layers + layer], left_sems.at[k * layers + layer]
        )

    def right_copy(group, t):
        k, at, start, step = tiles[t]
        half = (there if group == 0 else here)[0]
        column = pl.multiple_of(half * widths[k] + at, LANES)
        return pltpu.make_async_copy(
            pairs[2 * k + 1].at[:, pl.ds(column, step)],
            right.at[group, :, pl.ds(start, step)],
            right_sems.at[group, t],
        )

    def out_copies(group):
        if group == 0:
            return [pltpu.make_async_copy(sums.at[0], away, out_sems.at[0])]
        return [pltpu.make_async_copy(sums.at[1, s], outs[s], out_sems.at[1 + s]) for s in range(side)]

    for layer in range(layers):
        for k in range(count):
            left_copy(k, layer).start()
            if layer == 0:
                for t in range(len(tiles)):
                    if tiles[t][0] == k:
                        right_copy(0, t).start()
    for t in range(len(tiles)):
        right_copy(1, t).start()
    for group in range(2):
        where = there if group == 0 else here
        for layer in range(layers):
            for t, (k, at, start, step) in enumerate(tiles):
                if group == 0 and at == 0:
                    left_copy(k, layer).wait()
                    turned[k * layers + layer] = left[k * layers + layer].T
                if layer == 0:
                    right_copy(group, t).wait()
                columns = slice(start, start + step)
                acc[:, :step] = dot(turned[k * layers + layer], right[group, :, columns])
                put_pieces(acc, sums, group, columns, where, depth, side, rows, deep, layer * deep)
        for copy in out_copies(group):
            copy.start()
    for group in range(2):
        for copy in out_copies(group):
            copy.wait()


def rel_grad(pairs, shards):
    depth, side = grid_of(shards)
    length, features = pairs[0][0].shape
    widths = [rhs.shape[1] // 2 for _, rhs in pairs]
    width = sum(widths)
    rows = features // shards
    core = lax.axis_index("dp")
    there, here = place(shards, 1 - core), place(shards, core)
    if rows % 16 != 0:
        both = []
        for half, where in ((1 - core, there), (core, here)):
            wholes = [
                lax.dot_general(
                    lhs,
                    lax.dynamic_slice_in_dim(rhs, half * (rhs.shape[1] // 2), rhs.shape[1] // 2, axis=1),
                    (((0,), (0,)), ((), ())),
                    preferred_element_type=F32,
                )
                for lhs, rhs in pairs
            ]
            whole = jnp.concatenate(wholes, axis=1).reshape(depth, side, side, rows, width)
            rel = jnp.where(half == 0, whole.transpose(1, 2, 0, 3, 4), whole.transpose(2, 1, 0, 3, 4))
            rel = jnp.roll(rel, -where[3], axis=0)
            rel = jnp.roll(rel, -where[2], axis=1)
            both.append(jnp.roll(rel, -where[1], axis=2).astype(BF16))
        return both[0], [both[1][s] for s in range(side)]
    deep = depth if features <= 1024 else 1
    chunk = features if deep > 1 else features // depth
    layers = depth // deep
    count, pieces = len(pairs), len(tiles_of(widths))
    out = pl.pallas_call(
        functools.partial(grad_kernel, depth, side, rows, deep, widths),
        in_specs=[SMEM, SMEM] + [HBM] * (2 * count),
        out_specs=[HBM] * (1 + side),
        out_shape=[jax.ShapeDtypeStruct((side, side, depth, rows, width), BF16)]
        + [jax.ShapeDtypeStruct((side, depth, rows, width), BF16)] * side,
        scratch_shapes=[
            pltpu.VMEM((count * layers, length, chunk), BF16),
            pltpu.VMEM((count * layers, chunk, length), BF16),
            pltpu.VMEM((2, length, width), BF16),
            pltpu.VMEM((chunk, min(768, max(widths))), F32),
            pltpu.VMEM((2, side, side, depth, rows, width), BF16),
            pltpu.SemaphoreType.DMA((count * layers,)),
            pltpu.SemaphoreType.DMA((2, pieces)),
            pltpu.SemaphoreType.DMA((1 + side,)),
        ],
        compiler_params=pltpu.CompilerParams(vmem_limit_bytes=VMEM_MOST * MEBI),
        cost_estimate=pl.CostEstimate(flops=4 * length * features * width, bytes_accessed=20 * MEBI, transcendentals=0),
        name="grad",
    )(there, here, *(operand for pair in pairs for operand in pair))
    return out[0], out[1:]


def sum_of(*values):
    total = values[0].astype(F32)
    for value in values[1:]:
        total = total + value.astype(F32)
    return total.astype(BF16)


def reduce_second(own, got, shards):
    _, side = grid_of(shards)
    came = [arrive(sum_of(own[s], got[s]), shards, "second", side - s) for s in range(1, side)]
    return [sum_of(own[0][f], got[0, f], *(part[f] for part in came)) for f in range(side)]


def reduce_first(sums, shards):
    depth, side = grid_of(shards)
    came = [arrive(sums[f], shards, "first", side - f) for f in range(1, side)]
    return [sum_of(sums[0][z], *(part[z] for part in came)) for z in range(depth)]


def reduce_z(sums, shards):
    depth, _ = grid_of(shards)
    return sum_of(sums[0], *(arrive(sums[z], shards, "z", depth - z) for z in range(1, depth)))


def exchange_lines(lines, shards, kind):
    depth, side = grid_of(shards)
    count = {"z": depth, "core": 2}.get(kind, side)
    return sum_of(lines, *(arrive(lines, shards, kind, step) for step in range(1, count)))


def both_halves(mine, shards, widths):
    theirs = arrive(mine, shards, "core", 1)
    core = lax.axis_index("dp")
    left = jnp.where(core == 0, mine, theirs)
    right = jnp.where(core == 0, theirs, mine)
    wholes, start = [], 0
    for width in widths:
        columns = slice(start, start + width)
        wholes.append(jnp.concatenate([left[:, columns], right[:, columns]], axis=1).astype(F32))
        start += width
    return wholes


GAIN_ONE, SHIFT_ONE, BIAS_QUERY, BIAS_VALUE, BIAS_OUT, GAIN_TWO, SHIFT_TWO, BIAS_DOWN = range(8)
SCALE = HEAD_DIM ** (-0.5)


def weight_copies(plan, here, there, parts, outs, sems, first=0):
    groups = [[] for _ in outs]
    if plan is None:
        for k, (part, out) in enumerate(zip(parts, outs)):
            groups[k].append(pltpu.make_async_copy(part, out, sems.at[first + k]))
        return groups
    depth, side, rows, cuts = plan
    used = first
    for group in range(2):
        where = here if group == 0 else there
        for second in range(side):
            for ahead in range(side):
                for z in range(depth):
                    at = pl.multiple_of(row_of(where, depth, side, second, ahead, z) * rows, 16)
                    source = parts[group * side + second].at[ahead, z]
                    for k, ((start, width, split), out) in enumerate(zip(cuts, outs)):
                        if group == 1 and not split:
                            continue
                        column = pl.multiple_of(where[0] * width, LANES) if split else 0
                        groups[k].append(
                            pltpu.make_async_copy(
                                source.at[:, pl.ds(start, width)],
                                out.at[pl.ds(at, rows), pl.ds(column, width)],
                                sems.at[used],
                            )
                        )
                        used += 1
    return groups


def bring(groups):
    for group in groups:
        for copy in group:
            copy.start()
    for group in groups:
        for copy in group:
            copy.wait()


def copies_of(plan, shards, cuts):
    if plan is None:
        return len(cuts)
    return shards * sum(2 if split else 1 for _, _, split in cuts)


def standardize(values):
    average = jnp.mean(values, axis=-1, keepdims=True)
    centred = values - average
    spread = jnp.mean(centred * centred, axis=-1, keepdims=True)
    inverse = lax.rsqrt(spread + EPSILON)
    return centred * inverse, inverse


def dot(a, b, dims=((1,), (0,))):
    return lax.dot_general(a, b, (dims, ((), ())), preferred_element_type=F32)


NT = ((1,), (1,))
TN = ((0,), (0,))


def project_kernel(plan, count, here, there, tokens, lines, *refs):
    parts = refs[:count]
    normed_ref, qkv_ref = refs[count : count + 2]
    weight, sems = refs[count + 2 :]
    width = tokens.shape[1]

    @pl.when(pl.program_id(0) == 0)
    def _():
        bring(weight_copies(plan, here, there, parts, (weight,), sems))

    standard, _ = standardize(tokens[...].astype(F32))
    normed = (standard * lines[pl.ds(GAIN_ONE, 1), :] + lines[pl.ds(SHIFT_ONE, 1), :]).astype(BF16)
    normed_ref[...] = normed
    bias = (lines[pl.ds(BIAS_QUERY, 1), :], None, lines[pl.ds(BIAS_VALUE, 1), :])
    for part in range(3):
        columns = slice(part * width, (part + 1) * width)
        project = dot(normed, weight[:, columns])
        if bias[part] is not None:
            project = project + bias[part]
        qkv_ref[:, columns] = project.astype(BF16)


def attend_kernel(frames, qkv_ref, mixed_ref, power_ref, inverse_ref):
    tube = pl.program_id(0)
    length, width = mixed_ref.shape
    mask = jnp.where(lax.broadcasted_iota(jnp.int32, (1, length), 1) < frames[tube] * PATCH, 0.0, -1e30)
    lower = lax.broadcasted_iota(jnp.int32, (length, LANES), 1) < HEAD_DIM
    ones = jnp.ones((length, LANES), BF16)
    for pair in range(width // LANES):
        query = qkv_ref[:, pair * LANES : (pair + 1) * LANES] * jnp.asarray(SCALE, BF16)
        keys = qkv_ref[:, width + pair * LANES : width + (pair + 1) * LANES]
        values = qkv_ref[:, 2 * width + pair * LANES : 2 * width + (pair + 1) * LANES]
        values = jnp.concatenate([values, ones], axis=1)
        both = []
        for k in range(2):
            own = jnp.where(lower if k == 0 else ~lower, query, jnp.zeros_like(query))
            scores = dot(own, keys, NT) + mask
            power = jnp.exp(scores - jnp.max(scores, axis=-1, keepdims=True)).astype(BF16)
            power_ref[0, 2 * pair + k] = power
            both.append(dot(power, values))
        inverse = 1.0 / jnp.where(lower, both[0][:, LANES:], both[1][:, LANES:])
        inverse_ref[:, pair * LANES : (pair + 1) * LANES] = inverse.astype(BF16)
        mixed = jnp.where(lower, both[0][:, :LANES], both[1][:, :LANES]) * inverse
        mixed_ref[:, pair * LANES : (pair + 1) * LANES] = mixed.astype(BF16)


def feed_kernel(plan, count, here, there, frames, tokens, mixed, cotangent, lines, up_bias, *refs):
    parts = refs[:count]
    resid_ref, normed_ref, active_ref, slope_ref, upstream_ref = refs[count : count + 5]
    out_weight, up_weight, sems = refs[count + 5 :]
    tube = pl.program_id(0)
    first, last = weight_copies(plan, here, there, parts, (out_weight, up_weight), sems)

    @pl.when(tube == 0)
    def _():
        for copy in first + last:
            copy.start()
        for copy in first:
            copy.wait()

    length = tokens.shape[0]
    row_ok = lax.broadcasted_iota(jnp.int32, (length, 1), 0) < frames[tube] * PATCH
    upstream_ref[...] = jnp.where(row_ok, cotangent[...], jnp.zeros_like(cotangent))
    attended = dot(mixed[...], out_weight[...]) + lines[pl.ds(BIAS_OUT, 1), :]
    resid = tokens[...].astype(F32) + attended
    resid_ref[...] = resid.astype(BF16)
    standard, _ = standardize(resid)
    normed = (standard * lines[pl.ds(GAIN_TWO, 1), :] + lines[pl.ds(SHIFT_TWO, 1), :]).astype(BF16)
    normed_ref[...] = normed

    @pl.when(tube == 0)
    def _():
        for copy in last:
            copy.wait()

    units = up_weight.shape[1]
    step = 512
    for at in range(0, units, step):
        hidden = dot(normed, up_weight[:, at : at + step]) + up_bias[:, at : at + step]
        cumulative = 0.5 + 0.5 * lax.erf(hidden * SQRT_HALF)
        density = jnp.exp2(hidden * hidden * (-0.5 * LOG2_E) + LOG2_DENSITY)
        active_ref[:, at : at + step] = (hidden * cumulative).astype(BF16)
        slope_ref[:, at : at + step] = (cumulative + hidden * density).astype(BF16)


def norm_back(grad, standard, inverse, gain):
    scaled = grad * gain
    first = jnp.mean(scaled, axis=-1, keepdims=True)
    second = jnp.mean(scaled * standard, axis=-1, keepdims=True)
    return inverse * (scaled - first - standard * second)


def column_sum(values):
    return jnp.sum(values, axis=0, keepdims=True)


SUM_GAIN_TWO, SUM_SHIFT_TWO, SUM_BIAS_OUT, SUM_BIAS_DOWN = range(4)


def feed_back_kernel(plans, counts, depth, side, rows, direct, here, there, upstream, slope, resid, inverse_sums, lines, *refs):
    mixed_hbm, normed_hbm, refs = refs[0], refs[1], refs[2:]
    ff_parts, refs = refs[: counts[0]], refs[counts[0] :]
    down_parts, refs = refs[: counts[1]], refs[counts[1] :]
    attended_ref, scaled_ref, sums_ref, up_sum_ref = refs[:4]
    refs = refs[4:]
    if direct:
        away, outs, refs = refs[0], refs[1 : 1 + side], refs[1 + side :]
    else:
        hidden_hbm, refs = refs[0], refs[1:]
    out_weight, up_weight, down_weight, hidden_all, attended_all, sems, more_sems = refs[:7]
    tube, last = pl.program_id(0), pl.num_programs(0) - 1
    length, width = upstream.shape
    units = up_weight.shape[1]
    (down_copies,) = weight_copies(plans[1], here, there, down_parts, (down_weight,), sems)
    ff_copies = weight_copies(plans[0], here, there, ff_parts, (out_weight, up_weight), sems, len(down_copies))
    if direct:
        left, turned, acc, sums = refs[7:]
        left_copies = [
            pltpu.make_async_copy(mixed_hbm, left.at[0], more_sems.at[0]),
            pltpu.make_async_copy(normed_hbm, left.at[1], more_sems.at[1]),
        ]

    @pl.when(tube == 0)
    def _():
        for copy in down_copies:
            copy.start()
        for group in reversed(ff_copies):
            for copy in group:
                copy.start()
        if direct:
            for copy in left_copies:
                copy.start()
        sums_ref[...] = jnp.zeros_like(sums_ref)
        up_sum_ref[...] = jnp.zeros_like(up_sum_ref)
        for copy in down_copies:
            copy.wait()

    here_rows = pl.ds(pl.multiple_of(tube * length, 16), length)
    low = upstream[...]
    step = 768
    for at in range(0, units, step):
        grad = dot(low, down_weight[at : at + step, :], NT) * slope[:, at : at + step].astype(F32)
        hidden_all[here_rows, at : at + step] = grad.astype(BF16)
        up_sum_ref[:, at : at + step] += column_sum(grad)

    @pl.when(tube == 0)
    def _():
        for group in ff_copies:
            for copy in group:
                copy.wait()

    normed_grad = dot(hidden_all[here_rows, :], up_weight[...], NT)
    standard, inverse = standardize(resid[...].astype(F32))
    above = low.astype(F32)
    resid_grad = above + norm_back(normed_grad, standard, inverse, lines[pl.ds(GAIN_TWO, 1), :])
    attended_grad = resid_grad.astype(BF16)
    attended_ref[...] = attended_grad
    attended_all[here_rows, :] = attended_grad
    scaled_ref[...] = (dot(attended_grad, out_weight[...], NT) * inverse_sums[...].astype(F32)).astype(BF16)
    sums_ref[pl.ds(SUM_GAIN_TWO, 1), :] += column_sum(normed_grad * standard)
    sums_ref[pl.ds(SUM_SHIFT_TWO, 1), :] += column_sum(normed_grad)
    sums_ref[pl.ds(SUM_BIAS_OUT, 1), :] += column_sum(attended_grad.astype(F32))
    sums_ref[pl.ds(SUM_BIAS_DOWN, 1), :] += column_sum(above)

    if not direct:

        @pl.when(tube == last)
        def _():
            copy = pltpu.make_async_copy(hidden_all, hidden_hbm, more_sems.at[0])
            copy.start()
            copy.wait()

        return

    @pl.when(tube == 1)
    def _():
        for k in range(2):
            left_copies[k].wait()
            turned[k] = left[k].T

    @pl.when(tube == last)
    def _():
        waits = []
        for group in range(2):
            where = there if group == 0 else here
            for k, at, start, size in tiles_of((width // 2, units // 2)):
                right = attended_all if k == 0 else hidden_all
                column = pl.multiple_of(where[0] * (right.shape[1] // 2) + at, LANES)
                acc[:, :size] = dot(turned[k], right[:, pl.ds(column, size)])
                put_pieces(acc, sums, group, slice(start, start + size), where, depth, side, rows, depth, 0)
            if group == 0:
                waits.append(pltpu.make_async_copy(sums.at[0], away, more_sems.at[2]))
                waits[-1].start()
            else:
                for s in range(side):
                    waits.append(pltpu.make_async_copy(sums.at[1, s], outs[s], more_sems.at[3 + s]))
                    waits[-1].start()
        for copy in waits:
            copy.wait()


def attend_back_kernel(qkv, power_ref, mixed, scaled_grad, grad_ref, sums_ref):
    tube = pl.program_id(0)

    @pl.when(tube == 0)
    def _():
        sums_ref[...] = jnp.zeros_like(sums_ref)

    length, width = mixed.shape
    lower = lax.broadcasted_iota(jnp.int32, (length, LANES), 1) < HEAD_DIM
    for pair in range(width // LANES):
        lanes = slice(pair * LANES, (pair + 1) * LANES)
        query = qkv[:, lanes]
        keys = qkv[:, width + pair * LANES : width + (pair + 1) * LANES]
        values = qkv[:, 2 * width + pair * LANES : 2 * width + (pair + 1) * LANES]
        above = scaled_grad[:, lanes]
        product = above.astype(F32) * mixed[:, lanes].astype(F32)
        query_grad, keys_grad, values_grad = [], [], []
        for k in range(2):
            mine = lower if k == 0 else ~lower
            own = jnp.where(mine, above, jnp.zeros_like(above))
            power = power_ref[0, 2 * pair + k]
            inner = jnp.sum(jnp.where(mine, product, 0.0), axis=-1, keepdims=True)
            scores_grad = (power.astype(F32) * (dot(own, values, NT) - inner)).astype(BF16)
            values_grad.append(dot(power, above, TN))
            query_grad.append(dot(scores_grad, keys))
            keys_grad.append(dot(scores_grad, query, TN))
        for part, (pieces, scale) in enumerate(((query_grad, SCALE), (keys_grad, SCALE), (values_grad, None))):
            piece = jnp.where(lower, pieces[0], pieces[1])
            if scale is not None:
                piece = piece * scale
            grad_ref[:, part * width + pair * LANES : part * width + (pair + 1) * LANES] = piece.astype(BF16)
            if part != 1:
                sums_ref[pl.ds(part // 2, 1), lanes] += column_sum(piece)


def first_back_kernel(plan, count, here, there, tokens, project_grad, attended_grad, lines, *refs):
    parts = refs[:count]
    tokens_ref, sums_ref = refs[count : count + 2]
    weight, sems = refs[count + 2 :]
    tube = pl.program_id(0)

    @pl.when(tube == 0)
    def _():
        bring(weight_copies(plan, here, there, parts, (weight,), sems))
        sums_ref[...] = jnp.zeros_like(sums_ref)

    grad = dot(project_grad[...], weight[...], NT)
    standard, inverse = standardize(tokens[...].astype(F32))
    inputs_grad = norm_back(grad, standard, inverse, lines[pl.ds(GAIN_ONE, 1), :])
    tokens_ref[...] = (attended_grad[...].astype(F32) + inputs_grad).astype(BF16)
    sums_ref[pl.ds(0, 1), :] += column_sum(grad * standard)
    sums_ref[pl.ds(1, 1), :] += column_sum(grad)


def block_out_kernel(plan, count, here, there, active, resid, lines, *refs):
    parts = refs[:count]
    out_ref = refs[count]
    weight, sems = refs[count + 1 :]

    @pl.when(pl.program_id(0) == 0)
    def _():
        bring(weight_copies(plan, here, there, parts, (weight,), sems))

    branch = dot(active[...], weight[...]) + lines[pl.ds(BIAS_DOWN, 1), :]
    out_ref[...] = (resid[...].astype(F32) + branch).astype(BF16)


def rows_of(width, length):
    return pl.BlockSpec((length, width), lambda t: (t, 0))


def fixed(*shape):
    return pl.BlockSpec(shape, lambda t: (0,) * len(shape))


def shape_of(*shape, kind=BF16):
    return jax.ShapeDtypeStruct(shape, kind)


def call(kernel, name, grid, in_specs, outs, scratch, flops, *args):
    return pl.pallas_call(
        kernel,
        grid=(grid,),
        in_specs=in_specs,
        out_specs=[spec for spec, _ in outs],
        out_shape=[shape for _, shape in outs],
        scratch_shapes=scratch,
        compiler_params=pltpu.CompilerParams(vmem_limit_bytes=VMEM_MOST * MEBI),
        cost_estimate=pl.CostEstimate(flops=flops, bytes_accessed=16 * MEBI, transcendentals=0),
        name=name,
    )(*args)


def local(
    tokens,
    clip_frames,
    tube_clip,
    first_gain,
    first_shift,
    qkv_weight,
    query_bias,
    value_bias,
    out_weight,
    out_bias,
    second_gain,
    second_shift,
    up_weight,
    up_bias,
    down_weight,
    down_bias,
    cotangent,
):
    shards = lax.axis_size("fsdp")
    depth, side = grid_of(shards)
    core = lax.axis_index("dp")
    here, there = place(shards, core), place(shards, 1 - core)
    total, width = tokens.shape
    tubes = tube_clip.shape[0]
    length = total // tubes
    clip_count = clip_frames.shape[0]
    matches = tube_clip[:, None] == jnp.arange(clip_count, dtype=jnp.int32)[None, :]
    frames = jnp.sum(jnp.where(matches, clip_frames[None, :], 0), axis=1)

    def half(matrix):
        columns = matrix.shape[1] // 2
        return lax.dynamic_slice_in_dim(matrix, core * columns, columns, axis=1)

    wide, full, ff = qkv_weight.shape[1] // 2, out_weight.shape[1] // 2, up_weight.shape[1] // 2
    units = 2 * ff
    rows = first_gain.shape[0]
    vectors = [first_gain, first_shift, query_bias, value_bias, out_bias, second_gain, second_shift, down_bias]
    vectors += [up_bias[k * rows : (k + 1) * rows] for k in range(4)]
    pack_one = half(qkv_weight)
    pack_two = jnp.concatenate([half(out_weight), half(up_weight)], axis=1)
    pack_three = half(down_weight)
    cuts = (
        ((0, wide, True),),
        ((0, full, True), (full, ff, True)),
        ((0, full, True),),
    )
    plans, counts = [], []
    for pack, cut in zip((pack_one, pack_two, pack_three), cuts):
        direct = pack.shape[0] % 16 == 0
        plans.append((depth, side, pack.shape[0], cut) if direct else None)
        counts.append(2 * side if direct else len(cut))

    def finish(k, own, other):
        return [*own, *other] if plans[k] is not None else assemble(own, other, shards, cuts[k])

    number = [copies_of(plan, shards, cut) for plan, cut in zip(plans, cuts)]
    sem = pltpu.SemaphoreType.DMA
    big = 2 * total * width * width
    narrow, wide_rows, deep_rows = rows_of(width, length), rows_of(3 * width, length), rows_of(units, length)
    tall = total // 2
    tall_narrow, tall_wide, tall_deep = rows_of(width, tall), rows_of(3 * width, tall), rows_of(units, tall)
    probs_spec = pl.BlockSpec((1, HEADS, length, length), lambda t: (t, 0, 0, 0))

    z_one = gather_z(pack_one, shards)
    spread = spread_lines(vectors, shards)
    z_one, spread, pack_two, pack_three = lax.optimization_barrier((z_one, spread, pack_two, pack_three))
    first_one = gather_first(z_one, shards)
    spread = exchange_lines(spread, shards, "first")
    first_one, spread, pack_two = lax.optimization_barrier((first_one, spread, pack_two))
    second_one = gather_second(first_one, shards)
    z_two = gather_z(pack_two, shards)
    spread = exchange_lines(spread, shards, "z")
    second_one, z_two, pack_three, spread = lax.optimization_barrier((second_one, z_two, pack_three, spread))
    core_one = gather_core(second_one, shards)
    lines = join_lines(exchange_lines(spread, shards, "second"), len(vectors), rows)
    core_one, z_two, pack_three, tokens, lines = lax.optimization_barrier((core_one, z_two, pack_three, tokens, lines))
    parts_one = finish(0, second_one, core_one)
    first_two = gather_first(z_two, shards)

    normed_one, qkv = call(
        functools.partial(project_kernel, plans[0], counts[0]),
        "project",
        tubes,
        [SMEM, SMEM, narrow, fixed(16, width)] + [HBM] * counts[0],
        [(narrow, shape_of(total, width)), (wide_rows, shape_of(total, 3 * width))],
        [pltpu.VMEM((width, 3 * width), BF16), sem((number[0],))],
        3 * big,
        here, there, tokens, lines, *parts_one,
    )
    first_two, pack_three, qkv = lax.optimization_barrier((first_two, pack_three, qkv))
    second_two = gather_second(first_two, shards)
    z_three = gather_z(pack_three, shards)

    mixed, power, inverse = call(
        attend_kernel,
        "attend",
        tubes,
        [SMEM, wide_rows],
        [
            (narrow, shape_of(total, width)),
            (probs_spec, shape_of(tubes, HEADS, length, length)),
            (narrow, shape_of(total, width)),
        ],
        [],
        4 * big,
        frames, qkv,
    )
    up_row = lines[8:12].reshape(4, shards, rows).transpose(1, 0, 2).reshape(1, units)
    second_two, mixed, z_three = lax.optimization_barrier((second_two, mixed, z_three))
    core_two = gather_core(second_two, shards)
    core_two, z_three, mixed = lax.optimization_barrier((core_two, z_three, mixed))
    parts_two = finish(1, second_two, core_two)
    first_three = gather_first(z_three, shards)

    resid, normed_two, active, slope, upstream = call(
        functools.partial(feed_kernel, plans[1], counts[1]),
        "feed",
        tubes,
        [SMEM, SMEM, SMEM, narrow, narrow, narrow, fixed(16, width), fixed(1, units)] + [HBM] * counts[1],
        [
            (narrow, shape_of(total, width)),
            (narrow, shape_of(total, width)),
            (deep_rows, shape_of(total, units)),
            (deep_rows, shape_of(total, units)),
            (narrow, shape_of(total, width)),
        ],
        [pltpu.VMEM((width, width), BF16), pltpu.VMEM((width, units), BF16), sem((number[1],))],
        8 * big,
        here, there, frames, tokens, mixed, cotangent, lines, up_row, *parts_two,
    )
    first_three, active, upstream = lax.optimization_barrier((first_three, active, upstream))
    second_three = gather_second(first_three, shards)
    down_away, down_own = rel_grad([(active, upstream)], shards)
    second_three, down_away, slope = lax.optimization_barrier((second_three, down_away, slope))
    core_three = gather_core(second_three, shards)
    down_got = arrive(down_away, shards, "core", 1)
    core_three, down_got, slope = lax.optimization_barrier((core_three, down_got, slope))
    parts_three = finish(2, second_three, core_three)
    down_second = reduce_second(down_own, down_got, shards)

    direct = rows % 16 == 0
    ff_width = full + ff
    outs = [
        (narrow, shape_of(total, width)),
        (narrow, shape_of(total, width)),
        (fixed(8, width), shape_of(8, width, kind=F32)),
        (fixed(1, units), shape_of(1, units, kind=F32)),
    ]
    scratch = [
        pltpu.VMEM((width, width), BF16),
        pltpu.VMEM((width, units), BF16),
        pltpu.VMEM((units, width), BF16),
        pltpu.VMEM((total, units), BF16),
        pltpu.VMEM((total, width), BF16),
        sem((number[1] + number[2],)),
        sem((3 + side,)),
    ]
    if direct:
        outs.append((HBM, shape_of(side, side, depth, rows, ff_width)))
        outs += [(HBM, shape_of(side, depth, rows, ff_width))] * side
        scratch += [
            pltpu.VMEM((2, total, width), BF16),
            pltpu.VMEM((2, width, total), BF16),
            pltpu.VMEM((width, 768), F32),
            pltpu.VMEM((2, side, side, depth, rows, ff_width), BF16),
        ]
    else:
        outs.append((HBM, shape_of(total, units)))
    attended_grad, scaled_grad, sums_two, up_sum, *more = call(
        functools.partial(feed_back_kernel, plans[1:], counts[1:], depth, side, rows, direct),
        "feed_back",
        tubes,
        [SMEM, SMEM, narrow, deep_rows, narrow, narrow, fixed(16, width)] + [HBM] * (2 + counts[1] + counts[2]),
        outs,
        scratch,
        14 * big,
        here, there, upstream, slope, resid, inverse, lines, mixed, normed_two, *parts_two, *parts_three,
    )
    if direct:
        ff_away, ff_own = more[0], more[1:]
    else:
        ff_away, ff_own = rel_grad([(mixed, attended_grad), (normed_two, more[0])], shards)
    down_second, ff_away, scaled_grad = lax.optimization_barrier((down_second, ff_away, scaled_grad))
    ff_got = arrive(ff_away, shards, "core", 1)
    down_first = reduce_first(down_second, shards)

    project_grad, sums_heads = call(
        attend_back_kernel,
        "attend_back",
        tubes,
        [wide_rows, probs_spec, narrow, narrow],
        [(wide_rows, shape_of(total, 3 * width)), (fixed(8, width), shape_of(8, width, kind=F32))],
        [],
        4 * big,
        qkv, power, mixed, scaled_grad,
    )
    ff_got, down_first, project_grad = lax.optimization_barrier((ff_got, down_first, project_grad))
    ff_second = reduce_second(ff_own, ff_got, shards)
    down_half = reduce_z(down_first, shards)
    qkv_away, qkv_own = rel_grad([(normed_one, project_grad)], shards)
    qkv_away, project_grad, ff_second, down_half = lax.optimization_barrier((qkv_away, project_grad, ff_second, down_half))
    qkv_got = arrive(qkv_away, shards, "core", 1)
    ff_first = reduce_first(ff_second, shards)
    (down_whole,) = both_halves(down_half, shards, (full,))

    tokens_grad, sums_one = call(
        functools.partial(first_back_kernel, plans[0], counts[0]),
        "first_back",
        2,
        [SMEM, SMEM, tall_narrow, tall_wide, tall_narrow, fixed(16, width)] + [HBM] * counts[0],
        [(tall_narrow, shape_of(total, width)), (fixed(8, width), shape_of(8, width, kind=F32))],
        [pltpu.VMEM((width, 3 * width), BF16), sem((number[0],))],
        3 * big,
        here, there, tokens, project_grad, attended_grad, lines, *parts_one,
    )
    qkv_got, ff_first, tokens_grad, sums_one, active = lax.optimization_barrier(
        (qkv_got, ff_first, tokens_grad, sums_one, active)
    )
    sums = jnp.concatenate(
        [
            sums_one[:2],
            sums_heads[:2],
            sums_two[SUM_BIAS_OUT : SUM_BIAS_OUT + 1],
            sums_two[SUM_GAIN_TWO : SUM_GAIN_TWO + 1],
            sums_two[SUM_SHIFT_TWO : SUM_SHIFT_TWO + 1],
            sums_two[SUM_BIAS_DOWN : SUM_BIAS_DOWN + 1],
            up_sum.reshape(-1, width),
        ],
        axis=0,
    ).astype(BF16)
    qkv_second = reduce_second(qkv_own, qkv_got, shards)
    ff_half = reduce_z(ff_first, shards)
    sums = exchange_lines(sums, shards, "first")

    (block_out,) = call(
        functools.partial(block_out_kernel, plans[2], counts[2]),
        "block_out",
        tubes,
        [SMEM, SMEM, deep_rows, narrow, fixed(16, width)] + [HBM] * counts[2],
        [(narrow, shape_of(total, width))],
        [pltpu.VMEM((units, width), BF16), sem((number[2],))],
        4 * big,
        here, there, active, resid, lines, *parts_three,
    )
    qkv_second, ff_half, block_out, sums = lax.optimization_barrier((qkv_second, ff_half, block_out, sums))
    qkv_first = reduce_first(qkv_second, shards)
    out_whole, up_whole = both_halves(ff_half, shards, (full, ff))
    sums = exchange_lines(sums, shards, "second")
    qkv_first, sums, out_whole, up_whole = lax.optimization_barrier((qkv_first, sums, out_whole, up_whole))
    qkv_half = reduce_z(qkv_first, shards)
    sums = exchange_lines(sums, shards, "z")
    qkv_half, sums = lax.optimization_barrier((qkv_half, sums))
    sums = exchange_lines(sums, shards, "core")
    (qkv_whole,) = both_halves(qkv_half, shards, (wide,))
    at = lax.axis_index("fsdp")
    sums_here = lax.dynamic_slice_in_dim(sums[:8], at * rows, rows, axis=1).astype(F32)
    up_here = lax.dynamic_slice_in_dim(sums[8:].reshape(-1), at * up_bias.shape[0], up_bias.shape[0]).astype(F32)
    return (
        block_out,
        tokens_grad,
        sums_here[0],
        sums_here[1],
        qkv_whole,
        sums_here[2],
        sums_here[3],
        out_whole,
        sums_here[4],
        sums_here[5],
        sums_here[6],
        up_whole,
        up_here,
        down_whole,
        sums_here[7],
    )


def solution(mesh):
    return jax.shard_map(
        local,
        mesh=mesh,
        in_specs=(
            P(("dp", "fsdp"), None),
            P(),
            P(("dp", "fsdp")),
            P("fsdp"),
            P("fsdp"),
            P("fsdp", None),
            P("fsdp"),
            P("fsdp"),
            P("fsdp", None),
            P("fsdp"),
            P("fsdp"),
            P("fsdp"),
            P("fsdp", None),
            P("fsdp"),
            P("fsdp", None),
            P("fsdp"),
            P(("dp", "fsdp"), None),
        ),
        out_specs=(
            P(("dp", "fsdp"), None),
            P(("dp", "fsdp"), None),
            P("fsdp"),
            P("fsdp"),
            P("fsdp", None),
            P("fsdp"),
            P("fsdp"),
            P("fsdp", None),
            P("fsdp"),
            P("fsdp"),
            P("fsdp"),
            P("fsdp", None),
            P("fsdp"),
            P("fsdp", None),
            P("fsdp"),
        ),
        check_vma=False,
    )
```

```python
import functools
import math

import jax
import jax.numpy as jnp
from jax import lax
from jax.experimental import pallas as pl
from jax.experimental.pallas import tpu as pltpu
from jax.sharding import PartitionSpec as P

HEADS = 12
HEAD_DIM = 64
PATCH = 16
EPSILON = 1e-05
SQRT_HALF = 0.7071067811865476
LOG2_E = 1.4426950408889634
LOG2_DENSITY = -1.3257480647361593
AXES = ("dp", "fsdp")
F32 = jnp.float32
BF16 = jnp.bfloat16
LANES = 128
MEBI = 1 << 20
VMEM_MOST = 53
SMEM = pl.BlockSpec(memory_space=pltpu.SMEM)
HBM = pl.BlockSpec(memory_space=pl.ANY)


def grid_of(shards):
    side = math.isqrt(shards // 4)
    assert 4 * side * side == shards
    return 4, side


def arrive(value, shards, kind, step):
    depth, side = grid_of(shards)
    pairs = []
    for core in range(2):
        for z in range(depth):
            for y in range(side):
                for x in range(side):
                    to = core * shards + (z * side + y) * side + x
                    at = [core, z, y, x]
                    if kind == "core":
                        at[0] = 1 - core
                    elif kind == "z":
                        at[1] = (z + step) % depth
                    elif kind == "flip":
                        at[1] = z ^ step
                    elif (kind == "first") == (core == 0):
                        at[3] = (x + step) % side
                    else:
                        at[2] = (y + step) % side
                    pairs.append((at[0] * shards + (at[1] * side + at[2]) * side + at[3], to))
    with jax.named_scope(f"{kind}_exchange"):
        return lax.ppermute(value, AXES, pairs)


def place(shards, half):
    _, side = grid_of(shards)
    at = lax.axis_index("fsdp")
    z, y, x = at // (side * side), (at // side) % side, at % side
    first = jnp.where(half == 0, x, y)
    second = jnp.where(half == 0, y, x)
    return jnp.stack([half, z, first, second, lax.axis_index("dp")]).astype(jnp.int32)


def after(value, *earlier):
    return lax.optimization_barrier((value, *earlier))[0]


def spread_lines(vectors, shards):
    unit = jnp.concatenate(vectors)
    unit = jnp.pad(unit, (0, -unit.shape[0] % 1024)).reshape(1, -1, LANES)
    at = lax.broadcasted_iota(jnp.int32, (shards, 1, 1), 0) == lax.axis_index("fsdp")
    return jnp.where(at, unit, jnp.zeros_like(unit))


def join_lines(spread, count, rows):
    shards = spread.shape[0]
    whole = spread.reshape(shards, -1)[:, : count * rows].reshape(shards, count, rows)
    whole = whole.transpose(1, 0, 2).reshape(count, -1)
    return jnp.pad(whole.astype(F32), ((0, 16 - count), (0, 0)))


def from_z(unit, shards, steps):
    return [arrive(unit, shards, "z", s) for s in steps]


def gather_first(got, shards):
    _, side = grid_of(shards)
    return jnp.stack([got] + [arrive(got, shards, "first", s) for s in range(1, side)])


def gather_second(got, shards):
    _, side = grid_of(shards)
    return [got] + [arrive(got, shards, "second", s) for s in range(1, side)]


def gather_core(own, shards):
    return [arrive(part, shards, "core", 1) for part in own]


def row_of(where, depth, side, rel_second, rel_first, rel_z):
    z = lax.rem(where[1] + rel_z, depth)
    first = lax.rem(where[2] + rel_first, side)
    second = lax.rem(where[3] + rel_second, side)
    y = jnp.where(where[0] == 0, second, first)
    x = jnp.where(where[0] == 0, first, second)
    return (z * side + y) * side + x


def unroll_rows(parts, where, half, depth, side):
    rel = jnp.stack(parts)
    rel = jnp.roll(rel, where[3], axis=0)
    rel = jnp.roll(rel, where[2], axis=1)
    rel = jnp.roll(rel, where[1], axis=2)
    straight = jnp.where(half == 0, rel.transpose(2, 0, 1, 3, 4), rel.transpose(2, 1, 0, 3, 4))
    return straight.reshape(-1, rel.shape[-1])


def assemble(own, other, shards, cuts):
    depth, side = grid_of(shards)
    core = lax.axis_index("dp")
    here, there = place(shards, core), place(shards, 1 - core)
    mine = unroll_rows(own, here, core, depth, side)
    theirs = unroll_rows(other, there, 1 - core, depth, side)
    wholes = []
    for start, width, split in cuts:
        left, right = mine[:, start : start + width], theirs[:, start : start + width]
        if split:
            swapped = jnp.concatenate([right, left], axis=1)
            left = jnp.where(core == 0, jnp.concatenate([left, right], axis=1), swapped)
        wholes.append(left)
    return wholes


def tiles_of(widths):
    tiles, start = [], 0
    for k, width in enumerate(widths):
        at = 0
        while at < width:
            step = min(768, width - at)
            tiles.append((k, at, start + at, step))
            at += step
        start += width
    return tiles


def put_pieces(acc, sums, group, columns, where, depth, side, rows, deep, ahead):
    step = columns.stop - columns.start
    for second in range(side):
        for first in range(side):
            for z in range(deep):
                from_row = row_of(where, depth, side, second, first, z)
                if deep == 1:
                    from_row = lax.rem(from_row, side * side)
                piece = acc[pl.ds(pl.multiple_of(from_row * rows, 16), rows), :step]
                sums[group, second, first, ahead + z, :, columns] = piece.astype(BF16)


def grad_kernel(depth, side, rows, deep, widths, there, here, *refs):
    count = len(widths)
    layers = depth // deep
    tiles = tiles_of(widths)
    pairs, refs = refs[: 2 * count], refs[2 * count :]
    away, outs, refs = refs[0], refs[1 : 1 + side], refs[1 + side :]
    left, right, acc, sums, left_sems, right_sems, out_sems = refs
    chunk = left.shape[1]

    def left_copy(k, layer):
        row = pl.multiple_of(lax.rem(there[1] + layer, layers) * chunk, 16) if layers > 1 else 0
        return pltpu.make_async_copy(
            pairs[2 * k].at[pl.ds(row, chunk)], left.at[k * layers + layer], left_sems.at[k * layers + layer]
        )

    def right_copy(group, t):
        k, at, start, step = tiles[t]
        half = (there if group == 0 else here)[0]
        column = pl.multiple_of(half * widths[k] + at, LANES)
        return pltpu.make_async_copy(
            pairs[2 * k + 1].at[:, pl.ds(column, step)],
            right.at[group, :, pl.ds(start, step)],
            right_sems.at[group, t],
        )

    def out_copies(group):
        if group == 0:
            return [pltpu.make_async_copy(sums.at[0], away, out_sems.at[0])]
        return [pltpu.make_async_copy(sums.at[1, s], outs[s], out_sems.at[1 + s]) for s in range(side)]

    for layer in range(layers):
        for k in range(count):
            left_copy(k, layer).start()
            if layer == 0:
                for t in range(len(tiles)):
                    if tiles[t][0] == k:
                        right_copy(0, t).start()
    for t in range(len(tiles)):
        right_copy(1, t).start()
    for group in range(2):
        where = there if group == 0 else here
        for layer in range(layers):
            for t, (k, at, start, step) in enumerate(tiles):
                if group == 0 and at == 0:
                    left_copy(k, layer).wait()
                if layer == 0:
                    right_copy(group, t).wait()
                columns = slice(start, start + step)
                acc[:, :step] = dot(left[k * layers + layer], right[group, :, columns])
                put_pieces(acc, sums, group, columns, where, depth, side, rows, deep, layer * deep)
        for copy in out_copies(group):
            copy.start()
    for group in range(2):
        for copy in out_copies(group):
            copy.wait()


def layer_grad_kernel(depth, side, rows, there, here, lhs, rhs, *refs):
    away, outs, refs = refs[0], refs[1 : 1 + side], refs[1 + side :]
    left, right, acc, sums, left_sems, right_sem, out_sems = refs
    chunk, width = left.shape[1], right.shape[1] // 2

    def left_copy(z):
        row = pl.multiple_of(lax.rem(there[1] + z, depth) * chunk, 16)
        return pltpu.make_async_copy(lhs.at[pl.ds(row, chunk)], left.at[z], left_sems.at[z])

    def out_copies(z):
        copies = [pltpu.make_async_copy(sums.at[0, :, :, z], away.at[:, :, z], out_sems.at[z, 0])]
        for s in range(side):
            copies.append(pltpu.make_async_copy(sums.at[1, s, :, z], outs[s].at[:, z], out_sems.at[z, 1 + s]))
        return copies

    right_copy = pltpu.make_async_copy(rhs, right, right_sem)
    left_copy(0).start()
    right_copy.start()
    left_copy(1).start()
    right_copy.wait()
    for z in range(depth):
        left_copy(z).wait()
        if z + 2 < depth:
            left_copy(z + 2).start()
        acc[...] = dot(left[z], right[...])
        for group, where in ((0, there), (1, here)):
            column = pl.multiple_of(where[0] * width, LANES)
            for second in range(side):
                for first in range(side):
                    from_row = lax.rem(row_of(where, depth, side, second, first, z), side * side)
                    piece = acc[pl.ds(pl.multiple_of(from_row * rows, 16), rows), pl.ds(column, width)]
                    sums[group, second, first, z] = piece.astype(BF16)
        for copy in out_copies(z):
            copy.start()
    for z in range(depth):
        for copy in out_copies(z):
            copy.wait()


def rel_grad(pairs, shards, there, here):
    depth, side = grid_of(shards)
    features, length = pairs[0][0].shape
    widths = [rhs.shape[1] // 2 for _, rhs in pairs]
    width = sum(widths)
    rows = features // shards
    core = lax.axis_index("dp")
    if rows % 16 != 0:
        both = []
        for half, where in ((1 - core, there), (core, here)):
            wholes = [
                lax.dot_general(
                    lhs,
                    lax.dynamic_slice_in_dim(rhs, half * (rhs.shape[1] // 2), rhs.shape[1] // 2, axis=1),
                    (((1,), (0,)), ((), ())),
                    preferred_element_type=F32,
                )
                for lhs, rhs in pairs
            ]
            whole = jnp.concatenate(wholes, axis=1).reshape(depth, side, side, rows, width)
            rel = jnp.where(half == 0, whole.transpose(1, 2, 0, 3, 4), whole.transpose(2, 1, 0, 3, 4))
            rel = jnp.roll(rel, -where[3], axis=0)
            rel = jnp.roll(rel, -where[2], axis=1)
            both.append(jnp.roll(rel, -where[1], axis=2).astype(BF16))
        return both[0], [both[1][s] for s in range(side)]
    deep = depth if features <= 1024 else 1
    chunk = features if deep > 1 else features // depth
    layers = depth // deep
    count, pieces = len(pairs), len(tiles_of(widths))
    if layers > 1 and count == 1 and 2 * width <= 768:
        out = pl.pallas_call(
            functools.partial(layer_grad_kernel, depth, side, rows),
            in_specs=[SMEM, SMEM, HBM, HBM],
            out_specs=[HBM] * (1 + side),
            out_shape=[jax.ShapeDtypeStruct((side, side, depth, rows, width), BF16)]
            + [jax.ShapeDtypeStruct((side, depth, rows, width), BF16)] * side,
            scratch_shapes=[
                pltpu.VMEM((depth, chunk, length), BF16),
                pltpu.VMEM((length, 2 * width), BF16),
                pltpu.VMEM((chunk, 2 * width), F32),
                pltpu.VMEM((2, side, side, depth, rows, width), BF16),
                pltpu.SemaphoreType.DMA((depth,)),
                pltpu.SemaphoreType.DMA,
                pltpu.SemaphoreType.DMA((depth, 1 + side)),
            ],
            compiler_params=pltpu.CompilerParams(vmem_limit_bytes=VMEM_MOST * MEBI),
            cost_estimate=pl.CostEstimate(flops=4 * length * features * width, bytes_accessed=20 * MEBI, transcendentals=0),
            name="layer_grad",
        )(there, here, *pairs[0])
        return out[0], out[1:]
    out = pl.pallas_call(
        functools.partial(grad_kernel, depth, side, rows, deep, widths),
        in_specs=[SMEM, SMEM] + [HBM] * (2 * count),
        out_specs=[HBM] * (1 + side),
        out_shape=[jax.ShapeDtypeStruct((side, side, depth, rows, width), BF16)]
        + [jax.ShapeDtypeStruct((side, depth, rows, width), BF16)] * side,
        scratch_shapes=[
            pltpu.VMEM((count * layers, chunk, length), BF16),
            pltpu.VMEM((2, length, width), BF16),
            pltpu.VMEM((chunk, min(768, max(widths))), F32),
            pltpu.VMEM((2, side, side, depth, rows, width), BF16),
            pltpu.SemaphoreType.DMA((count * layers,)),
            pltpu.SemaphoreType.DMA((2, pieces)),
            pltpu.SemaphoreType.DMA((1 + side,)),
        ],
        compiler_params=pltpu.CompilerParams(vmem_limit_bytes=VMEM_MOST * MEBI),
        cost_estimate=pl.CostEstimate(flops=4 * length * features * width, bytes_accessed=20 * MEBI, transcendentals=0),
        name="grad",
    )(there, here, *(operand for pair in pairs for operand in pair))
    return out[0], out[1:]


def sum_of(*values):
    total = values[0].astype(F32)
    for value in values[1:]:
        total = total + value.astype(F32)
    return total.astype(BF16)


def second_sends(own, got):
    return [sum_of(own[s], got[s]) for s in range(1, got.shape[0])]


def second_parts(sends, shards):
    _, side = grid_of(shards)
    return [arrive(send, shards, "second", side - 1 - k) for k, send in enumerate(sends)]


def second_sums(own, got, parts):
    return [sum_of(own[0][f], got[0, f], *(part[f] for part in parts)) for f in range(got.shape[1])]


def first_parts(sums, shards):
    _, side = grid_of(shards)
    return [arrive(sums[f], shards, "first", side - f) for f in range(1, side)]


def first_sums(sums, parts):
    return [sum_of(sums[0][z], *(part[z] for part in parts)) for z in range(sums[0].shape[0])]


def z_parts(sums, shards):
    depth, _ = grid_of(shards)
    return [sums[0]] + [arrive(sums[z], shards, "z", depth - z) for z in range(1, depth)]


def line_parts(lines, shards, kind):
    _, side = grid_of(shards)
    if kind in ("flip_1", "flip_2"):
        return [lines, arrive(lines, shards, "flip", int(kind[-1]))]
    count = 2 if kind == "core" else side
    return [lines] + [arrive(lines, shards, kind, step) for step in range(1, count)]


def exchange_lines(lines, shards, kind):
    return sum_of(*line_parts(lines, shards, kind))


def both_halves(mine, shards, widths):
    theirs = arrive(mine, shards, "core", 1)
    core = lax.axis_index("dp")
    left = jnp.where(core == 0, mine, theirs)
    right = jnp.where(core == 0, theirs, mine)
    wholes, start = [], 0
    for width in widths:
        columns = slice(start, start + width)
        wholes.append(jnp.concatenate([left[:, columns], right[:, columns]], axis=1).astype(F32))
        start += width
    return wholes


GAIN_ONE, SHIFT_ONE, BIAS_QUERY, BIAS_VALUE, BIAS_OUT, GAIN_TWO, SHIFT_TWO, BIAS_DOWN = range(8)
SCALE = HEAD_DIM ** (-0.5)


def weight_copies(plan, here, there, parts, outs, sems, first=0):
    groups = [[] for _ in outs]
    if plan is None:
        for k, (part, out) in enumerate(zip(parts, outs)):
            groups[k].append(pltpu.make_async_copy(part, out, sems.at[first + k]))
        return groups
    depth, side, rows, cuts = plan
    used = first
    for group in range(2):
        where = here if group == 0 else there
        for second in range(side):
            for ahead in range(side):
                for z in range(depth):
                    at = pl.multiple_of(row_of(where, depth, side, second, ahead, z) * rows, 16)
                    source = parts[group * side + second].at[ahead, z]
                    for k, ((start, width, split), out) in enumerate(zip(cuts, outs)):
                        if group == 1 and not split:
                            continue
                        column = pl.multiple_of(where[0] * width, LANES) if split else 0
                        groups[k].append(
                            pltpu.make_async_copy(
                                source.at[:, pl.ds(start, width)],
                                out.at[pl.ds(at, rows), pl.ds(column, width)],
                                sems.at[used],
                            )
                        )
                        used += 1
    return groups


def bring(groups):
    for group in groups:
        for copy in group:
            copy.start()
    for group in groups:
        for copy in group:
            copy.wait()


def copies_of(plan, shards, cuts):
    if plan is None:
        return len(cuts)
    return shards * sum(2 if split else 1 for _, _, split in cuts)


def standardize(values):
    average = jnp.mean(values, axis=-1, keepdims=True)
    centred = values - average
    spread = jnp.mean(centred * centred, axis=-1, keepdims=True)
    inverse = lax.rsqrt(spread + EPSILON)
    return centred * inverse, inverse


def dot(a, b, dims=((1,), (0,))):
    return lax.dot_general(a, b, (dims, ((), ())), preferred_element_type=F32)


NT = ((1,), (1,))
TN = ((0,), (0,))


def project_kernel(plan, count, here, there, tokens, lines, *refs):
    parts = refs[:count]
    normed_ref, qkv_ref = refs[count : count + 2]
    weight, sems = refs[count + 2 :]
    width = tokens.shape[1]

    @pl.when(pl.program_id(0) == 0)
    def _():
        bring(weight_copies(plan, here, there, parts, (weight,), sems))

    standard, _ = standardize(tokens[...].astype(F32))
    normed = (standard * lines[pl.ds(GAIN_ONE, 1), :] + lines[pl.ds(SHIFT_ONE, 1), :]).astype(BF16)
    normed_ref[...] = normed.T
    bias = (lines[pl.ds(BIAS_QUERY, 1), :], None, lines[pl.ds(BIAS_VALUE, 1), :])
    for part in range(3):
        columns = slice(part * width, (part + 1) * width)
        project = dot(normed, weight[:, columns])
        if bias[part] is not None:
            project = project + bias[part]
        qkv_ref[:, columns] = project.astype(BF16)


def attend_kernel(frames, qkv_ref, mixed_ref, turned_ref, power_ref, inverse_ref):
    tube = pl.program_id(0)
    length, width = mixed_ref.shape
    mask = jnp.where(lax.broadcasted_iota(jnp.int32, (1, length), 1) < frames[tube] * PATCH, 0.0, -1e30)
    lower = lax.broadcasted_iota(jnp.int32, (length, LANES), 1) < HEAD_DIM
    ones = jnp.ones((length, LANES), BF16)
    for pair in range(width // LANES):
        query = qkv_ref[:, pair * LANES : (pair + 1) * LANES] * jnp.asarray(SCALE, BF16)
        keys = qkv_ref[:, width + pair * LANES : width + (pair + 1) * LANES]
        values = qkv_ref[:, 2 * width + pair * LANES : 2 * width + (pair + 1) * LANES]
        values = jnp.concatenate([values, ones], axis=1)
        both = []
        for k in range(2):
            own = jnp.where(lower if k == 0 else ~lower, query, jnp.zeros_like(query))
            scores = dot(own, keys, NT) + mask
            power = jnp.exp(scores - jnp.max(scores, axis=-1, keepdims=True)).astype(BF16)
            power_ref[0, 2 * pair + k] = power
            both.append(dot(power, values))
        inverse = 1.0 / jnp.where(lower, both[0][:, LANES:], both[1][:, LANES:])
        inverse_ref[:, pair * LANES : (pair + 1) * LANES] = inverse.astype(BF16)
        mixed = jnp.where(lower, both[0][:, :LANES], both[1][:, :LANES]) * inverse
        mixed = mixed.astype(BF16)
        mixed_ref[:, pair * LANES : (pair + 1) * LANES] = mixed
        turned_ref[pair * LANES : (pair + 1) * LANES, :] = mixed.T


def feed_kernel(plan, count, here, there, frames, tokens, mixed, cotangent, lines, up_bias, *refs):
    parts = refs[:count]
    resid_ref, normed_ref, active_ref, turned_ref, slope_ref, upstream_ref = refs[count : count + 6]
    out_weight, up_weight, sems = refs[count + 6 :]
    tube = pl.program_id(0)
    first, last = weight_copies(plan, here, there, parts, (out_weight, up_weight), sems)

    @pl.when(tube == 0)
    def _():
        for copy in first + last:
            copy.start()
        for copy in first:
            copy.wait()

    length = tokens.shape[0]
    row_ok = lax.broadcasted_iota(jnp.int32, (length, 1), 0) < frames[tube] * PATCH
    upstream_ref[...] = jnp.where(row_ok, cotangent[...], jnp.zeros_like(cotangent))
    attended = dot(mixed[...], out_weight[...]) + lines[pl.ds(BIAS_OUT, 1), :]
    resid = tokens[...].astype(F32) + attended
    resid_ref[...] = resid.astype(BF16)
    standard, _ = standardize(resid)
    normed = (standard * lines[pl.ds(GAIN_TWO, 1), :] + lines[pl.ds(SHIFT_TWO, 1), :]).astype(BF16)
    normed_ref[...] = normed.T

    @pl.when(tube == 0)
    def _():
        for copy in last:
            copy.wait()

    units = up_weight.shape[1]
    step = 512
    for at in range(0, units, step):
        hidden = dot(normed, up_weight[:, at : at + step]) + up_bias[:, at : at + step]
        cumulative = 0.5 + 0.5 * lax.erf(hidden * SQRT_HALF)
        density = jnp.exp2(hidden * hidden * (-0.5 * LOG2_E) + LOG2_DENSITY)
        active = (hidden * cumulative).astype(BF16)
        active_ref[:, at : at + step] = active
        turned_ref[at : at + step, :] = active.T
        slope_ref[:, at : at + step] = (cumulative + hidden * density).astype(BF16)


def norm_back(grad, standard, inverse, gain):
    scaled = grad * gain
    first = jnp.mean(scaled, axis=-1, keepdims=True)
    second = jnp.mean(scaled * standard, axis=-1, keepdims=True)
    return inverse * (scaled - first - standard * second)


def column_sum(values):
    return jnp.sum(values, axis=0, keepdims=True)


SUM_GAIN_TWO, SUM_SHIFT_TWO, SUM_BIAS_OUT, SUM_BIAS_DOWN = range(4)


def feed_back_kernel(plans, counts, depth, side, rows, direct, here, there, upstream, slope, resid, inverse_sums, lines, *refs):
    mixed_hbm, normed_hbm, refs = refs[0], refs[1], refs[2:]
    ff_parts, refs = refs[: counts[0]], refs[counts[0] :]
    down_parts, refs = refs[: counts[1]], refs[counts[1] :]
    attended_ref, scaled_ref, sums_ref, up_sum_ref = refs[:4]
    refs = refs[4:]
    if direct:
        away, outs, refs = refs[0], refs[1 : 1 + side], refs[1 + side :]
    else:
        hidden_hbm, refs = refs[0], refs[1:]
    out_weight, up_weight, down_weight, hidden_all, attended_all, sems, more_sems = refs[:7]
    tube, last = pl.program_id(0), pl.num_programs(0) - 1
    length, width = upstream.shape
    units = up_weight.shape[1]
    (down_copies,) = weight_copies(plans[1], here, there, down_parts, (down_weight,), sems)
    ff_copies = weight_copies(plans[0], here, there, ff_parts, (out_weight, up_weight), sems, len(down_copies))
    if direct:
        turned, acc, sums = refs[7:]
        left_copies = [
            pltpu.make_async_copy(mixed_hbm, turned.at[0], more_sems.at[0]),
            pltpu.make_async_copy(normed_hbm, turned.at[1], more_sems.at[1]),
        ]

    @pl.when(tube == 0)
    def _():
        for copy in down_copies:
            copy.start()
        for group in reversed(ff_copies):
            for copy in group:
                copy.start()
        if direct:
            for copy in left_copies:
                copy.start()
        sums_ref[...] = jnp.zeros_like(sums_ref)
        up_sum_ref[...] = jnp.zeros_like(up_sum_ref)
        for copy in down_copies:
            copy.wait()

    here_rows = pl.ds(pl.multiple_of(tube * length, 16), length)
    low = upstream[...]
    standard, inverse = standardize(resid[...].astype(F32))
    step = 768
    for at in range(0, units, step):
        grad = dot(low, down_weight[at : at + step, :], NT) * slope[:, at : at + step].astype(F32)
        hidden_all[here_rows, at : at + step] = grad.astype(BF16)
        up_sum_ref[:, at : at + step] += column_sum(grad)

    @pl.when(tube == 0)
    def _():
        for group in ff_copies:
            for copy in group:
                copy.wait()

    normed_grad = dot(hidden_all[here_rows, :], up_weight[...], NT)
    above = low.astype(F32)
    resid_grad = above + norm_back(normed_grad, standard, inverse, lines[pl.ds(GAIN_TWO, 1), :])
    attended_grad = resid_grad.astype(BF16)
    attended_ref[...] = attended_grad
    attended_all[here_rows, :] = attended_grad
    scaled_ref[...] = (dot(attended_grad, out_weight[...], NT) * inverse_sums[...].astype(F32)).astype(BF16)
    sums_ref[pl.ds(SUM_GAIN_TWO, 1), :] += column_sum(normed_grad * standard)
    sums_ref[pl.ds(SUM_SHIFT_TWO, 1), :] += column_sum(normed_grad)
    sums_ref[pl.ds(SUM_BIAS_OUT, 1), :] += column_sum(attended_grad.astype(F32))
    sums_ref[pl.ds(SUM_BIAS_DOWN, 1), :] += column_sum(above)

    if not direct:

        @pl.when(tube == last)
        def _():
            copy = pltpu.make_async_copy(hidden_all, hidden_hbm, more_sems.at[0])
            copy.start()
            copy.wait()

        return

    @pl.when(tube == 1)
    def _():
        for k in range(2):
            left_copies[k].wait()

    @pl.when(tube == last)
    def _():
        waits = []
        for group in range(2):
            where = there if group == 0 else here
            for k, at, start, size in tiles_of((width // 2, units // 2)):
                right = attended_all if k == 0 else hidden_all
                column = pl.multiple_of(where[0] * (right.shape[1] // 2) + at, LANES)
                acc[:, :size] = dot(turned[k], right[:, pl.ds(column, size)])
                put_pieces(acc, sums, group, slice(start, start + size), where, depth, side, rows, depth, 0)
            if group == 0:
                waits.append(pltpu.make_async_copy(sums.at[0], away, more_sems.at[2]))
                waits[-1].start()
            else:
                for s in range(side):
                    waits.append(pltpu.make_async_copy(sums.at[1, s], outs[s], more_sems.at[3 + s]))
                    waits[-1].start()
        for copy in waits:
            copy.wait()


def attend_back_kernel(qkv, power_ref, mixed, scaled_grad, grad_ref, sums_ref):
    tube = pl.program_id(0)

    @pl.when(tube == 0)
    def _():
        sums_ref[...] = jnp.zeros_like(sums_ref)

    length, width = mixed.shape
    lower = lax.broadcasted_iota(jnp.int32, (length, LANES), 1) < HEAD_DIM
    for pair in range(width // LANES):
        lanes = slice(pair * LANES, (pair + 1) * LANES)
        query = qkv[:, lanes]
        keys = qkv[:, width + pair * LANES : width + (pair + 1) * LANES]
        values = qkv[:, 2 * width + pair * LANES : 2 * width + (pair + 1) * LANES]
        above = scaled_grad[:, lanes]
        product = above.astype(F32) * mixed[:, lanes].astype(F32)
        query_grad, keys_grad, values_grad = [], [], []
        for k in range(2):
            mine = lower if k == 0 else ~lower
            own = jnp.where(mine, above, jnp.zeros_like(above))
            power = power_ref[0, 2 * pair + k]
            inner = jnp.sum(jnp.where(mine, product, 0.0), axis=-1, keepdims=True)
            scores_grad = (power.astype(F32) * (dot(own, values, NT) - inner)).astype(BF16)
            values_grad.append(dot(power, above, TN))
            query_grad.append(dot(scores_grad, keys))
            keys_grad.append(dot(scores_grad, query, TN))
        for part, (pieces, scale) in enumerate(((query_grad, SCALE), (keys_grad, SCALE), (values_grad, None))):
            piece = jnp.where(lower, pieces[0], pieces[1])
            if scale is not None:
                piece = piece * scale
            grad_ref[:, part * width + pair * LANES : part * width + (pair + 1) * LANES] = piece.astype(BF16)
            if part != 1:
                sums_ref[pl.ds(part // 2, 1), lanes] += column_sum(piece)


def first_back_kernel(plan, count, here, there, tokens, project_grad, attended_grad, lines, *refs):
    parts = refs[:count]
    tokens_ref, sums_ref = refs[count : count + 2]
    weight, sems = refs[count + 2 :]
    tube = pl.program_id(0)

    @pl.when(tube == 0)
    def _():
        bring(weight_copies(plan, here, there, parts, (weight,), sems))
        sums_ref[...] = jnp.zeros_like(sums_ref)

    grad = dot(project_grad[...], weight[...], NT)
    standard, inverse = standardize(tokens[...].astype(F32))
    inputs_grad = norm_back(grad, standard, inverse, lines[pl.ds(GAIN_ONE, 1), :])
    tokens_ref[...] = (attended_grad[...].astype(F32) + inputs_grad).astype(BF16)
    sums_ref[pl.ds(0, 1), :] += column_sum(grad * standard)
    sums_ref[pl.ds(1, 1), :] += column_sum(grad)


def block_out_kernel(plan, count, here, there, active, resid, lines, *refs):
    parts = refs[:count]
    out_ref = refs[count]
    weight, sems = refs[count + 1 :]

    @pl.when(pl.program_id(0) == 0)
    def _():
        bring(weight_copies(plan, here, there, parts, (weight,), sems))

    branch = dot(active[...], weight[...]) + lines[pl.ds(BIAS_DOWN, 1), :]
    out_ref[...] = (resid[...].astype(F32) + branch).astype(BF16)


def rows_of(width, length):
    return pl.BlockSpec((length, width), lambda t: (t, 0))


def fixed(*shape):
    return pl.BlockSpec(shape, lambda t: (0,) * len(shape))


def shape_of(*shape, kind=BF16):
    return jax.ShapeDtypeStruct(shape, kind)


def call(kernel, name, grid, in_specs, outs, scratch, flops, *args):
    return pl.pallas_call(
        kernel,
        grid=(grid,),
        in_specs=in_specs,
        out_specs=[spec for spec, _ in outs],
        out_shape=[shape for _, shape in outs],
        scratch_shapes=scratch,
        compiler_params=pltpu.CompilerParams(vmem_limit_bytes=VMEM_MOST * MEBI),
        cost_estimate=pl.CostEstimate(flops=flops, bytes_accessed=16 * MEBI, transcendentals=0),
        name=name,
    )(*args)


def local(
    tokens,
    clip_frames,
    tube_clip,
    first_gain,
    first_shift,
    qkv_weight,
    query_bias,
    value_bias,
    out_weight,
    out_bias,
    second_gain,
    second_shift,
    up_weight,
    up_bias,
    down_weight,
    down_bias,
    cotangent,
):
    shards = lax.axis_size("fsdp")
    depth, side = grid_of(shards)
    core = lax.axis_index("dp")
    total, width = tokens.shape
    tubes = tube_clip.shape[0]
    length = total // tubes
    clip_count = clip_frames.shape[0]

    def half(matrix):
        columns = matrix.shape[1] // 2
        return lax.dynamic_slice_in_dim(matrix, core * columns, columns, axis=1)

    wide, full, ff = qkv_weight.shape[1] // 2, out_weight.shape[1] // 2, up_weight.shape[1] // 2
    units = 2 * ff
    rows = first_gain.shape[0]
    vectors = [first_gain, first_shift, query_bias, value_bias, out_bias, second_gain, second_shift, down_bias]
    vectors += [up_bias[k * rows : (k + 1) * rows] for k in range(4)]
    pack_one = half(qkv_weight)
    pack_two = jnp.concatenate([half(out_weight), half(up_weight)], axis=1)
    cuts = (
        ((0, wide, True),),
        ((0, full, True), (full, ff, True)),
        ((0, full, True),),
    )
    plans, counts = [], []
    for pack, cut in zip((pack_one, pack_two, down_weight), cuts):
        direct = pack.shape[0] % 16 == 0
        plans.append((depth, side, pack.shape[0], cut) if direct else None)
        counts.append(2 * side if direct else len(cut))

    def finish(k, own, other):
        return [*own, *other] if plans[k] is not None else assemble(own, other, shards, cuts[k])

    number = [copies_of(plan, shards, cut) for plan, cut in zip(plans, cuts)]
    sem = pltpu.SemaphoreType.DMA
    big = 2 * total * width * width
    narrow, wide_rows, deep_rows = rows_of(width, length), rows_of(3 * width, length), rows_of(units, length)
    upright = pl.BlockSpec((width, length), lambda t: (0, t))
    tall = total // 2
    tall_narrow, tall_wide, tall_deep = rows_of(width, tall), rows_of(3 * width, tall), rows_of(units, tall)
    probs_spec = pl.BlockSpec((1, HEADS, length, length), lambda t: (t, 0, 0, 0))

    near, far = (1, depth - 1), range(2, depth - 1)

    def stack_z(unit, near_units, far_units):
        return jnp.stack([unit, near_units[0], *far_units, near_units[1]])

    spread = spread_lines(vectors, shards)
    z_one = stack_z(pack_one, from_z(pack_one, shards, near), from_z(pack_one, shards, far))
    z_one, spread, pack_two = lax.optimization_barrier((z_one, spread, pack_two))
    first_one = gather_first(z_one, shards)
    near_two = from_z(pack_two, shards, near)
    spread = exchange_lines(spread, shards, "first")
    first_one, near_two, spread, pack_two, tube_clip, down_weight = lax.optimization_barrier(
        (first_one, near_two, spread, pack_two, tube_clip, down_weight)
    )
    second_one = gather_second(first_one, shards)
    early_one = arrive(first_one, shards, "core", 1)
    z_two = stack_z(pack_two, near_two, from_z(pack_two, shards, far))
    spread = exchange_lines(spread, shards, "second")
    pack_three = half(down_weight)
    here, there = place(shards, core), place(shards, 1 - core)
    matches = tube_clip[:, None] == jnp.arange(clip_count, dtype=jnp.int32)[None, :]
    frames = jnp.sum(jnp.where(matches, clip_frames[None, :], 0), axis=1)
    second_one, early_one, z_two, spread, pack_three, here, there, frames = lax.optimization_barrier(
        (second_one, early_one, z_two, spread, pack_three, here, there, frames)
    )
    core_one = [early_one] + gather_core(second_one[1:], shards)
    first_two = gather_first(z_two, shards)
    for kind in ("flip_1", "flip_2"):
        spread = exchange_lines(spread, shards, kind)
    lines = join_lines(spread, len(vectors), rows)
    up_row = lines[8:12].reshape(4, shards, rows).transpose(1, 0, 2).reshape(1, units)
    core_one, first_two, pack_three, tokens, lines, up_row = lax.optimization_barrier(
        (core_one, first_two, pack_three, tokens, lines, up_row)
    )
    parts_one = finish(0, second_one, core_one)
    second_two = gather_second(first_two, shards)
    early_two = arrive(first_two, shards, "core", 1)
    z_three = stack_z(pack_three, from_z(pack_three, shards, near), from_z(pack_three, shards, far))

    normed_one, qkv = call(
        functools.partial(project_kernel, plans[0], counts[0]),
        "project",
        tubes,
        [SMEM, SMEM, narrow, fixed(16, width)] + [HBM] * counts[0],
        [(upright, shape_of(width, total)), (wide_rows, shape_of(total, 3 * width))],
        [pltpu.VMEM((width, 3 * width), BF16), sem((number[0],))],
        3 * big,
        here, there, tokens, lines, *parts_one,
    )
    z_three, qkv, early_two = lax.optimization_barrier((z_three, qkv, early_two))

    mixed, mixed_turned, power, inverse = call(
        attend_kernel,
        "attend",
        tubes,
        [SMEM, wide_rows],
        [
            (narrow, shape_of(total, width)),
            (upright, shape_of(width, total)),
            (probs_spec, shape_of(tubes, HEADS, length, length)),
            (narrow, shape_of(total, width)),
        ],
        [],
        4 * big,
        frames, qkv,
    )
    second_two, mixed, z_three = lax.optimization_barrier((second_two, mixed, z_three))
    core_two = [early_two] + gather_core(second_two[1:], shards)
    core_two, z_three, mixed = lax.optimization_barrier((core_two, z_three, mixed))
    parts_two = finish(1, second_two, core_two)
    first_three = gather_first(z_three, shards)

    resid, normed_two, active, active_turned, slope, upstream = call(
        functools.partial(feed_kernel, plans[1], counts[1]),
        "feed",
        tubes,
        [SMEM, SMEM, SMEM, narrow, narrow, narrow, fixed(16, width), fixed(1, units)] + [HBM] * counts[1],
        [
            (narrow, shape_of(total, width)),
            (upright, shape_of(width, total)),
            (deep_rows, shape_of(total, units)),
            (pl.BlockSpec((units, length), lambda t: (0, t)), shape_of(units, total)),
            (deep_rows, shape_of(total, units)),
            (narrow, shape_of(total, width)),
        ],
        [pltpu.VMEM((width, width), BF16), pltpu.VMEM((width, units), BF16), sem((number[1],))],
        8 * big,
        here, there, frames, tokens, mixed, cotangent, lines, up_row, *parts_two,
    )
    first_three, active_turned, upstream = lax.optimization_barrier((first_three, active_turned, upstream))
    second_three = gather_second(first_three, shards)
    early_three = arrive(first_three, shards, "core", 1)
    down_away, down_own = rel_grad([(active_turned, upstream)], shards, there, here)
    second_three, early_three, down_away, slope = lax.optimization_barrier((second_three, early_three, down_away, slope))
    core_three = [early_three] + gather_core(second_three[1:], shards)
    down_got = arrive(down_away, shards, "core", 1)
    core_three, down_got, slope = lax.optimization_barrier((core_three, down_got, slope))
    parts_three = finish(2, second_three, core_three)
    down_sends, slope = lax.optimization_barrier((second_sends(down_own, down_got), slope))
    down_parts = second_parts(down_sends, shards)

    direct = rows % 16 == 0
    ff_width = full + ff
    outs = [
        (narrow, shape_of(total, width)),
        (narrow, shape_of(total, width)),
        (fixed(8, width), shape_of(8, width, kind=F32)),
        (fixed(1, units), shape_of(1, units, kind=F32)),
    ]
    scratch = [
        pltpu.VMEM((width, width), BF16),
        pltpu.VMEM((width, units), BF16),
        pltpu.VMEM((units, width), BF16),
        pltpu.VMEM((total, units), BF16),
        pltpu.VMEM((total, width), BF16),
        sem((number[1] + number[2],)),
        sem((3 + side,)),
    ]
    if direct:
        outs.append((HBM, shape_of(side, side, depth, rows, ff_width)))
        outs += [(HBM, shape_of(side, depth, rows, ff_width))] * side
        scratch += [
            pltpu.VMEM((2, width, total), BF16),
            pltpu.VMEM((width, 768), F32),
            pltpu.VMEM((2, side, side, depth, rows, ff_width), BF16),
        ]
    else:
        outs.append((HBM, shape_of(total, units)))
    attended_grad, scaled_grad, sums_two, up_sum, *more = call(
        functools.partial(feed_back_kernel, plans[1:], counts[1:], depth, side, rows, direct),
        "feed_back",
        tubes,
        [SMEM, SMEM, narrow, deep_rows, narrow, narrow, fixed(16, width)] + [HBM] * (2 + counts[1] + counts[2]),
        outs,
        scratch,
        14 * big,
        here, there, upstream, slope, resid, inverse, lines, mixed_turned, normed_two, *parts_two, *parts_three,
    )
    if direct:
        ff_away, ff_own = more[0], more[1:]
    else:
        ff_away, ff_own = rel_grad([(mixed_turned, attended_grad), (normed_two, more[0])], shards, there, here)
    down_parts, ff_away, scaled_grad = lax.optimization_barrier((down_parts, ff_away, scaled_grad))
    ff_got = arrive(ff_away, shards, "core", 1)
    down_sums = second_sums(down_own, down_got, down_parts)
    down_parts = first_parts(down_sums, shards)
    ff_got, scaled_grad, down_sums = lax.optimization_barrier((ff_got, scaled_grad, down_sums))
    ff_sends, scaled_grad = lax.optimization_barrier((second_sends(ff_own, ff_got), scaled_grad))
    ff_parts = second_parts(ff_sends, shards)

    project_grad, sums_heads = call(
        attend_back_kernel,
        "attend_back",
        tubes,
        [wide_rows, probs_spec, narrow, narrow],
        [(wide_rows, shape_of(total, 3 * width)), (fixed(8, width), shape_of(8, width, kind=F32))],
        [],
        4 * big,
        qkv, power, mixed, scaled_grad,
    )
    project_grad, down_parts = lax.optimization_barrier((project_grad, down_parts))
    down_sums, project_grad = lax.optimization_barrier((first_sums(down_sums, down_parts), project_grad))
    down_parts = z_parts(down_sums, shards)
    qkv_away, qkv_own = rel_grad([(normed_one, project_grad)], shards, there, here)
    qkv_away, project_grad, ff_parts = lax.optimization_barrier((qkv_away, project_grad, ff_parts))
    qkv_got = arrive(qkv_away, shards, "core", 1)
    ff_sums, project_grad = lax.optimization_barrier((second_sums(ff_own, ff_got, ff_parts), project_grad))
    ff_parts = first_parts(ff_sums, shards)

    tokens_grad, sums_one = call(
        functools.partial(first_back_kernel, plans[0], counts[0]),
        "first_back",
        2,
        [SMEM, SMEM, tall_narrow, tall_wide, tall_narrow, fixed(16, width)] + [HBM] * counts[0],
        [(tall_narrow, shape_of(total, width)), (fixed(8, width), shape_of(8, width, kind=F32))],
        [pltpu.VMEM((width, 3 * width), BF16), sem((number[0],))],
        3 * big,
        here, there, tokens, project_grad, attended_grad, lines, *parts_one,
    )
    qkv_got, ff_parts, tokens_grad, sums_one, active, down_parts = lax.optimization_barrier(
        (qkv_got, ff_parts, tokens_grad, sums_one, active, down_parts)
    )
    sums = jnp.concatenate(
        [
            sums_one[:2],
            sums_heads[:2],
            sums_two[SUM_BIAS_OUT : SUM_BIAS_OUT + 1],
            sums_two[SUM_GAIN_TWO : SUM_GAIN_TWO + 1],
            sums_two[SUM_SHIFT_TWO : SUM_SHIFT_TWO + 1],
            sums_two[SUM_BIAS_DOWN : SUM_BIAS_DOWN + 1],
            up_sum.reshape(-1, width),
        ],
        axis=0,
    ).astype(BF16)
    ff_sums, qkv_sends, sums, active = lax.optimization_barrier(
        (first_sums(ff_sums, ff_parts), second_sends(qkv_own, qkv_got), sums, active)
    )
    ff_parts = z_parts(ff_sums, shards)
    qkv_parts = second_parts(qkv_sends, shards)
    sums = line_parts(sums, shards, "first")

    (block_out,) = call(
        functools.partial(block_out_kernel, plans[2], counts[2]),
        "block_out",
        tubes,
        [SMEM, SMEM, deep_rows, narrow, fixed(16, width)] + [HBM] * counts[2],
        [(narrow, shape_of(total, width))],
        [pltpu.VMEM((units, width), BF16), sem((number[2],))],
        4 * big,
        here, there, active, resid, lines, *parts_three,
    )
    block_out, ff_parts, qkv_parts, sums, down_parts = lax.optimization_barrier(
        (block_out, ff_parts, qkv_parts, sums, down_parts)
    )
    qkv_sums = second_sums(qkv_own, qkv_got, qkv_parts)
    qkv_parts = first_parts(qkv_sums, shards)
    sums = exchange_lines(sum_of(*sums), shards, "second")
    sums = line_parts(sums, shards, "flip_1")
    qkv_parts, sums, ff_parts, down_parts = lax.optimization_barrier((qkv_parts, sums, ff_parts, down_parts))
    qkv_sums, sums = lax.optimization_barrier((first_sums(qkv_sums, qkv_parts), sum_of(*sums)))
    qkv_parts = z_parts(qkv_sums, shards)
    (down_whole,) = both_halves(sum_of(*down_parts), shards, (full,))
    out_whole, up_whole = both_halves(sum_of(*ff_parts), shards, (full, ff))
    sums = exchange_lines(sums, shards, "flip_2")
    qkv_parts, sums, down_whole, out_whole, up_whole = lax.optimization_barrier(
        (qkv_parts, sums, down_whole, out_whole, up_whole)
    )
    sums = exchange_lines(sums, shards, "core")
    (qkv_whole,) = both_halves(sum_of(*qkv_parts), shards, (wide,))
    at = lax.axis_index("fsdp")
    sums_here = lax.dynamic_slice_in_dim(sums[:8], at * rows, rows, axis=1).astype(F32)
    up_here = lax.dynamic_slice_in_dim(sums[8:].reshape(-1), at * up_bias.shape[0], up_bias.shape[0]).astype(F32)
    return (
        block_out,
        tokens_grad,
        sums_here[0],
        sums_here[1],
        qkv_whole,
        sums_here[2],
        sums_here[3],
        out_whole,
        sums_here[4],
        sums_here[5],
        sums_here[6],
        up_whole,
        up_here,
        down_whole,
        sums_here[7],
    )


def solution(mesh):
    return jax.shard_map(
        local,
        mesh=mesh,
        in_specs=(
            P(("dp", "fsdp"), None),
            P(),
            P(("dp", "fsdp")),
            P("fsdp"),
            P("fsdp"),
            P("fsdp", None),
            P("fsdp"),
            P("fsdp"),
            P("fsdp", None),
            P("fsdp"),
            P("fsdp"),
            P("fsdp"),
            P("fsdp", None),
            P("fsdp"),
            P("fsdp", None),
            P("fsdp"),
            P(("dp", "fsdp"), None),
        ),
        out_specs=(
            P(("dp", "fsdp"), None),
            P(("dp", "fsdp"), None),
            P("fsdp"),
            P("fsdp"),
            P("fsdp", None),
            P("fsdp"),
            P("fsdp"),
            P("fsdp", None),
            P("fsdp"),
            P("fsdp"),
            P("fsdp"),
            P("fsdp", None),
            P("fsdp"),
            P("fsdp", None),
            P("fsdp"),
        ),
        check_vma=False,
    )
```

```python
import functools
import math

import jax
import jax.numpy as jnp
from jax import lax
from jax.experimental import pallas as pl
from jax.experimental.pallas import tpu as pltpu
from jax.sharding import PartitionSpec as P

HEADS = 12
HEAD_DIM = 64
PATCH = 16
EPSILON = 1e-05
SQRT_HALF = 0.7071067811865476
LOG2_E = 1.4426950408889634
LOG2_DENSITY = -1.3257480647361593
AXES = ("dp", "fsdp")
F32 = jnp.float32
BF16 = jnp.bfloat16
LANES = 128
MEBI = 1 << 20
VMEM_MOST = 53
SMEM = pl.BlockSpec(memory_space=pltpu.SMEM)
HBM = pl.BlockSpec(memory_space=pl.ANY)


def grid_of(shards):
    side = math.isqrt(shards // 4)
    assert 4 * side * side == shards
    return 4, side


def arrive(value, shards, kind, step):
    depth, side = grid_of(shards)
    pairs = []
    for core in range(2):
        for z in range(depth):
            for y in range(side):
                for x in range(side):
                    to = core * shards + (z * side + y) * side + x
                    at = [core, z, y, x]
                    if kind == "core":
                        at[0] = 1 - core
                    elif kind == "z":
                        at[1] = (z + step) % depth
                    elif kind == "flip":
                        at[1] = z ^ step
                    elif kind == "slant":
                        at[1] = 1 ^ z
                        if core == 0:
                            at[2] = (y + step) % side
                        else:
                            at[3] = (x + step) % side
                    elif (kind == "first") == (core == 0):
                        at[3] = (x + step) % side
                    else:
                        at[2] = (y + step) % side
                    pairs.append((at[0] * shards + (at[1] * side + at[2]) * side + at[3], to))
    with jax.named_scope(f"{kind}_exchange"):
        return lax.ppermute(value, AXES, pairs)


def place(shards, half):
    _, side = grid_of(shards)
    at = lax.axis_index("fsdp")
    z, y, x = at // (side * side), (at // side) % side, at % side
    first = jnp.where(half == 0, x, y)
    second = jnp.where(half == 0, y, x)
    return jnp.stack([half, z, first, second, lax.axis_index("dp")]).astype(jnp.int32)


def after(value, *earlier):
    return lax.optimization_barrier((value, *earlier))[0]


def spread_lines(vectors, shards):
    unit = jnp.concatenate(vectors)
    unit = jnp.pad(unit, (0, -unit.shape[0] % 1024)).reshape(1, -1, LANES)
    at = lax.broadcasted_iota(jnp.int32, (shards, 1, 1), 0) == lax.axis_index("fsdp")
    return jnp.where(at, unit, jnp.zeros_like(unit))


def join_lines(spread, count, rows):
    shards = spread.shape[0]
    whole = spread.reshape(shards, -1)[:, : count * rows].reshape(shards, count, rows)
    whole = whole.transpose(1, 0, 2).reshape(count, -1)
    return jnp.pad(whole.astype(F32), ((0, 16 - count), (0, 0)))


def from_z(unit, shards, steps):
    return [arrive(unit, shards, "z", s) for s in steps]


def gather_first(got, shards):
    _, side = grid_of(shards)
    return jnp.stack([got] + [arrive(got, shards, "first", s) for s in range(1, side)])


def gather_second(got, shards):
    _, side = grid_of(shards)
    return [got] + [arrive(got, shards, "second", s) for s in range(1, side)]


def gather_core(own, shards):
    return [arrive(part, shards, "core", 1) for part in own]


def row_of(where, depth, side, rel_second, rel_first, rel_z):
    z = lax.rem(where[1] + rel_z, depth)
    first = lax.rem(where[2] + rel_first, side)
    second = lax.rem(where[3] + rel_second, side)
    y = jnp.where(where[0] == 0, second, first)
    x = jnp.where(where[0] == 0, first, second)
    return (z * side + y) * side + x


def unroll_rows(parts, where, half, depth, side):
    rel = jnp.stack(parts)
    rel = jnp.roll(rel, where[3], axis=0)
    rel = jnp.roll(rel, where[2], axis=1)
    rel = jnp.roll(rel, where[1], axis=2)
    straight = jnp.where(half == 0, rel.transpose(2, 0, 1, 3, 4), rel.transpose(2, 1, 0, 3, 4))
    return straight.reshape(-1, rel.shape[-1])


def assemble(own, other, shards, cuts):
    depth, side = grid_of(shards)
    core = lax.axis_index("dp")
    here, there = place(shards, core), place(shards, 1 - core)
    mine = unroll_rows(own, here, core, depth, side)
    theirs = unroll_rows(other, there, 1 - core, depth, side)
    wholes = []
    for start, width, split in cuts:
        left, right = mine[:, start : start + width], theirs[:, start : start + width]
        if split:
            swapped = jnp.concatenate([right, left], axis=1)
            left = jnp.where(core == 0, jnp.concatenate([left, right], axis=1), swapped)
        wholes.append(left)
    return wholes


def tiles_of(widths):
    tiles, start = [], 0
    for k, width in enumerate(widths):
        at = 0
        while at < width:
            step = min(768, width - at)
            tiles.append((k, at, start + at, step))
            at += step
        start += width
    return tiles


def put_pieces(acc, sums, group, columns, where, depth, side, rows, deep, ahead):
    step = columns.stop - columns.start
    for second in range(side):
        for first in range(side):
            for z in range(deep):
                from_row = row_of(where, depth, side, second, first, z)
                if deep == 1:
                    from_row = lax.rem(from_row, side * side)
                piece = acc[pl.ds(pl.multiple_of(from_row * rows, 16), rows), :step]
                sums[group, second, first, ahead + z, :, columns] = piece.astype(BF16)


def grad_kernel(depth, side, rows, deep, widths, there, here, *refs):
    count = len(widths)
    layers = depth // deep
    tiles = tiles_of(widths)
    pairs, refs = refs[: 2 * count], refs[2 * count :]
    away, outs, refs = refs[0], refs[1 : 1 + side], refs[1 + side :]
    left, right, acc, sums, left_sems, right_sems, out_sems = refs
    chunk = left.shape[1]

    def left_copy(k, layer):
        row = pl.multiple_of(lax.rem(there[1] + layer, layers) * chunk, 16) if layers > 1 else 0
        return pltpu.make_async_copy(
            pairs[2 * k].at[pl.ds(row, chunk)], left.at[k * layers + layer], left_sems.at[k * layers + layer]
        )

    def right_copy(group, t):
        k, at, start, step = tiles[t]
        half = (there if group == 0 else here)[0]
        column = pl.multiple_of(half * widths[k] + at, LANES)
        return pltpu.make_async_copy(
            pairs[2 * k + 1].at[:, pl.ds(column, step)],
            right.at[group, :, pl.ds(start, step)],
            right_sems.at[group, t],
        )

    def out_copies(group):
        if group == 0:
            return [pltpu.make_async_copy(sums.at[0], away, out_sems.at[0])]
        return [pltpu.make_async_copy(sums.at[1, s], outs[s], out_sems.at[1 + s]) for s in range(side)]

    for layer in range(layers):
        for k in range(count):
            left_copy(k, layer).start()
            if layer == 0:
                for t in range(len(tiles)):
                    if tiles[t][0] == k:
                        right_copy(0, t).start()
    for t in range(len(tiles)):
        right_copy(1, t).start()
    for group in range(2):
        where = there if group == 0 else here
        for layer in range(layers):
            for t, (k, at, start, step) in enumerate(tiles):
                if group == 0 and at == 0:
                    left_copy(k, layer).wait()
                if layer == 0:
                    right_copy(group, t).wait()
                columns = slice(start, start + step)
                acc[:, :step] = dot(left[k * layers + layer], right[group, :, columns])
                put_pieces(acc, sums, group, columns, where, depth, side, rows, deep, layer * deep)
        for copy in out_copies(group):
            copy.start()
    for group in range(2):
        for copy in out_copies(group):
            copy.wait()


def layer_grad_kernel(depth, side, rows, there, here, lhs, rhs, *refs):
    away, outs, refs = refs[0], refs[1 : 1 + side], refs[1 + side :]
    left, right, acc, sums, left_sems, right_sem, out_sems = refs
    chunk, width = left.shape[1], right.shape[1] // 2

    def left_copy(z):
        row = pl.multiple_of(lax.rem(there[1] + z, depth) * chunk, 16)
        return pltpu.make_async_copy(lhs.at[pl.ds(row, chunk)], left.at[z], left_sems.at[z])

    def out_copies(z):
        copies = [pltpu.make_async_copy(sums.at[0, :, :, z], away.at[:, :, z], out_sems.at[z, 0])]
        for s in range(side):
            copies.append(pltpu.make_async_copy(sums.at[1, s, :, z], outs[s].at[:, z], out_sems.at[z, 1 + s]))
        return copies

    right_copy = pltpu.make_async_copy(rhs, right, right_sem)
    left_copy(0).start()
    right_copy.start()
    left_copy(1).start()
    right_copy.wait()
    for z in range(depth):
        left_copy(z).wait()
        if z + 2 < depth:
            left_copy(z + 2).start()
        acc[...] = dot(left[z], right[...])
        for group, where in ((0, there), (1, here)):
            column = pl.multiple_of(where[0] * width, LANES)
            for second in range(side):
                for first in range(side):
                    from_row = lax.rem(row_of(where, depth, side, second, first, z), side * side)
                    piece = acc[pl.ds(pl.multiple_of(from_row * rows, 16), rows), pl.ds(column, width)]
                    sums[group, second, first, z] = piece.astype(BF16)
        for copy in out_copies(z):
            copy.start()
    for z in range(depth):
        for copy in out_copies(z):
            copy.wait()


def rel_grad(pairs, shards, there, here):
    depth, side = grid_of(shards)
    features, length = pairs[0][0].shape
    widths = [rhs.shape[1] // 2 for _, rhs in pairs]
    width = sum(widths)
    rows = features // shards
    core = lax.axis_index("dp")
    if rows % 16 != 0:
        both = []
        for half, where in ((1 - core, there), (core, here)):
            wholes = [
                lax.dot_general(
                    lhs,
                    lax.dynamic_slice_in_dim(rhs, half * (rhs.shape[1] // 2), rhs.shape[1] // 2, axis=1),
                    (((1,), (0,)), ((), ())),
                    preferred_element_type=F32,
                )
                for lhs, rhs in pairs
            ]
            whole = jnp.concatenate(wholes, axis=1).reshape(depth, side, side, rows, width)
            rel = jnp.where(half == 0, whole.transpose(1, 2, 0, 3, 4), whole.transpose(2, 1, 0, 3, 4))
            rel = jnp.roll(rel, -where[3], axis=0)
            rel = jnp.roll(rel, -where[2], axis=1)
            both.append(jnp.roll(rel, -where[1], axis=2).astype(BF16))
        return both[0], [both[1][s] for s in range(side)]
    deep = depth if features <= 1024 else 1
    chunk = features if deep > 1 else features // depth
    layers = depth // deep
    count, pieces = len(pairs), len(tiles_of(widths))
    if layers > 1 and count == 1 and 2 * width <= 768:
        out = pl.pallas_call(
            functools.partial(layer_grad_kernel, depth, side, rows),
            in_specs=[SMEM, SMEM, HBM, HBM],
            out_specs=[HBM] * (1 + side),
            out_shape=[jax.ShapeDtypeStruct((side, side, depth, rows, width), BF16)]
            + [jax.ShapeDtypeStruct((side, depth, rows, width), BF16)] * side,
            scratch_shapes=[
                pltpu.VMEM((depth, chunk, length), BF16),
                pltpu.VMEM((length, 2 * width), BF16),
                pltpu.VMEM((chunk, 2 * width), F32),
                pltpu.VMEM((2, side, side, depth, rows, width), BF16),
                pltpu.SemaphoreType.DMA((depth,)),
                pltpu.SemaphoreType.DMA,
                pltpu.SemaphoreType.DMA((depth, 1 + side)),
            ],
            compiler_params=pltpu.CompilerParams(vmem_limit_bytes=VMEM_MOST * MEBI),
            cost_estimate=pl.CostEstimate(flops=4 * length * features * width, bytes_accessed=20 * MEBI, transcendentals=0),
            name="layer_grad",
        )(there, here, *pairs[0])
        return out[0], out[1:]
    out = pl.pallas_call(
        functools.partial(grad_kernel, depth, side, rows, deep, widths),
        in_specs=[SMEM, SMEM] + [HBM] * (2 * count),
        out_specs=[HBM] * (1 + side),
        out_shape=[jax.ShapeDtypeStruct((side, side, depth, rows, width), BF16)]
        + [jax.ShapeDtypeStruct((side, depth, rows, width), BF16)] * side,
        scratch_shapes=[
            pltpu.VMEM((count * layers, chunk, length), BF16),
            pltpu.VMEM((2, length, width), BF16),
            pltpu.VMEM((chunk, min(768, max(widths))), F32),
            pltpu.VMEM((2, side, side, depth, rows, width), BF16),
            pltpu.SemaphoreType.DMA((count * layers,)),
            pltpu.SemaphoreType.DMA((2, pieces)),
            pltpu.SemaphoreType.DMA((1 + side,)),
        ],
        compiler_params=pltpu.CompilerParams(vmem_limit_bytes=VMEM_MOST * MEBI),
        cost_estimate=pl.CostEstimate(flops=4 * length * features * width, bytes_accessed=20 * MEBI, transcendentals=0),
        name="grad",
    )(there, here, *(operand for pair in pairs for operand in pair))
    return out[0], out[1:]


def sum_of(*values):
    total = values[0].astype(F32)
    for value in values[1:]:
        total = total + value.astype(F32)
    return total.astype(BF16)


def second_sends(own, got):
    return [sum_of(own[s], got[s]) for s in range(1, got.shape[0])]


def second_parts(sends, shards):
    _, side = grid_of(shards)
    return [arrive(send, shards, "second", side - 1 - k) for k, send in enumerate(sends)]


def second_sums(own, got, parts):
    return [sum_of(own[0][f], got[0, f], *(part[f] for part in parts)) for f in range(got.shape[1])]


def first_parts(sums, shards):
    _, side = grid_of(shards)
    return [arrive(sums[f], shards, "first", side - f) for f in range(1, side)]


def first_sums(sums, parts):
    return [sum_of(sums[0][z], *(part[z] for part in parts)) for z in range(sums[0].shape[0])]


def z_parts(sums, shards):
    depth, _ = grid_of(shards)
    return [sums[0]] + [arrive(sums[z], shards, "z", depth - z) for z in range(1, depth)]


def line_parts(lines, shards, kind):
    _, side = grid_of(shards)
    if kind == "second_flip_1":
        straight = line_parts(lines, shards, "second")
        return straight + [arrive(lines, shards, "slant", step) for step in range(side)]
    if kind in ("flip_1", "flip_2"):
        return [lines, arrive(lines, shards, "flip", int(kind[-1]))]
    count = 2 if kind == "core" else side
    return [lines] + [arrive(lines, shards, kind, step) for step in range(1, count)]


def exchange_lines(lines, shards, kind):
    return sum_of(*line_parts(lines, shards, kind))


def both_halves(mine, shards, widths):
    theirs = arrive(mine, shards, "core", 1)
    core = lax.axis_index("dp")
    left = jnp.where(core == 0, mine, theirs)
    right = jnp.where(core == 0, theirs, mine)
    wholes, start = [], 0
    for width in widths:
        columns = slice(start, start + width)
        wholes.append(jnp.concatenate([left[:, columns], right[:, columns]], axis=1).astype(F32))
        start += width
    return wholes


GAIN_ONE, SHIFT_ONE, BIAS_QUERY, BIAS_VALUE, BIAS_OUT, GAIN_TWO, SHIFT_TWO, BIAS_DOWN = range(8)
SCALE = HEAD_DIM ** (-0.5)


def weight_copies(plan, here, there, parts, outs, sems, first=0):
    groups = [[] for _ in outs]
    if plan is None:
        for k, (part, out) in enumerate(zip(parts, outs)):
            groups[k].append(pltpu.make_async_copy(part, out, sems.at[first + k]))
        return groups
    depth, side, rows, cuts = plan
    used = first
    for group in range(2):
        where = here if group == 0 else there
        for second in range(side):
            for ahead in range(side):
                for z in range(depth):
                    at = pl.multiple_of(row_of(where, depth, side, second, ahead, z) * rows, 16)
                    source = parts[group * side + second].at[ahead, z]
                    for k, ((start, width, split), out) in enumerate(zip(cuts, outs)):
                        if group == 1 and not split:
                            continue
                        column = pl.multiple_of(where[0] * width, LANES) if split else 0
                        groups[k].append(
                            pltpu.make_async_copy(
                                source.at[:, pl.ds(start, width)],
                                out.at[pl.ds(at, rows), pl.ds(column, width)],
                                sems.at[used],
                            )
                        )
                        used += 1
    return groups


def bring(groups):
    for group in groups:
        for copy in group:
            copy.start()
    for group in groups:
        for copy in group:
            copy.wait()


def copies_of(plan, shards, cuts):
    if plan is None:
        return len(cuts)
    return shards * sum(2 if split else 1 for _, _, split in cuts)


def standardize(values):
    average = jnp.mean(values, axis=-1, keepdims=True)
    centred = values - average
    spread = jnp.mean(centred * centred, axis=-1, keepdims=True)
    inverse = lax.rsqrt(spread + EPSILON)
    return centred * inverse, inverse


def dot(a, b, dims=((1,), (0,))):
    return lax.dot_general(a, b, (dims, ((), ())), preferred_element_type=F32)


NT = ((1,), (1,))
TN = ((0,), (0,))


def project_kernel(plan, count, here, there, tokens, lines, *refs):
    parts = refs[:count]
    normed_ref, qkv_ref = refs[count : count + 2]
    weight, sems = refs[count + 2 :]
    width = tokens.shape[1]

    @pl.when(pl.program_id(0) == 0)
    def _():
        bring(weight_copies(plan, here, there, parts, (weight,), sems))

    standard, _ = standardize(tokens[...].astype(F32))
    normed = (standard * lines[pl.ds(GAIN_ONE, 1), :] + lines[pl.ds(SHIFT_ONE, 1), :]).astype(BF16)
    normed_ref[...] = normed.T
    bias = (lines[pl.ds(BIAS_QUERY, 1), :], None, lines[pl.ds(BIAS_VALUE, 1), :])
    for part in range(3):
        columns = slice(part * width, (part + 1) * width)
        project = dot(normed, weight[:, columns])
        if bias[part] is not None:
            project = project + bias[part]
        qkv_ref[:, columns] = project.astype(BF16)


def attend_kernel(frames, qkv_ref, mixed_ref, turned_ref, power_ref, inverse_ref):
    tube = pl.program_id(0)
    length, width = mixed_ref.shape
    mask = jnp.where(lax.broadcasted_iota(jnp.int32, (1, length), 1) < frames[tube] * PATCH, 0.0, -1e30)
    lower = lax.broadcasted_iota(jnp.int32, (length, LANES), 1) < HEAD_DIM
    ones = jnp.ones((length, LANES), BF16)
    for pair in range(width // LANES):
        query = qkv_ref[:, pair * LANES : (pair + 1) * LANES] * jnp.asarray(SCALE, BF16)
        keys = qkv_ref[:, width + pair * LANES : width + (pair + 1) * LANES]
        values = qkv_ref[:, 2 * width + pair * LANES : 2 * width + (pair + 1) * LANES]
        values = jnp.concatenate([values, ones], axis=1)
        both = []
        for k in range(2):
            own = jnp.where(lower if k == 0 else ~lower, query, jnp.zeros_like(query))
            scores = dot(own, keys, NT) + mask
            power = jnp.exp(scores - jnp.max(scores, axis=-1, keepdims=True)).astype(BF16)
            power_ref[0, 2 * pair + k] = power
            both.append(dot(power, values))
        inverse = 1.0 / jnp.where(lower, both[0][:, LANES:], both[1][:, LANES:])
        inverse_ref[:, pair * LANES : (pair + 1) * LANES] = inverse.astype(BF16)
        mixed = jnp.where(lower, both[0][:, :LANES], both[1][:, :LANES]) * inverse
        mixed = mixed.astype(BF16)
        mixed_ref[:, pair * LANES : (pair + 1) * LANES] = mixed
        turned_ref[pair * LANES : (pair + 1) * LANES, :] = mixed.T


def feed_kernel(plan, count, here, there, frames, tokens, mixed, cotangent, lines, up_bias, *refs):
    parts = refs[:count]
    resid_ref, normed_ref, active_ref, turned_ref, slope_ref, upstream_ref = refs[count : count + 6]
    out_weight, up_weight, sems = refs[count + 6 :]
    tube = pl.program_id(0)
    first, last = weight_copies(plan, here, there, parts, (out_weight, up_weight), sems)

    @pl.when(tube == 0)
    def _():
        for copy in first + last:
            copy.start()
        for copy in first:
            copy.wait()

    length = tokens.shape[0]
    row_ok = lax.broadcasted_iota(jnp.int32, (length, 1), 0) < frames[tube] * PATCH
    upstream_ref[...] = jnp.where(row_ok, cotangent[...], jnp.zeros_like(cotangent))
    attended = dot(mixed[...], out_weight[...]) + lines[pl.ds(BIAS_OUT, 1), :]
    resid = tokens[...].astype(F32) + attended
    resid_ref[...] = resid.astype(BF16)
    standard, _ = standardize(resid)
    normed = (standard * lines[pl.ds(GAIN_TWO, 1), :] + lines[pl.ds(SHIFT_TWO, 1), :]).astype(BF16)
    normed_ref[...] = normed.T

    @pl.when(tube == 0)
    def _():
        for copy in last:
            copy.wait()

    units = up_weight.shape[1]
    step = 512
    for at in range(0, units, step):
        hidden = dot(normed, up_weight[:, at : at + step]) + up_bias[:, at : at + step]
        cumulative = 0.5 + 0.5 * lax.erf(hidden * SQRT_HALF)
        density = jnp.exp2(hidden * hidden * (-0.5 * LOG2_E) + LOG2_DENSITY)
        active = (hidden * cumulative).astype(BF16)
        active_ref[:, at : at + step] = active
        turned_ref[at : at + step, :] = active.T
        slope_ref[:, at : at + step] = (cumulative + hidden * density).astype(BF16)


def norm_back(grad, standard, inverse, gain):
    scaled = grad * gain
    first = jnp.mean(scaled, axis=-1, keepdims=True)
    second = jnp.mean(scaled * standard, axis=-1, keepdims=True)
    return inverse * (scaled - first - standard * second)


def column_sum(values):
    return jnp.sum(values, axis=0, keepdims=True)


SUM_GAIN_TWO, SUM_SHIFT_TWO, SUM_BIAS_OUT, SUM_BIAS_DOWN = range(4)


def feed_back_kernel(plans, counts, depth, side, rows, direct, here, there, upstream, slope, resid, inverse_sums, lines, *refs):
    mixed_hbm, normed_hbm, refs = refs[0], refs[1], refs[2:]
    ff_parts, refs = refs[: counts[0]], refs[counts[0] :]
    down_parts, refs = refs[: counts[1]], refs[counts[1] :]
    attended_ref, scaled_ref, sums_ref, up_sum_ref = refs[:4]
    refs = refs[4:]
    if direct:
        away, outs, refs = refs[0], refs[1 : 1 + side], refs[1 + side :]
    else:
        hidden_hbm, refs = refs[0], refs[1:]
    out_weight, up_weight, down_weight, hidden_all, attended_all, sems, more_sems = refs[:7]
    tube, last = pl.program_id(0), pl.num_programs(0) - 1
    length, width = upstream.shape
    units = up_weight.shape[1]
    (down_copies,) = weight_copies(plans[1], here, there, down_parts, (down_weight,), sems)
    ff_copies = weight_copies(plans[0], here, there, ff_parts, (out_weight, up_weight), sems, len(down_copies))
    if direct:
        turned, acc, sums = refs[7:]
        left_copies = [
            pltpu.make_async_copy(mixed_hbm, turned.at[0], more_sems.at[0]),
            pltpu.make_async_copy(normed_hbm, turned.at[1], more_sems.at[1]),
        ]

    @pl.when(tube == 0)
    def _():
        for copy in down_copies:
            copy.start()
        for group in reversed(ff_copies):
            for copy in group:
                copy.start()
        if direct:
            for copy in left_copies:
                copy.start()
        sums_ref[...] = jnp.zeros_like(sums_ref)
        up_sum_ref[...] = jnp.zeros_like(up_sum_ref)
        for copy in down_copies:
            copy.wait()

    here_rows = pl.ds(pl.multiple_of(tube * length, 16), length)
    low = upstream[...]
    standard, inverse = standardize(resid[...].astype(F32))
    step = 768
    for at in range(0, units, step):
        grad = dot(low, down_weight[at : at + step, :], NT) * slope[:, at : at + step].astype(F32)
        hidden_all[here_rows, at : at + step] = grad.astype(BF16)
        up_sum_ref[:, at : at + step] += column_sum(grad)

    @pl.when(tube == 0)
    def _():
        for group in ff_copies:
            for copy in group:
                copy.wait()

    normed_grad = dot(hidden_all[here_rows, :], up_weight[...], NT)
    above = low.astype(F32)
    resid_grad = above + norm_back(normed_grad, standard, inverse, lines[pl.ds(GAIN_TWO, 1), :])
    attended_grad = resid_grad.astype(BF16)
    attended_ref[...] = attended_grad
    attended_all[here_rows, :] = attended_grad
    scaled_ref[...] = (dot(attended_grad, out_weight[...], NT) * inverse_sums[...].astype(F32)).astype(BF16)
    sums_ref[pl.ds(SUM_GAIN_TWO, 1), :] += column_sum(normed_grad * standard)
    sums_ref[pl.ds(SUM_SHIFT_TWO, 1), :] += column_sum(normed_grad)
    sums_ref[pl.ds(SUM_BIAS_OUT, 1), :] += column_sum(attended_grad.astype(F32))
    sums_ref[pl.ds(SUM_BIAS_DOWN, 1), :] += column_sum(above)

    if not direct:

        @pl.when(tube == last)
        def _():
            copy = pltpu.make_async_copy(hidden_all, hidden_hbm, more_sems.at[0])
            copy.start()
            copy.wait()

        return

    @pl.when(tube == 1)
    def _():
        for k in range(2):
            left_copies[k].wait()

    @pl.when(tube == last)
    def _():
        waits = []
        for group in range(2):
            where = there if group == 0 else here
            for k, at, start, size in tiles_of((width // 2, units // 2)):
                right = attended_all if k == 0 else hidden_all
                column = pl.multiple_of(where[0] * (right.shape[1] // 2) + at, LANES)
                acc[:, :size] = dot(turned[k], right[:, pl.ds(column, size)])
                put_pieces(acc, sums, group, slice(start, start + size), where, depth, side, rows, depth, 0)
            if group == 0:
                waits.append(pltpu.make_async_copy(sums.at[0], away, more_sems.at[2]))
                waits[-1].start()
            else:
                for s in range(side):
                    waits.append(pltpu.make_async_copy(sums.at[1, s], outs[s], more_sems.at[3 + s]))
                    waits[-1].start()
        for copy in waits:
            copy.wait()


def attend_back_kernel(qkv, power_ref, mixed, scaled_grad, grad_ref, sums_ref):
    tube = pl.program_id(0)

    @pl.when(tube == 0)
    def _():
        sums_ref[...] = jnp.zeros_like(sums_ref)

    length, width = mixed.shape
    lower = lax.broadcasted_iota(jnp.int32, (length, LANES), 1) < HEAD_DIM
    for pair in range(width // LANES):
        lanes = slice(pair * LANES, (pair + 1) * LANES)
        query = qkv[:, lanes]
        keys = qkv[:, width + pair * LANES : width + (pair + 1) * LANES]
        values = qkv[:, 2 * width + pair * LANES : 2 * width + (pair + 1) * LANES]
        above = scaled_grad[:, lanes]
        product = above.astype(F32) * mixed[:, lanes].astype(F32)
        query_grad, keys_grad, values_grad = [], [], []
        for k in range(2):
            mine = lower if k == 0 else ~lower
            own = jnp.where(mine, above, jnp.zeros_like(above))
            power = power_ref[0, 2 * pair + k]
            inner = jnp.sum(jnp.where(mine, product, 0.0), axis=-1, keepdims=True)
            scores_grad = (power.astype(F32) * (dot(own, values, NT) - inner)).astype(BF16)
            values_grad.append(dot(power, above, TN))
            query_grad.append(dot(scores_grad, keys))
            keys_grad.append(dot(scores_grad, query, TN))
        for part, (pieces, scale) in enumerate(((query_grad, SCALE), (keys_grad, SCALE), (values_grad, None))):
            piece = jnp.where(lower, pieces[0], pieces[1])
            if scale is not None:
                piece = piece * scale
            grad_ref[:, part * width + pair * LANES : part * width + (pair + 1) * LANES] = piece.astype(BF16)
            if part != 1:
                sums_ref[pl.ds(part // 2, 1), lanes] += column_sum(piece)


def first_back_kernel(plan, count, here, there, tokens, project_grad, attended_grad, lines, *refs):
    parts = refs[:count]
    tokens_ref, sums_ref = refs[count : count + 2]
    weight, sems = refs[count + 2 :]
    tube = pl.program_id(0)

    @pl.when(tube == 0)
    def _():
        bring(weight_copies(plan, here, there, parts, (weight,), sems))
        sums_ref[...] = jnp.zeros_like(sums_ref)

    grad = dot(project_grad[...], weight[...], NT)
    standard, inverse = standardize(tokens[...].astype(F32))
    inputs_grad = norm_back(grad, standard, inverse, lines[pl.ds(GAIN_ONE, 1), :])
    tokens_ref[...] = (attended_grad[...].astype(F32) + inputs_grad).astype(BF16)
    sums_ref[pl.ds(0, 1), :] += column_sum(grad * standard)
    sums_ref[pl.ds(1, 1), :] += column_sum(grad)


def block_out_kernel(plan, count, here, there, active, resid, lines, *refs):
    parts = refs[:count]
    out_ref = refs[count]
    weight, sems = refs[count + 1 :]

    @pl.when(pl.program_id(0) == 0)
    def _():
        bring(weight_copies(plan, here, there, parts, (weight,), sems))

    branch = dot(active[...], weight[...]) + lines[pl.ds(BIAS_DOWN, 1), :]
    out_ref[...] = (resid[...].astype(F32) + branch).astype(BF16)


def rows_of(width, length):
    return pl.BlockSpec((length, width), lambda t: (t, 0))


def fixed(*shape):
    return pl.BlockSpec(shape, lambda t: (0,) * len(shape))


def shape_of(*shape, kind=BF16):
    return jax.ShapeDtypeStruct(shape, kind)


def call(kernel, name, grid, in_specs, outs, scratch, flops, *args):
    return pl.pallas_call(
        kernel,
        grid=(grid,),
        in_specs=in_specs,
        out_specs=[spec for spec, _ in outs],
        out_shape=[shape for _, shape in outs],
        scratch_shapes=scratch,
        compiler_params=pltpu.CompilerParams(vmem_limit_bytes=VMEM_MOST * MEBI),
        cost_estimate=pl.CostEstimate(flops=flops, bytes_accessed=16 * MEBI, transcendentals=0),
        name=name,
    )(*args)


def local(
    tokens,
    clip_frames,
    tube_clip,
    first_gain,
    first_shift,
    qkv_weight,
    query_bias,
    value_bias,
    out_weight,
    out_bias,
    second_gain,
    second_shift,
    up_weight,
    up_bias,
    down_weight,
    down_bias,
    cotangent,
):
    shards = lax.axis_size("fsdp")
    depth, side = grid_of(shards)
    core = lax.axis_index("dp")
    total, width = tokens.shape
    tubes = tube_clip.shape[0]
    length = total // tubes
    clip_count = clip_frames.shape[0]

    def half(matrix):
        columns = matrix.shape[1] // 2
        return lax.dynamic_slice_in_dim(matrix, core * columns, columns, axis=1)

    wide, full, ff = qkv_weight.shape[1] // 2, out_weight.shape[1] // 2, up_weight.shape[1] // 2
    units = 2 * ff
    rows = first_gain.shape[0]
    vectors = [first_gain, first_shift, query_bias, value_bias, out_bias, second_gain, second_shift, down_bias]
    vectors += [up_bias[k * rows : (k + 1) * rows] for k in range(4)]
    pack_one = half(qkv_weight)
    pack_two = jnp.concatenate([half(out_weight), half(up_weight)], axis=1)
    cuts = (
        ((0, wide, True),),
        ((0, full, True), (full, ff, True)),
        ((0, full, True),),
    )
    plans, counts = [], []
    for pack, cut in zip((pack_one, pack_two, down_weight), cuts):
        direct = pack.shape[0] % 16 == 0
        plans.append((depth, side, pack.shape[0], cut) if direct else None)
        counts.append(2 * side if direct else len(cut))

    def finish(k, own, other):
        return [*own, *other] if plans[k] is not None else assemble(own, other, shards, cuts[k])

    number = [copies_of(plan, shards, cut) for plan, cut in zip(plans, cuts)]
    sem = pltpu.SemaphoreType.DMA
    big = 2 * total * width * width
    narrow, wide_rows, deep_rows = rows_of(width, length), rows_of(3 * width, length), rows_of(units, length)
    upright = pl.BlockSpec((width, length), lambda t: (0, t))
    tall = total // 2
    tall_narrow, tall_wide, tall_deep = rows_of(width, tall), rows_of(3 * width, tall), rows_of(units, tall)
    probs_spec = pl.BlockSpec((1, HEADS, length, length), lambda t: (t, 0, 0, 0))

    near, far = (1, depth - 1), range(2, depth - 1)

    def stack_z(unit, near_units, far_units):
        return jnp.stack([unit, near_units[0], *far_units, near_units[1]])

    spread = spread_lines(vectors, shards)
    z_one = stack_z(pack_one, from_z(pack_one, shards, near), from_z(pack_one, shards, far))
    z_one, spread, pack_two = lax.optimization_barrier((z_one, spread, pack_two))
    first_one = gather_first(z_one, shards)
    near_two = from_z(pack_two, shards, near)
    spread = exchange_lines(spread, shards, "first")
    first_one, near_two, spread, pack_two, tube_clip, down_weight = lax.optimization_barrier(
        (first_one, near_two, spread, pack_two, tube_clip, down_weight)
    )
    second_one = gather_second(first_one, shards)
    early_one = arrive(first_one, shards, "core", 1)
    z_two = stack_z(pack_two, near_two, from_z(pack_two, shards, far))
    spread = exchange_lines(spread, shards, "second")
    pack_three = half(down_weight)
    here, there = place(shards, core), place(shards, 1 - core)
    matches = tube_clip[:, None] == jnp.arange(clip_count, dtype=jnp.int32)[None, :]
    frames = jnp.sum(jnp.where(matches, clip_frames[None, :], 0), axis=1)
    second_one, early_one, z_two, spread, pack_three, here, there, frames = lax.optimization_barrier(
        (second_one, early_one, z_two, spread, pack_three, here, there, frames)
    )
    core_one = [early_one] + gather_core(second_one[1:], shards)
    first_two = gather_first(z_two, shards)
    for kind in ("flip_1", "flip_2"):
        spread = exchange_lines(spread, shards, kind)
    lines = join_lines(spread, len(vectors), rows)
    up_row = lines[8:12].reshape(4, shards, rows).transpose(1, 0, 2).reshape(1, units)
    core_one, first_two, pack_three, tokens, lines, up_row = lax.optimization_barrier(
        (core_one, first_two, pack_three, tokens, lines, up_row)
    )
    parts_one = finish(0, second_one, core_one)
    second_two = gather_second(first_two, shards)
    early_two = arrive(first_two, shards, "core", 1)
    z_three = stack_z(pack_three, from_z(pack_three, shards, near), from_z(pack_three, shards, far))

    normed_one, qkv = call(
        functools.partial(project_kernel, plans[0], counts[0]),
        "project",
        tubes,
        [SMEM, SMEM, narrow, fixed(16, width)] + [HBM] * counts[0],
        [(upright, shape_of(width, total)), (wide_rows, shape_of(total, 3 * width))],
        [pltpu.VMEM((width, 3 * width), BF16), sem((number[0],))],
        3 * big,
        here, there, tokens, lines, *parts_one,
    )
    z_three, qkv, early_two = lax.optimization_barrier((z_three, qkv, early_two))

    mixed, mixed_turned, power, inverse = call(
        attend_kernel,
        "attend",
        tubes,
        [SMEM, wide_rows],
        [
            (narrow, shape_of(total, width)),
            (upright, shape_of(width, total)),
            (probs_spec, shape_of(tubes, HEADS, length, length)),
            (narrow, shape_of(total, width)),
        ],
        [],
        4 * big,
        frames, qkv,
    )
    first_three = gather_first(z_three, shards)
    second_two, mixed, first_three = lax.optimization_barrier((second_two, mixed, first_three))
    core_two = [early_two] + gather_core(second_two[1:], shards)
    core_two, first_three, mixed = lax.optimization_barrier((core_two, first_three, mixed))
    parts_two = finish(1, second_two, core_two)
    second_three = gather_second(first_three, shards)
    early_three = arrive(first_three, shards, "core", 1)

    resid, normed_two, active, active_turned, slope, upstream = call(
        functools.partial(feed_kernel, plans[1], counts[1]),
        "feed",
        tubes,
        [SMEM, SMEM, SMEM, narrow, narrow, narrow, fixed(16, width), fixed(1, units)] + [HBM] * counts[1],
        [
            (narrow, shape_of(total, width)),
            (upright, shape_of(width, total)),
            (deep_rows, shape_of(total, units)),
            (pl.BlockSpec((units, length), lambda t: (0, t)), shape_of(units, total)),
            (deep_rows, shape_of(total, units)),
            (narrow, shape_of(total, width)),
        ],
        [pltpu.VMEM((width, width), BF16), pltpu.VMEM((width, units), BF16), sem((number[1],))],
        8 * big,
        here, there, frames, tokens, mixed, cotangent, lines, up_row, *parts_two,
    )
    second_three, early_three, active_turned, upstream = lax.optimization_barrier(
        (second_three, early_three, active_turned, upstream)
    )
    core_three = [early_three] + gather_core(second_three[1:], shards)
    down_away, down_own = rel_grad([(active_turned, upstream)], shards, there, here)
    core_three, down_away, slope = lax.optimization_barrier((core_three, down_away, slope))
    down_got = arrive(down_away, shards, "core", 1)
    down_got, slope = lax.optimization_barrier((down_got, slope))
    parts_three = finish(2, second_three, core_three)
    down_sends, slope = lax.optimization_barrier((second_sends(down_own, down_got), slope))
    down_parts = second_parts(down_sends, shards)

    direct = rows % 16 == 0
    ff_width = full + ff
    outs = [
        (narrow, shape_of(total, width)),
        (narrow, shape_of(total, width)),
        (fixed(8, width), shape_of(8, width, kind=F32)),
        (fixed(1, units), shape_of(1, units, kind=F32)),
    ]
    scratch = [
        pltpu.VMEM((width, width), BF16),
        pltpu.VMEM((width, units), BF16),
        pltpu.VMEM((units, width), BF16),
        pltpu.VMEM((total, units), BF16),
        pltpu.VMEM((total, width), BF16),
        sem((number[1] + number[2],)),
        sem((3 + side,)),
    ]
    if direct:
        outs.append((HBM, shape_of(side, side, depth, rows, ff_width)))
        outs += [(HBM, shape_of(side, depth, rows, ff_width))] * side
        scratch += [
            pltpu.VMEM((2, width, total), BF16),
            pltpu.VMEM((width, 768), F32),
            pltpu.VMEM((2, side, side, depth, rows, ff_width), BF16),
        ]
    else:
        outs.append((HBM, shape_of(total, units)))
    attended_grad, scaled_grad, sums_two, up_sum, *more = call(
        functools.partial(feed_back_kernel, plans[1:], counts[1:], depth, side, rows, direct),
        "feed_back",
        tubes,
        [SMEM, SMEM, narrow, deep_rows, narrow, narrow, fixed(16, width)] + [HBM] * (2 + counts[1] + counts[2]),
        outs,
        scratch,
        14 * big,
        here, there, upstream, slope, resid, inverse, lines, mixed_turned, normed_two, *parts_two, *parts_three,
    )
    if direct:
        ff_away, ff_own = more[0], more[1:]
    else:
        ff_away, ff_own = rel_grad([(mixed_turned, attended_grad), (normed_two, more[0])], shards, there, here)
    down_parts, ff_away, scaled_grad = lax.optimization_barrier((down_parts, ff_away, scaled_grad))
    ff_got = arrive(ff_away, shards, "core", 1)
    down_sums = second_sums(down_own, down_got, down_parts)
    down_parts = first_parts(down_sums, shards)
    ff_got, scaled_grad, down_sums = lax.optimization_barrier((ff_got, scaled_grad, down_sums))
    ff_sends, scaled_grad = lax.optimization_barrier((second_sends(ff_own, ff_got), scaled_grad))
    ff_parts = second_parts(ff_sends, shards)

    project_grad, sums_heads = call(
        attend_back_kernel,
        "attend_back",
        tubes,
        [wide_rows, probs_spec, narrow, narrow],
        [(wide_rows, shape_of(total, 3 * width)), (fixed(8, width), shape_of(8, width, kind=F32))],
        [],
        4 * big,
        qkv, power, mixed, scaled_grad,
    )
    project_grad, down_parts = lax.optimization_barrier((project_grad, down_parts))
    down_sums, project_grad = lax.optimization_barrier((first_sums(down_sums, down_parts), project_grad))
    down_parts = z_parts(down_sums, shards)
    qkv_away, qkv_own = rel_grad([(normed_one, project_grad)], shards, there, here)
    qkv_away, project_grad, ff_parts = lax.optimization_barrier((qkv_away, project_grad, ff_parts))
    qkv_got = arrive(qkv_away, shards, "core", 1)
    ff_sums, project_grad = lax.optimization_barrier((second_sums(ff_own, ff_got, ff_parts), project_grad))
    ff_parts = first_parts(ff_sums, shards)

    tokens_grad, sums_one = call(
        functools.partial(first_back_kernel, plans[0], counts[0]),
        "first_back",
        2,
        [SMEM, SMEM, tall_narrow, tall_wide, tall_narrow, fixed(16, width)] + [HBM] * counts[0],
        [(tall_narrow, shape_of(total, width)), (fixed(8, width), shape_of(8, width, kind=F32))],
        [pltpu.VMEM((width, 3 * width), BF16), sem((number[0],))],
        3 * big,
        here, there, tokens, project_grad, attended_grad, lines, *parts_one,
    )
    qkv_got, ff_parts, tokens_grad, sums_one, active, down_parts = lax.optimization_barrier(
        (qkv_got, ff_parts, tokens_grad, sums_one, active, down_parts)
    )
    sums = jnp.concatenate(
        [
            sums_one[:2],
            sums_heads[:2],
            sums_two[SUM_BIAS_OUT : SUM_BIAS_OUT + 1],
            sums_two[SUM_GAIN_TWO : SUM_GAIN_TWO + 1],
            sums_two[SUM_SHIFT_TWO : SUM_SHIFT_TWO + 1],
            sums_two[SUM_BIAS_DOWN : SUM_BIAS_DOWN + 1],
            up_sum.reshape(-1, width),
        ],
        axis=0,
    ).astype(BF16)
    ff_sums, qkv_sends, sums, active = lax.optimization_barrier(
        (first_sums(ff_sums, ff_parts), second_sends(qkv_own, qkv_got), sums, active)
    )
    ff_parts = z_parts(ff_sums, shards)
    qkv_parts = second_parts(qkv_sends, shards)
    sums = line_parts(sums, shards, "first")

    (block_out,) = call(
        functools.partial(block_out_kernel, plans[2], counts[2]),
        "block_out",
        tubes,
        [SMEM, SMEM, deep_rows, narrow, fixed(16, width)] + [HBM] * counts[2],
        [(narrow, shape_of(total, width))],
        [pltpu.VMEM((units, width), BF16), sem((number[2],))],
        4 * big,
        here, there, active, resid, lines, *parts_three,
    )
    block_out, ff_parts, qkv_parts, sums, down_parts = lax.optimization_barrier(
        (block_out, ff_parts, qkv_parts, sums, down_parts)
    )
    qkv_sums = second_sums(qkv_own, qkv_got, qkv_parts)
    qkv_parts = first_parts(qkv_sums, shards)
    sums = exchange_lines(sum_of(*sums), shards, "second_flip_1")
    sums = line_parts(sums, shards, "flip_2")
    qkv_parts, sums, ff_parts, down_parts = lax.optimization_barrier((qkv_parts, sums, ff_parts, down_parts))
    qkv_sums, sums = lax.optimization_barrier((first_sums(qkv_sums, qkv_parts), sum_of(*sums)))
    qkv_parts = z_parts(qkv_sums, shards)
    (down_whole,) = both_halves(sum_of(*down_parts), shards, (full,))
    out_whole, up_whole = both_halves(sum_of(*ff_parts), shards, (full, ff))
    sums = exchange_lines(sums, shards, "core")
    at = lax.axis_index("fsdp")
    sums_here = lax.dynamic_slice_in_dim(sums[:8], at * rows, rows, axis=1).astype(F32)
    up_here = lax.dynamic_slice_in_dim(sums[8:].reshape(-1), at * up_bias.shape[0], up_bias.shape[0]).astype(F32)
    qkv_parts, sums_here, up_here, down_whole, out_whole, up_whole = lax.optimization_barrier(
        (qkv_parts, sums_here, up_here, down_whole, out_whole, up_whole)
    )
    (qkv_whole,) = both_halves(sum_of(*qkv_parts), shards, (wide,))
    return (
        block_out,
        tokens_grad,
        sums_here[0],
        sums_here[1],
        qkv_whole,
        sums_here[2],
        sums_here[3],
        out_whole,
        sums_here[4],
        sums_here[5],
        sums_here[6],
        up_whole,
        up_here,
        down_whole,
        sums_here[7],
    )


def solution(mesh):
    return jax.shard_map(
        local,
        mesh=mesh,
        in_specs=(
            P(("dp", "fsdp"), None),
            P(),
            P(("dp", "fsdp")),
            P("fsdp"),
            P("fsdp"),
            P("fsdp", None),
            P("fsdp"),
            P("fsdp"),
            P("fsdp", None),
            P("fsdp"),
            P("fsdp"),
            P("fsdp"),
            P("fsdp", None),
            P("fsdp"),
            P("fsdp", None),
            P("fsdp"),
            P(("dp", "fsdp"), None),
        ),
        out_specs=(
            P(("dp", "fsdp"), None),
            P(("dp", "fsdp"), None),
            P("fsdp"),
            P("fsdp"),
            P("fsdp", None),
            P("fsdp"),
            P("fsdp"),
            P("fsdp", None),
            P("fsdp"),
            P("fsdp"),
            P("fsdp"),
            P("fsdp", None),
            P("fsdp"),
            P("fsdp", None),
            P("fsdp"),
        ),
        check_vma=False,
    )
```

```python
import functools
import math

import jax
import jax.numpy as jnp
from jax import lax
from jax.experimental import pallas as pl
from jax.experimental.pallas import tpu as pltpu
from jax.sharding import PartitionSpec as P

HEADS = 12
HEAD_DIM = 64
PATCH = 16
EPSILON = 1e-05
SQRT_HALF = 0.7071067811865476
LOG2_E = 1.4426950408889634
LOG2_DENSITY = -1.3257480647361593
AXES = ("dp", "fsdp")
F32 = jnp.float32
BF16 = jnp.bfloat16
LANES = 128
MEBI = 1 << 20
VMEM_MOST = 53
SMEM = pl.BlockSpec(memory_space=pltpu.SMEM)
HBM = pl.BlockSpec(memory_space=pl.ANY)


def grid_of(shards):
    side = math.isqrt(shards // 4)
    assert 4 * side * side == shards
    return 4, side


def arrive(value, shards, kind, step):
    depth, side = grid_of(shards)
    pairs = []
    for core in range(2):
        for z in range(depth):
            for y in range(side):
                for x in range(side):
                    to = core * shards + (z * side + y) * side + x
                    at = [core, z, y, x]
                    if kind == "core":
                        at[0] = 1 - core
                    elif kind == "z":
                        at[1] = (z + step) % depth
                    elif kind == "flip":
                        at[1] = z ^ step
                    elif kind == "slant":
                        at[1] = 1 ^ z
                        if core == 0:
                            at[2] = (y + step) % side
                        else:
                            at[3] = (x + step) % side
                    elif (kind == "first") == (core == 0):
                        at[3] = (x + step) % side
                    else:
                        at[2] = (y + step) % side
                    pairs.append((at[0] * shards + (at[1] * side + at[2]) * side + at[3], to))
    with jax.named_scope(f"{kind}_exchange"):
        return lax.ppermute(value, AXES, pairs)


def place(shards, half):
    _, side = grid_of(shards)
    at = lax.axis_index("fsdp")
    z, y, x = at // (side * side), (at // side) % side, at % side
    first = jnp.where(half == 0, x, y)
    second = jnp.where(half == 0, y, x)
    return jnp.stack([half, z, first, second, lax.axis_index("dp")]).astype(jnp.int32)


def after(value, *earlier):
    return lax.optimization_barrier((value, *earlier))[0]


def spread_lines(vectors, shards):
    unit = jnp.concatenate(vectors)
    unit = jnp.pad(unit, (0, -unit.shape[0] % 1024)).reshape(1, -1, LANES)
    at = lax.broadcasted_iota(jnp.int32, (shards, 1, 1), 0) == lax.axis_index("fsdp")
    return jnp.where(at, unit, jnp.zeros_like(unit))


def join_lines(spread, count, rows):
    shards = spread.shape[0]
    whole = spread.reshape(shards, -1)[:, : count * rows].reshape(shards, count, rows)
    whole = whole.transpose(1, 0, 2).reshape(count, -1)
    return jnp.pad(whole.astype(F32), ((0, 16 - count), (0, 0)))


def from_z(unit, shards, steps):
    return [arrive(unit, shards, "z", s) for s in steps]


def gather_first(got, shards):
    _, side = grid_of(shards)
    return jnp.stack([got] + [arrive(got, shards, "first", s) for s in range(1, side)])


def gather_second(got, shards):
    _, side = grid_of(shards)
    return [got] + [arrive(got, shards, "second", s) for s in range(1, side)]


def gather_core(own, shards):
    return [arrive(part, shards, "core", 1) for part in own]


def row_of(where, depth, side, rel_second, rel_first, rel_z):
    z = lax.rem(where[1] + rel_z, depth)
    first = lax.rem(where[2] + rel_first, side)
    second = lax.rem(where[3] + rel_second, side)
    y = jnp.where(where[0] == 0, second, first)
    x = jnp.where(where[0] == 0, first, second)
    return (z * side + y) * side + x


def unroll_rows(parts, where, half, depth, side):
    rel = jnp.stack(parts)
    rel = jnp.roll(rel, where[3], axis=0)
    rel = jnp.roll(rel, where[2], axis=1)
    rel = jnp.roll(rel, where[1], axis=2)
    straight = jnp.where(half == 0, rel.transpose(2, 0, 1, 3, 4), rel.transpose(2, 1, 0, 3, 4))
    return straight.reshape(-1, rel.shape[-1])


def assemble(own, other, shards, cuts):
    depth, side = grid_of(shards)
    core = lax.axis_index("dp")
    here, there = place(shards, core), place(shards, 1 - core)
    mine = unroll_rows(own, here, core, depth, side)
    theirs = unroll_rows(other, there, 1 - core, depth, side)
    wholes = []
    for start, width, split in cuts:
        left, right = mine[:, start : start + width], theirs[:, start : start + width]
        if split:
            swapped = jnp.concatenate([right, left], axis=1)
            left = jnp.where(core == 0, jnp.concatenate([left, right], axis=1), swapped)
        wholes.append(left)
    return wholes


def tiles_of(widths):
    tiles, start = [], 0
    for k, width in enumerate(widths):
        at = 0
        while at < width:
            step = min(768, width - at)
            tiles.append((k, at, start + at, step))
            at += step
        start += width
    return tiles


def put_pieces(acc, sums, group, columns, where, depth, side, rows, deep, ahead):
    step = columns.stop - columns.start
    for second in range(side):
        for first in range(side):
            for z in range(deep):
                from_row = row_of(where, depth, side, second, first, z)
                if deep == 1:
                    from_row = lax.rem(from_row, side * side)
                piece = acc[pl.ds(pl.multiple_of(from_row * rows, 16), rows), :step]
                sums[group, second, first, ahead + z, :, columns] = piece.astype(BF16)


def grad_kernel(depth, side, rows, deep, widths, there, here, *refs):
    count = len(widths)
    layers = depth // deep
    tiles = tiles_of(widths)
    pairs, refs = refs[: 2 * count], refs[2 * count :]
    away, outs, refs = refs[:side], refs[side : 2 * side], refs[2 * side :]
    left, right, acc, sums, left_sems, right_sems, out_sems = refs
    chunk = left.shape[1]

    def left_copy(k, layer):
        row = pl.multiple_of(lax.rem(there[1] + layer, layers) * chunk, 16) if layers > 1 else 0
        return pltpu.make_async_copy(
            pairs[2 * k].at[pl.ds(row, chunk)], left.at[k * layers + layer], left_sems.at[k * layers + layer]
        )

    def right_copy(group, t):
        k, at, start, step = tiles[t]
        half = (there if group == 0 else here)[0]
        column = pl.multiple_of(half * widths[k] + at, LANES)
        return pltpu.make_async_copy(
            pairs[2 * k + 1].at[:, pl.ds(column, step)],
            right.at[group, :, pl.ds(start, step)],
            right_sems.at[group, t],
        )

    def out_copies(group):
        targets = away if group == 0 else outs
        return [
            pltpu.make_async_copy(sums.at[group, s], targets[s], out_sems.at[group * side + s]) for s in range(side)
        ]

    for layer in range(layers):
        for k in range(count):
            left_copy(k, layer).start()
            if layer == 0:
                for t in range(len(tiles)):
                    if tiles[t][0] == k:
                        right_copy(0, t).start()
    for t in range(len(tiles)):
        right_copy(1, t).start()
    for group in range(2):
        where = there if group == 0 else here
        for layer in range(layers):
            for t, (k, at, start, step) in enumerate(tiles):
                if group == 0 and at == 0:
                    left_copy(k, layer).wait()
                if layer == 0:
                    right_copy(group, t).wait()
                columns = slice(start, start + step)
                acc[:, :step] = dot(left[k * layers + layer], right[group, :, columns])
                put_pieces(acc, sums, group, columns, where, depth, side, rows, deep, layer * deep)
        for copy in out_copies(group):
            copy.start()
    for group in range(2):
        for copy in out_copies(group):
            copy.wait()


def layer_grad_kernel(depth, side, rows, there, here, lhs, rhs, *refs):
    away, outs, refs = refs[:side], refs[side : 2 * side], refs[2 * side :]
    left, right, acc, sums, left_sems, right_sem, out_sems = refs
    chunk, width = left.shape[1], right.shape[1] // 2

    def left_copy(z):
        row = pl.multiple_of(lax.rem(there[1] + z, depth) * chunk, 16)
        return pltpu.make_async_copy(lhs.at[pl.ds(row, chunk)], left.at[z], left_sems.at[z])

    def out_copies(z):
        copies = []
        for s in range(side):
            copies.append(pltpu.make_async_copy(sums.at[0, s, :, z], away[s].at[:, z], out_sems.at[z, s]))
            copies.append(pltpu.make_async_copy(sums.at[1, s, :, z], outs[s].at[:, z], out_sems.at[z, side + s]))
        return copies

    right_copy = pltpu.make_async_copy(rhs, right, right_sem)
    left_copy(0).start()
    right_copy.start()
    left_copy(1).start()
    right_copy.wait()
    for z in range(depth):
        left_copy(z).wait()
        if z + 2 < depth:
            left_copy(z + 2).start()
        acc[...] = dot(left[z], right[...])
        for group, where in ((0, there), (1, here)):
            column = pl.multiple_of(where[0] * width, LANES)
            for second in range(side):
                for first in range(side):
                    from_row = lax.rem(row_of(where, depth, side, second, first, z), side * side)
                    piece = acc[pl.ds(pl.multiple_of(from_row * rows, 16), rows), pl.ds(column, width)]
                    sums[group, second, first, z] = piece.astype(BF16)
        for copy in out_copies(z):
            copy.start()
    for z in range(depth):
        for copy in out_copies(z):
            copy.wait()


def rel_grad(pairs, shards, there, here):
    depth, side = grid_of(shards)
    features, length = pairs[0][0].shape
    widths = [rhs.shape[1] // 2 for _, rhs in pairs]
    width = sum(widths)
    rows = features // shards
    core = lax.axis_index("dp")
    if rows % 16 != 0:
        both = []
        for half, where in ((1 - core, there), (core, here)):
            wholes = [
                lax.dot_general(
                    lhs,
                    lax.dynamic_slice_in_dim(rhs, half * (rhs.shape[1] // 2), rhs.shape[1] // 2, axis=1),
                    (((1,), (0,)), ((), ())),
                    preferred_element_type=F32,
                )
                for lhs, rhs in pairs
            ]
            whole = jnp.concatenate(wholes, axis=1).reshape(depth, side, side, rows, width)
            rel = jnp.where(half == 0, whole.transpose(1, 2, 0, 3, 4), whole.transpose(2, 1, 0, 3, 4))
            rel = jnp.roll(rel, -where[3], axis=0)
            rel = jnp.roll(rel, -where[2], axis=1)
            both.append(jnp.roll(rel, -where[1], axis=2).astype(BF16))
        return [both[0][s] for s in range(side)], [both[1][s] for s in range(side)]
    deep = depth if features <= 1024 else 1
    chunk = features if deep > 1 else features // depth
    layers = depth // deep
    count, pieces = len(pairs), len(tiles_of(widths))
    if layers > 1 and count == 1 and 2 * width <= 768:
        out = pl.pallas_call(
            functools.partial(layer_grad_kernel, depth, side, rows),
            in_specs=[SMEM, SMEM, HBM, HBM],
            out_specs=[HBM] * (2 * side),
            out_shape=[jax.ShapeDtypeStruct((side, depth, rows, width), BF16)] * (2 * side),
            scratch_shapes=[
                pltpu.VMEM((depth, chunk, length), BF16),
                pltpu.VMEM((length, 2 * width), BF16),
                pltpu.VMEM((chunk, 2 * width), F32),
                pltpu.VMEM((2, side, side, depth, rows, width), BF16),
                pltpu.SemaphoreType.DMA((depth,)),
                pltpu.SemaphoreType.DMA,
                pltpu.SemaphoreType.DMA((depth, 2 * side)),
            ],
            compiler_params=pltpu.CompilerParams(vmem_limit_bytes=VMEM_MOST * MEBI),
            cost_estimate=pl.CostEstimate(flops=4 * length * features * width, bytes_accessed=20 * MEBI, transcendentals=0),
            name="layer_grad",
        )(there, here, *pairs[0])
        return out[:side], out[side:]
    out = pl.pallas_call(
        functools.partial(grad_kernel, depth, side, rows, deep, widths),
        in_specs=[SMEM, SMEM] + [HBM] * (2 * count),
        out_specs=[HBM] * (2 * side),
        out_shape=[jax.ShapeDtypeStruct((side, depth, rows, width), BF16)] * (2 * side),
        scratch_shapes=[
            pltpu.VMEM((count * layers, chunk, length), BF16),
            pltpu.VMEM((2, length, width), BF16),
            pltpu.VMEM((chunk, min(768, max(widths))), F32),
            pltpu.VMEM((2, side, side, depth, rows, width), BF16),
            pltpu.SemaphoreType.DMA((count * layers,)),
            pltpu.SemaphoreType.DMA((2, pieces)),
            pltpu.SemaphoreType.DMA((2 * side,)),
        ],
        compiler_params=pltpu.CompilerParams(vmem_limit_bytes=VMEM_MOST * MEBI),
        cost_estimate=pl.CostEstimate(flops=4 * length * features * width, bytes_accessed=20 * MEBI, transcendentals=0),
        name="grad",
    )(there, here, *(operand for pair in pairs for operand in pair))
    return out[:side], out[side:]


def sum_of(*values):
    total = values[0].astype(F32)
    for value in values[1:]:
        total = total + value.astype(F32)
    return total.astype(BF16)


def second_sends(own, got):
    return [sum_of(own[s], got[s]) for s in range(1, len(got))]


def second_parts(sends, shards):
    _, side = grid_of(shards)
    return [arrive(send, shards, "second", side - 1 - k) for k, send in enumerate(sends)]


def second_sums(own, got, parts):
    return [sum_of(own[0][f], got[0][f], *(part[f] for part in parts)) for f in range(own[0].shape[0])]


def first_parts(sums, shards):
    _, side = grid_of(shards)
    return [arrive(sums[f], shards, "first", side - f) for f in range(1, side)]


def first_sums(sums, parts):
    return [sum_of(sums[0][z], *(part[z] for part in parts)) for z in range(sums[0].shape[0])]


def z_parts(sums, shards):
    depth, _ = grid_of(shards)
    return [sums[0]] + [arrive(sums[z], shards, "z", depth - z) for z in range(1, depth)]


def line_parts(lines, shards, kind):
    _, side = grid_of(shards)
    if kind == "second_flip_1":
        straight = line_parts(lines, shards, "second")
        return straight + [arrive(lines, shards, "slant", step) for step in range(side)]
    if kind in ("flip_1", "flip_2"):
        return [lines, arrive(lines, shards, "flip", int(kind[-1]))]
    count = 2 if kind == "core" else side
    return [lines] + [arrive(lines, shards, kind, step) for step in range(1, count)]


def exchange_lines(lines, shards, kind):
    return sum_of(*line_parts(lines, shards, kind))


def both_halves(mine, shards, widths):
    theirs = arrive(mine, shards, "core", 1)
    core = lax.axis_index("dp")
    left = jnp.where(core == 0, mine, theirs)
    right = jnp.where(core == 0, theirs, mine)
    wholes, start = [], 0
    for width in widths:
        columns = slice(start, start + width)
        wholes.append(jnp.concatenate([left[:, columns], right[:, columns]], axis=1).astype(F32))
        start += width
    return wholes


GAIN_ONE, SHIFT_ONE, BIAS_QUERY, BIAS_VALUE, BIAS_OUT, GAIN_TWO, SHIFT_TWO, BIAS_DOWN = range(8)
SCALE = HEAD_DIM ** (-0.5)


def weight_copies(plan, here, there, parts, outs, sems, first=0):
    groups = [[] for _ in outs]
    if plan is None:
        for k, (part, out) in enumerate(zip(parts, outs)):
            groups[k].append(pltpu.make_async_copy(part, out, sems.at[first + k]))
        return groups
    depth, side, rows, cuts = plan
    used = first
    for group in range(2):
        where = here if group == 0 else there
        for second in range(side):
            for ahead in range(side):
                for z in range(depth):
                    at = pl.multiple_of(row_of(where, depth, side, second, ahead, z) * rows, 16)
                    source = parts[group * side + second].at[ahead, z]
                    for k, ((start, width, split), out) in enumerate(zip(cuts, outs)):
                        if group == 1 and not split:
                            continue
                        column = pl.multiple_of(where[0] * width, LANES) if split else 0
                        groups[k].append(
                            pltpu.make_async_copy(
                                source.at[:, pl.ds(start, width)],
                                out.at[pl.ds(at, rows), pl.ds(column, width)],
                                sems.at[used],
                            )
                        )
                        used += 1
    return groups


def bring(groups):
    for group in groups:
        for copy in group:
            copy.start()
    for group in groups:
        for copy in group:
            copy.wait()


def copies_of(plan, shards, cuts):
    if plan is None:
        return len(cuts)
    return shards * sum(2 if split else 1 for _, _, split in cuts)


def standardize(values):
    average = jnp.mean(values, axis=-1, keepdims=True)
    centred = values - average
    spread = jnp.mean(centred * centred, axis=-1, keepdims=True)
    inverse = lax.rsqrt(spread + EPSILON)
    return centred * inverse, inverse


def dot(a, b, dims=((1,), (0,))):
    return lax.dot_general(a, b, (dims, ((), ())), preferred_element_type=F32)


NT = ((1,), (1,))
TN = ((0,), (0,))


def project_kernel(plan, count, here, there, tokens, lines, *refs):
    parts = refs[:count]
    normed_ref, qkv_ref = refs[count : count + 2]
    weight, sems = refs[count + 2 :]
    width = tokens.shape[1]

    @pl.when(pl.program_id(0) == 0)
    def _():
        bring(weight_copies(plan, here, there, parts, (weight,), sems))

    standard, _ = standardize(tokens[...].astype(F32))
    normed = (standard * lines[pl.ds(GAIN_ONE, 1), :] + lines[pl.ds(SHIFT_ONE, 1), :]).astype(BF16)
    normed_ref[...] = normed.T
    bias = (lines[pl.ds(BIAS_QUERY, 1), :], None, lines[pl.ds(BIAS_VALUE, 1), :])
    for part in range(3):
        columns = slice(part * width, (part + 1) * width)
        project = dot(normed, weight[:, columns])
        if bias[part] is not None:
            project = project + bias[part]
        qkv_ref[:, columns] = project.astype(BF16)


def attend_kernel(frames, qkv_ref, mixed_ref, turned_ref, power_ref, inverse_ref):
    tube = pl.program_id(0)
    length, width = mixed_ref.shape
    mask = jnp.where(lax.broadcasted_iota(jnp.int32, (1, length), 1) < frames[tube] * PATCH, 0.0, -1e30)
    lower = lax.broadcasted_iota(jnp.int32, (length, LANES), 1) < HEAD_DIM
    ones = jnp.ones((length, LANES), BF16)
    for pair in range(width // LANES):
        query = qkv_ref[:, pair * LANES : (pair + 1) * LANES] * jnp.asarray(SCALE, BF16)
        keys = qkv_ref[:, width + pair * LANES : width + (pair + 1) * LANES]
        values = qkv_ref[:, 2 * width + pair * LANES : 2 * width + (pair + 1) * LANES]
        values = jnp.concatenate([values, ones], axis=1)
        both = []
        for k in range(2):
            own = jnp.where(lower if k == 0 else ~lower, query, jnp.zeros_like(query))
            scores = dot(own, keys, NT) + mask
            power = jnp.exp(scores - jnp.max(scores, axis=-1, keepdims=True)).astype(BF16)
            power_ref[0, 2 * pair + k] = power
            both.append(dot(power, values))
        inverse = 1.0 / jnp.where(lower, both[0][:, LANES:], both[1][:, LANES:])
        inverse_ref[:, pair * LANES : (pair + 1) * LANES] = inverse.astype(BF16)
        mixed = jnp.where(lower, both[0][:, :LANES], both[1][:, :LANES]) * inverse
        mixed = mixed.astype(BF16)
        mixed_ref[:, pair * LANES : (pair + 1) * LANES] = mixed
        turned_ref[pair * LANES : (pair + 1) * LANES, :] = mixed.T


def feed_kernel(plan, count, here, there, frames, tokens, mixed, cotangent, lines, up_bias, *refs):
    parts = refs[:count]
    resid_ref, normed_ref, active_ref, turned_ref, slope_ref, upstream_ref = refs[count : count + 6]
    out_weight, up_weight, sems = refs[count + 6 :]
    tube = pl.program_id(0)
    first, last = weight_copies(plan, here, there, parts, (out_weight, up_weight), sems)

    @pl.when(tube == 0)
    def _():
        for copy in first + last:
            copy.start()
        for copy in first:
            copy.wait()

    length = tokens.shape[0]
    row_ok = lax.broadcasted_iota(jnp.int32, (length, 1), 0) < frames[tube] * PATCH
    upstream_ref[...] = jnp.where(row_ok, cotangent[...], jnp.zeros_like(cotangent))
    attended = dot(mixed[...], out_weight[...]) + lines[pl.ds(BIAS_OUT, 1), :]
    resid = tokens[...].astype(F32) + attended
    resid_ref[...] = resid.astype(BF16)
    standard, _ = standardize(resid)
    normed = (standard * lines[pl.ds(GAIN_TWO, 1), :] + lines[pl.ds(SHIFT_TWO, 1), :]).astype(BF16)
    normed_ref[...] = normed.T

    @pl.when(tube == 0)
    def _():
        for copy in last:
            copy.wait()

    units = up_weight.shape[1]
    step = 512
    for at in range(0, units, step):
        hidden = dot(normed, up_weight[:, at : at + step]) + up_bias[:, at : at + step]
        cumulative = 0.5 + 0.5 * lax.erf(hidden * SQRT_HALF)
        density = jnp.exp2(hidden * hidden * (-0.5 * LOG2_E) + LOG2_DENSITY)
        active = (hidden * cumulative).astype(BF16)
        active_ref[:, at : at + step] = active
        turned_ref[at : at + step, :] = active.T
        slope_ref[:, at : at + step] = (cumulative + hidden * density).astype(BF16)


def norm_back(grad, standard, inverse, gain):
    scaled = grad * gain
    first = jnp.mean(scaled, axis=-1, keepdims=True)
    second = jnp.mean(scaled * standard, axis=-1, keepdims=True)
    return inverse * (scaled - first - standard * second)


def column_sum(values):
    return jnp.sum(values, axis=0, keepdims=True)


SUM_GAIN_TWO, SUM_SHIFT_TWO, SUM_BIAS_OUT, SUM_BIAS_DOWN = range(4)


def feed_back_kernel(plans, counts, depth, side, rows, direct, here, there, upstream, slope, resid, inverse_sums, lines, *refs):
    mixed_hbm, normed_hbm, refs = refs[0], refs[1], refs[2:]
    ff_parts, refs = refs[: counts[0]], refs[counts[0] :]
    down_parts, refs = refs[: counts[1]], refs[counts[1] :]
    attended_ref, scaled_ref, sums_ref, up_sum_ref = refs[:4]
    refs = refs[4:]
    if direct:
        away, outs, refs = refs[:side], refs[side : 2 * side], refs[2 * side :]
    else:
        hidden_hbm, refs = refs[0], refs[1:]
    out_weight, up_weight, down_weight, hidden_all, attended_all, sems, more_sems = refs[:7]
    tube, last = pl.program_id(0), pl.num_programs(0) - 1
    length, width = upstream.shape
    units = up_weight.shape[1]
    (down_copies,) = weight_copies(plans[1], here, there, down_parts, (down_weight,), sems)
    ff_copies = weight_copies(plans[0], here, there, ff_parts, (out_weight, up_weight), sems, len(down_copies))
    if direct:
        turned, acc, sums = refs[7:]
        left_copies = [
            pltpu.make_async_copy(mixed_hbm, turned.at[0], more_sems.at[0]),
            pltpu.make_async_copy(normed_hbm, turned.at[1], more_sems.at[1]),
        ]

    @pl.when(tube == 0)
    def _():
        for copy in down_copies:
            copy.start()
        for group in reversed(ff_copies):
            for copy in group:
                copy.start()
        if direct:
            for copy in left_copies:
                copy.start()
        sums_ref[...] = jnp.zeros_like(sums_ref)
        up_sum_ref[...] = jnp.zeros_like(up_sum_ref)
        for copy in down_copies:
            copy.wait()

    here_rows = pl.ds(pl.multiple_of(tube * length, 16), length)
    low = upstream[...]
    standard, inverse = standardize(resid[...].astype(F32))
    step = 768
    for at in range(0, units, step):
        grad = dot(low, down_weight[at : at + step, :], NT) * slope[:, at : at + step].astype(F32)
        hidden_all[here_rows, at : at + step] = grad.astype(BF16)
        up_sum_ref[:, at : at + step] += column_sum(grad)

    @pl.when(tube == 0)
    def _():
        for group in ff_copies:
            for copy in group:
                copy.wait()

    normed_grad = dot(hidden_all[here_rows, :], up_weight[...], NT)
    above = low.astype(F32)
    resid_grad = above + norm_back(normed_grad, standard, inverse, lines[pl.ds(GAIN_TWO, 1), :])
    attended_grad = resid_grad.astype(BF16)
    attended_ref[...] = attended_grad
    attended_all[here_rows, :] = attended_grad
    scaled_ref[...] = (dot(attended_grad, out_weight[...], NT) * inverse_sums[...].astype(F32)).astype(BF16)
    sums_ref[pl.ds(SUM_GAIN_TWO, 1), :] += column_sum(normed_grad * standard)
    sums_ref[pl.ds(SUM_SHIFT_TWO, 1), :] += column_sum(normed_grad)
    sums_ref[pl.ds(SUM_BIAS_OUT, 1), :] += column_sum(attended_grad.astype(F32))
    sums_ref[pl.ds(SUM_BIAS_DOWN, 1), :] += column_sum(above)

    if not direct:

        @pl.when(tube == last)
        def _():
            copy = pltpu.make_async_copy(hidden_all, hidden_hbm, more_sems.at[0])
            copy.start()
            copy.wait()

        return

    @pl.when(tube == 1)
    def _():
        for k in range(2):
            left_copies[k].wait()

    @pl.when(tube == last)
    def _():
        waits = []
        for group in range(2):
            where = there if group == 0 else here
            for k, at, start, size in tiles_of((width // 2, units // 2)):
                right = attended_all if k == 0 else hidden_all
                column = pl.multiple_of(where[0] * (right.shape[1] // 2) + at, LANES)
                acc[:, :size] = dot(turned[k], right[:, pl.ds(column, size)])
                put_pieces(acc, sums, group, slice(start, start + size), where, depth, side, rows, depth, 0)
            targets = away if group == 0 else outs
            for s in range(side):
                waits.append(pltpu.make_async_copy(sums.at[group, s], targets[s], more_sems.at[2 + group * side + s]))
                waits[-1].start()
        for copy in waits:
            copy.wait()


def attend_back_kernel(qkv, power_ref, mixed, scaled_grad, grad_ref, sums_ref):
    tube = pl.program_id(0)

    @pl.when(tube == 0)
    def _():
        sums_ref[...] = jnp.zeros_like(sums_ref)

    length, width = mixed.shape
    lower = lax.broadcasted_iota(jnp.int32, (length, LANES), 1) < HEAD_DIM
    for pair in range(width // LANES):
        lanes = slice(pair * LANES, (pair + 1) * LANES)
        query = qkv[:, lanes]
        keys = qkv[:, width + pair * LANES : width + (pair + 1) * LANES]
        values = qkv[:, 2 * width + pair * LANES : 2 * width + (pair + 1) * LANES]
        above = scaled_grad[:, lanes]
        product = above.astype(F32) * mixed[:, lanes].astype(F32)
        query_grad, keys_grad, values_grad = [], [], []
        for k in range(2):
            mine = lower if k == 0 else ~lower
            own = jnp.where(mine, above, jnp.zeros_like(above))
            power = power_ref[0, 2 * pair + k]
            inner = jnp.sum(jnp.where(mine, product, 0.0), axis=-1, keepdims=True)
            scores_grad = (power.astype(F32) * (dot(own, values, NT) - inner)).astype(BF16)
            values_grad.append(dot(power, above, TN))
            query_grad.append(dot(scores_grad, keys))
            keys_grad.append(dot(scores_grad, query, TN))
        for part, (pieces, scale) in enumerate(((query_grad, SCALE), (keys_grad, SCALE), (values_grad, None))):
            piece = jnp.where(lower, pieces[0], pieces[1])
            if scale is not None:
                piece = piece * scale
            grad_ref[:, part * width + pair * LANES : part * width + (pair + 1) * LANES] = piece.astype(BF16)
            if part != 1:
                sums_ref[pl.ds(part // 2, 1), lanes] += column_sum(piece)


def first_back_kernel(plan, count, here, there, tokens, project_grad, attended_grad, lines, *refs):
    parts = refs[:count]
    tokens_ref, sums_ref = refs[count : count + 2]
    weight, sems = refs[count + 2 :]
    tube = pl.program_id(0)

    @pl.when(tube == 0)
    def _():
        bring(weight_copies(plan, here, there, parts, (weight,), sems))
        sums_ref[...] = jnp.zeros_like(sums_ref)

    grad = dot(project_grad[...], weight[...], NT)
    standard, inverse = standardize(tokens[...].astype(F32))
    inputs_grad = norm_back(grad, standard, inverse, lines[pl.ds(GAIN_ONE, 1), :])
    tokens_ref[...] = (attended_grad[...].astype(F32) + inputs_grad).astype(BF16)
    sums_ref[pl.ds(0, 1), :] += column_sum(grad * standard)
    sums_ref[pl.ds(1, 1), :] += column_sum(grad)


def block_out_kernel(plan, count, here, there, active, resid, lines, *refs):
    parts = refs[:count]
    out_ref = refs[count]
    weight, sems = refs[count + 1 :]

    @pl.when(pl.program_id(0) == 0)
    def _():
        bring(weight_copies(plan, here, there, parts, (weight,), sems))

    branch = dot(active[...], weight[...]) + lines[pl.ds(BIAS_DOWN, 1), :]
    out_ref[...] = (resid[...].astype(F32) + branch).astype(BF16)


def rows_of(width, length):
    return pl.BlockSpec((length, width), lambda t: (t, 0))


def fixed(*shape):
    return pl.BlockSpec(shape, lambda t: (0,) * len(shape))


def shape_of(*shape, kind=BF16):
    return jax.ShapeDtypeStruct(shape, kind)


def call(kernel, name, grid, in_specs, outs, scratch, flops, *args):
    return pl.pallas_call(
        kernel,
        grid=(grid,),
        in_specs=in_specs,
        out_specs=[spec for spec, _ in outs],
        out_shape=[shape for _, shape in outs],
        scratch_shapes=scratch,
        compiler_params=pltpu.CompilerParams(vmem_limit_bytes=VMEM_MOST * MEBI),
        cost_estimate=pl.CostEstimate(flops=flops, bytes_accessed=16 * MEBI, transcendentals=0),
        name=name,
    )(*args)


def local(
    tokens,
    clip_frames,
    tube_clip,
    first_gain,
    first_shift,
    qkv_weight,
    query_bias,
    value_bias,
    out_weight,
    out_bias,
    second_gain,
    second_shift,
    up_weight,
    up_bias,
    down_weight,
    down_bias,
    cotangent,
):
    shards = lax.axis_size("fsdp")
    depth, side = grid_of(shards)
    core = lax.axis_index("dp")
    total, width = tokens.shape
    tubes = tube_clip.shape[0]
    length = total // tubes
    clip_count = clip_frames.shape[0]

    def half(matrix):
        columns = matrix.shape[1] // 2
        return lax.dynamic_slice_in_dim(matrix, core * columns, columns, axis=1)

    wide, full, ff = qkv_weight.shape[1] // 2, out_weight.shape[1] // 2, up_weight.shape[1] // 2
    units = 2 * ff
    rows = first_gain.shape[0]
    vectors = [first_gain, first_shift, query_bias, value_bias, out_bias, second_gain, second_shift, down_bias]
    vectors += [up_bias[k * rows : (k + 1) * rows] for k in range(4)]
    pack_one = half(qkv_weight)
    pack_two = jnp.concatenate([half(out_weight), half(up_weight)], axis=1)
    cuts = (
        ((0, wide, True),),
        ((0, full, True), (full, ff, True)),
        ((0, full, True),),
    )
    plans, counts = [], []
    for pack, cut in zip((pack_one, pack_two, down_weight), cuts):
        direct = pack.shape[0] % 16 == 0
        plans.append((depth, side, pack.shape[0], cut) if direct else None)
        counts.append(2 * side if direct else len(cut))

    def finish(k, own, other):
        return [*own, *other] if plans[k] is not None else assemble(own, other, shards, cuts[k])

    number = [copies_of(plan, shards, cut) for plan, cut in zip(plans, cuts)]
    sem = pltpu.SemaphoreType.DMA
    big = 2 * total * width * width
    narrow, wide_rows, deep_rows = rows_of(width, length), rows_of(3 * width, length), rows_of(units, length)
    upright = pl.BlockSpec((width, length), lambda t: (0, t))
    tall = total // 2
    tall_narrow, tall_wide, tall_deep = rows_of(width, tall), rows_of(3 * width, tall), rows_of(units, tall)
    probs_spec = pl.BlockSpec((1, HEADS, length, length), lambda t: (t, 0, 0, 0))

    near, far = (1, depth - 1), range(2, depth - 1)

    def stack_z(unit, near_units, far_units):
        return jnp.stack([unit, near_units[0], *far_units, near_units[1]])

    spread = spread_lines(vectors, shards)
    z_one = stack_z(pack_one, from_z(pack_one, shards, near), from_z(pack_one, shards, far))
    z_one, spread, pack_two = lax.optimization_barrier((z_one, spread, pack_two))
    first_one = gather_first(z_one, shards)
    near_two = from_z(pack_two, shards, near)
    spread = exchange_lines(spread, shards, "first")
    first_one, near_two, spread, pack_two, tube_clip, down_weight = lax.optimization_barrier(
        (first_one, near_two, spread, pack_two, tube_clip, down_weight)
    )
    second_one = gather_second(first_one, shards)
    early_one = arrive(first_one, shards, "core", 1)
    z_two = stack_z(pack_two, near_two, from_z(pack_two, shards, far))
    spread = exchange_lines(spread, shards, "second")
    pack_three = half(down_weight)
    here, there = place(shards, core), place(shards, 1 - core)
    matches = tube_clip[:, None] == jnp.arange(clip_count, dtype=jnp.int32)[None, :]
    frames = jnp.sum(jnp.where(matches, clip_frames[None, :], 0), axis=1)
    second_one, early_one, z_two, spread, pack_three, here, there, frames = lax.optimization_barrier(
        (second_one, early_one, z_two, spread, pack_three, here, there, frames)
    )
    core_one = [early_one] + gather_core(second_one[1:], shards)
    first_two = gather_first(z_two, shards)
    for kind in ("flip_1", "flip_2"):
        spread = exchange_lines(spread, shards, kind)
    lines = join_lines(spread, len(vectors), rows)
    up_row = lines[8:12].reshape(4, shards, rows).transpose(1, 0, 2).reshape(1, units)
    core_one, first_two, pack_three, tokens, lines, up_row = lax.optimization_barrier(
        (core_one, first_two, pack_three, tokens, lines, up_row)
    )
    parts_one = finish(0, second_one, core_one)
    second_two = gather_second(first_two, shards)
    early_two = arrive(first_two, shards, "core", 1)
    z_three = stack_z(pack_three, from_z(pack_three, shards, near), from_z(pack_three, shards, far))

    normed_one, qkv = call(
        functools.partial(project_kernel, plans[0], counts[0]),
        "project",
        tubes,
        [SMEM, SMEM, narrow, fixed(16, width)] + [HBM] * counts[0],
        [(upright, shape_of(width, total)), (wide_rows, shape_of(total, 3 * width))],
        [pltpu.VMEM((width, 3 * width), BF16), sem((number[0],))],
        3 * big,
        here, there, tokens, lines, *parts_one,
    )
    z_three, qkv, early_two = lax.optimization_barrier((z_three, qkv, early_two))

    mixed, mixed_turned, power, inverse = call(
        attend_kernel,
        "attend",
        tubes,
        [SMEM, wide_rows],
        [
            (narrow, shape_of(total, width)),
            (upright, shape_of(width, total)),
            (probs_spec, shape_of(tubes, HEADS, length, length)),
            (narrow, shape_of(total, width)),
        ],
        [],
        4 * big,
        frames, qkv,
    )
    first_three = gather_first(z_three, shards)
    second_two, mixed, first_three = lax.optimization_barrier((second_two, mixed, first_three))
    core_two = [early_two] + gather_core(second_two[1:], shards)
    core_two, first_three, mixed = lax.optimization_barrier((core_two, first_three, mixed))
    parts_two = finish(1, second_two, core_two)
    second_three = gather_second(first_three, shards)
    early_three = arrive(first_three, shards, "core", 1)

    resid, normed_two, active, active_turned, slope, upstream = call(
        functools.partial(feed_kernel, plans[1], counts[1]),
        "feed",
        tubes,
        [SMEM, SMEM, SMEM, narrow, narrow, narrow, fixed(16, width), fixed(1, units)] + [HBM] * counts[1],
        [
            (narrow, shape_of(total, width)),
            (upright, shape_of(width, total)),
            (deep_rows, shape_of(total, units)),
            (pl.BlockSpec((units, length), lambda t: (0, t)), shape_of(units, total)),
            (deep_rows, shape_of(total, units)),
            (narrow, shape_of(total, width)),
        ],
        [pltpu.VMEM((width, width), BF16), pltpu.VMEM((width, units), BF16), sem((number[1],))],
        8 * big,
        here, there, frames, tokens, mixed, cotangent, lines, up_row, *parts_two,
    )
    second_three, early_three, active_turned, upstream = lax.optimization_barrier(
        (second_three, early_three, active_turned, upstream)
    )
    core_three = [early_three] + gather_core(second_three[1:], shards)
    down_away, down_own = rel_grad([(active_turned, upstream)], shards, there, here)
    core_three, down_away, slope = lax.optimization_barrier((core_three, down_away, slope))
    down_got = gather_core(down_away, shards)
    down_got, slope = lax.optimization_barrier((down_got, slope))
    parts_three = finish(2, second_three, core_three)
    down_sends, slope = lax.optimization_barrier((second_sends(down_own, down_got), slope))
    down_parts = second_parts(down_sends, shards)

    direct = rows % 16 == 0
    ff_width = full + ff
    outs = [
        (narrow, shape_of(total, width)),
        (narrow, shape_of(total, width)),
        (fixed(8, width), shape_of(8, width, kind=F32)),
        (fixed(1, units), shape_of(1, units, kind=F32)),
    ]
    scratch = [
        pltpu.VMEM((width, width), BF16),
        pltpu.VMEM((width, units), BF16),
        pltpu.VMEM((units, width), BF16),
        pltpu.VMEM((total, units), BF16),
        pltpu.VMEM((total, width), BF16),
        sem((number[1] + number[2],)),
        sem((2 + 2 * side,)),
    ]
    if direct:
        outs += [(HBM, shape_of(side, depth, rows, ff_width))] * (2 * side)
        scratch += [
            pltpu.VMEM((2, width, total), BF16),
            pltpu.VMEM((width, 768), F32),
            pltpu.VMEM((2, side, side, depth, rows, ff_width), BF16),
        ]
    else:
        outs.append((HBM, shape_of(total, units)))
    attended_grad, scaled_grad, sums_two, up_sum, *more = call(
        functools.partial(feed_back_kernel, plans[1:], counts[1:], depth, side, rows, direct),
        "feed_back",
        tubes,
        [SMEM, SMEM, narrow, deep_rows, narrow, narrow, fixed(16, width)] + [HBM] * (2 + counts[1] + counts[2]),
        outs,
        scratch,
        14 * big,
        here, there, upstream, slope, resid, inverse, lines, mixed_turned, normed_two, *parts_two, *parts_three,
    )
    if direct:
        ff_away, ff_own = more[:side], more[side:]
    else:
        ff_away, ff_own = rel_grad([(mixed_turned, attended_grad), (normed_two, more[0])], shards, there, here)
    down_parts, down_got, ff_away, scaled_grad = lax.optimization_barrier((down_parts, down_got, ff_away, scaled_grad))
    ff_rest = gather_core(ff_away[1:], shards)
    down_sums = second_sums(down_own, down_got, down_parts)
    down_parts = first_parts(down_sums, shards)
    ff_rest, ff_near, scaled_grad, down_sums = lax.optimization_barrier((ff_rest, ff_away[0], scaled_grad, down_sums))
    ff_sends, scaled_grad = lax.optimization_barrier((second_sends(ff_own, [None] + ff_rest), scaled_grad))
    ff_parts = second_parts(ff_sends, shards)
    ff_got = gather_core([ff_near], shards) + ff_rest

    project_grad, sums_heads = call(
        attend_back_kernel,
        "attend_back",
        tubes,
        [wide_rows, probs_spec, narrow, narrow],
        [(wide_rows, shape_of(total, 3 * width)), (fixed(8, width), shape_of(8, width, kind=F32))],
        [],
        4 * big,
        qkv, power, mixed, scaled_grad,
    )
    project_grad, down_parts, ff_got = lax.optimization_barrier((project_grad, down_parts, ff_got))
    down_sums, project_grad = lax.optimization_barrier((first_sums(down_sums, down_parts), project_grad))
    down_parts = z_parts(down_sums, shards)
    qkv_away, qkv_own = rel_grad([(normed_one, project_grad)], shards, there, here)
    qkv_away, project_grad, ff_parts = lax.optimization_barrier((qkv_away, project_grad, ff_parts))
    qkv_got = gather_core(qkv_away, shards)
    ff_sums, project_grad = lax.optimization_barrier((second_sums(ff_own, ff_got, ff_parts), project_grad))
    ff_parts = first_parts(ff_sums, shards)

    tokens_grad, sums_one = call(
        functools.partial(first_back_kernel, plans[0], counts[0]),
        "first_back",
        2,
        [SMEM, SMEM, tall_narrow, tall_wide, tall_narrow, fixed(16, width)] + [HBM] * counts[0],
        [(tall_narrow, shape_of(total, width)), (fixed(8, width), shape_of(8, width, kind=F32))],
        [pltpu.VMEM((width, 3 * width), BF16), sem((number[0],))],
        3 * big,
        here, there, tokens, project_grad, attended_grad, lines, *parts_one,
    )
    qkv_got, ff_parts, tokens_grad, sums_one, active, down_parts = lax.optimization_barrier(
        (qkv_got, ff_parts, tokens_grad, sums_one, active, down_parts)
    )
    sums = jnp.concatenate(
        [
            sums_one[:2],
            sums_heads[:2],
            sums_two[SUM_BIAS_OUT : SUM_BIAS_OUT + 1],
            sums_two[SUM_GAIN_TWO : SUM_GAIN_TWO + 1],
            sums_two[SUM_SHIFT_TWO : SUM_SHIFT_TWO + 1],
            sums_two[SUM_BIAS_DOWN : SUM_BIAS_DOWN + 1],
            up_sum.reshape(-1, width),
        ],
        axis=0,
    ).astype(BF16)
    ff_sums, qkv_sends, sums, active = lax.optimization_barrier(
        (first_sums(ff_sums, ff_parts), second_sends(qkv_own, qkv_got), sums, active)
    )
    ff_parts = z_parts(ff_sums, shards)
    qkv_parts = second_parts(qkv_sends, shards)
    sums = line_parts(sums, shards, "first")

    (block_out,) = call(
        functools.partial(block_out_kernel, plans[2], counts[2]),
        "block_out",
        tubes,
        [SMEM, SMEM, deep_rows, narrow, fixed(16, width)] + [HBM] * counts[2],
        [(narrow, shape_of(total, width))],
        [pltpu.VMEM((units, width), BF16), sem((number[2],))],
        4 * big,
        here, there, active, resid, lines, *parts_three,
    )
    block_out, ff_parts, qkv_parts, sums, down_parts = lax.optimization_barrier(
        (block_out, ff_parts, qkv_parts, sums, down_parts)
    )
    qkv_sums = second_sums(qkv_own, qkv_got, qkv_parts)
    qkv_parts = first_parts(qkv_sums, shards)
    sums = exchange_lines(sum_of(*sums), shards, "second_flip_1")
    sums = line_parts(sums, shards, "flip_2")
    qkv_parts, sums, ff_parts, down_parts = lax.optimization_barrier((qkv_parts, sums, ff_parts, down_parts))
    qkv_sums, sums = lax.optimization_barrier((first_sums(qkv_sums, qkv_parts), sum_of(*sums)))
    qkv_parts = z_parts(qkv_sums, shards)
    (down_whole,) = both_halves(sum_of(*down_parts), shards, (full,))
    out_whole, up_whole = both_halves(sum_of(*ff_parts), shards, (full, ff))
    sums = exchange_lines(sums, shards, "core")
    at = lax.axis_index("fsdp")
    sums_here = lax.dynamic_slice_in_dim(sums[:8], at * rows, rows, axis=1).astype(F32)
    up_here = lax.dynamic_slice_in_dim(sums[8:].reshape(-1), at * up_bias.shape[0], up_bias.shape[0]).astype(F32)
    qkv_parts, sums_here, up_here, down_whole, out_whole, up_whole = lax.optimization_barrier(
        (qkv_parts, sums_here, up_here, down_whole, out_whole, up_whole)
    )
    (qkv_whole,) = both_halves(sum_of(*qkv_parts), shards, (wide,))
    return (
        block_out,
        tokens_grad,
        sums_here[0],
        sums_here[1],
        qkv_whole,
        sums_here[2],
        sums_here[3],
        out_whole,
        sums_here[4],
        sums_here[5],
        sums_here[6],
        up_whole,
        up_here,
        down_whole,
        sums_here[7],
    )


def solution(mesh):
    return jax.shard_map(
        local,
        mesh=mesh,
        in_specs=(
            P(("dp", "fsdp"), None),
            P(),
            P(("dp", "fsdp")),
            P("fsdp"),
            P("fsdp"),
            P("fsdp", None),
            P("fsdp"),
            P("fsdp"),
            P("fsdp", None),
            P("fsdp"),
            P("fsdp"),
            P("fsdp"),
            P("fsdp", None),
            P("fsdp"),
            P("fsdp", None),
            P("fsdp"),
            P(("dp", "fsdp"), None),
        ),
        out_specs=(
            P(("dp", "fsdp"), None),
            P(("dp", "fsdp"), None),
            P("fsdp"),
            P("fsdp"),
            P("fsdp", None),
            P("fsdp"),
            P("fsdp"),
            P("fsdp", None),
            P("fsdp"),
            P("fsdp"),
            P("fsdp"),
            P("fsdp", None),
            P("fsdp"),
            P("fsdp", None),
            P("fsdp"),
        ),
        check_vma=False,
    )
```
